256 devices in a mesh: modes: 8 (over y, core), mesh: 32 (over z, x).
Axes of the slice: x: 4, y: 4, z: 8, core: 2. Of those that a mesh axis runs over, the one named last changes fastest.
Arguments:
- velocity: float32 [3, 128, 7, 7, 4096], P(None, 'modes', None, None, 'mesh'), may hold values from -30 to 30
- element_slot: int32 [4096], P('mesh'), may hold values from 0 to 127, as said below
Outputs:
- advanced: float32 [3, 128, 7, 7, 4096], P(None, 'modes', None, None, 'mesh')
The draws below stay inside these ranges and needn't reach their ends.
Inputs may be any that keep to these rules, and one draw needn't show every extreme that they name: `element_slot`: each aligned block of 128 entries is a permutation of 0 to 127.
All inputs are finite; a program needn't handle non-finite values.
Results may differ from the reference program's by a relative error of at most 0.0003.
Values sent between devices are 32-bit elements; how exact they have to be, the bound alone decides.
A program may use at most 192 MiB of HBM per device.

```python
import jax
import jax.numpy as jnp
import numpy as np
from jax import lax

NODES = 7
MODES = 64
NCOEF = 128
EX = 8
EY = 16
E_DEV = 128
ELEMS = 4096
ITERS = 3
N_MESH = 32


def draw_velocity(key, part):
    key = jax.random.fold_in(key, 3)
    key_values, key_rough = jax.random.split(key, 2)
    extent = (3, NCOEF, NODES, NODES, ELEMS)
    column = (jnp.arange(ELEMS) // EY).astype(jnp.float32) / (ELEMS // EY)
    numbers = jnp.arange(NCOEF)
    wavenumber = jnp.where(numbers <= MODES, numbers, numbers - MODES).astype(jnp.float32)
    spectrum = (1.0 / (1.0 + wavenumber / 16.0)).reshape(1, NCOEF, 1, 1, 1)
    roughness = jax.random.uniform(key_rough, (3, 1, 1, 1, ELEMS), jnp.float32, 0.5, 1.5)
    values = jax.random.normal(key_values, extent, jnp.float32)
    envelope = 0.3 * 10.0 ** column
    return values * spectrum * roughness * envelope


def draw_element_slot(key, part):
    key = jax.random.fold_in(key, 7)
    strip_keys = jax.random.split(key, ELEMS // E_DEV)
    orders = jax.vmap(lambda strip_key: jax.random.permutation(strip_key, E_DEV))(strip_keys)
    return orders.reshape(-1).astype(jnp.int32)


def setup_inputs(seed: int = 0) -> dict:
    key_list = jax.random.split(jax.random.key(seed), 3)
    return {
        "velocity": draw_velocity(jax.random.fold_in(key_list[2], 71), 0),
        "element_slot": draw_element_slot(jax.random.fold_in(key_list[2], 71), 0),
    }


PRECISE = lax.Precision.HIGHEST
SIGMA_BASE = 8.0
SPAN_WAVE = 0.25
STEP_TIME = 0.01

def gll_tables():
    inner_point = np.sqrt((5.0 - 2.0 * np.sqrt(5.0 / 3.0)) / 11.0)
    outer_point = np.sqrt((5.0 + 2.0 * np.sqrt(5.0 / 3.0)) / 11.0)
    points = np.array([-1.0, -outer_point, -inner_point, 0.0, inner_point, outer_point, 1.0])
    legendre_prev = points * 0.0 + 1.0
    legendre_now = points.copy()
    for degree in range(1, points.shape[0] - 1):
        legendre_next = ((2 * degree + 1) * points * legendre_now - degree * legendre_prev) / (degree + 1)
        legendre_prev = legendre_now
        legendre_now = legendre_next
    order_value = points.shape[0] - 1
    quadrature = 2.0 / (order_value * (order_value + 1) * legendre_now ** 2)
    counter = np.arange(points.shape[0])
    same_node = counter[:, None] == counter[None, :]
    distances = np.where(same_node, 1.0, points[:, None] - points[None, :])
    barycentric = 1.0 / np.prod(distances, axis=1)
    off_diagonal = np.where(same_node, 0.0, barycentric[None, :] / barycentric[:, None] / distances)
    derivative = np.where(same_node, -np.sum(off_diagonal, axis=1)[:, None], off_diagonal)
    stiffness = derivative.T @ (quadrature[:, None] * derivative)
    return (jnp.asarray(quadrature, jnp.float32), jnp.asarray(derivative, jnp.float32), jnp.asarray(stiffness, jnp.float32))

def fourier_tables(coeff_total):
    half_count = coeff_total // 2
    planes = np.arange(coeff_total) * 2.0 * np.pi / coeff_total
    numbers = np.arange(coeff_total)
    wavenumber = np.where(numbers <= half_count, numbers, numbers - half_count)
    cosine_mask = (numbers <= half_count)[None, :]
    phase = planes[:, None] * wavenumber[None, :]
    inverse = np.where(cosine_mask, np.cos(phase), np.sin(phase))
    slope = SPAN_WAVE * wavenumber[None, :] * np.where(cosine_mask, -np.sin(phase), np.cos(phase))
    normaliser = np.where((numbers == 0) | (numbers == half_count), 1.0 / coeff_total, 2.0 / coeff_total)
    forward = normaliser[:, None] * inverse.T
    return (jnp.asarray(inverse, jnp.float32), jnp.asarray(slope, jnp.float32), jnp.asarray(forward, jnp.float32))

def transport(physical, stream_slope, cross_slope, span_slope, forward):
    product = -(physical[0:1] * stream_slope + physical[1:2] * cross_slope + physical[2:3] * span_slope)
    return jnp.einsum('cp,fp...->fc...', forward, product, precision=PRECISE)

def nonlinear(values, inverse, slope, forward, derivative):
    physical = jnp.einsum('pc,fc...->fp...', inverse, values, precision=PRECISE)
    span_slope = jnp.einsum('pc,fc...->fp...', slope, values, precision=PRECISE)
    stream_slope = 2.0 * jnp.einsum('ia,fpab...->fpib...', derivative, physical, precision=PRECISE)
    cross_slope = 2.0 * jnp.einsum('jb,fpab...->fpaj...', derivative, physical, precision=PRECISE)
    return transport(physical, stream_slope, cross_slope, span_slope, forward)

def operate(values, helmholtz, stiffness, quadrature):
    stream_part = jnp.einsum('ia,sajn->sijn', stiffness, values, precision=PRECISE) * quadrature[None, None, :, None]
    cross_part = jnp.einsum('jb,sibn->sijn', stiffness, values, precision=PRECISE) * quadrature[None, :, None, None]
    mass_diag = 0.25 * quadrature[:, None] * quadrature[None, :]
    return stream_part + cross_part + helmholtz[:, None, None, None] * mass_diag[None, :, :, None] * values

def assemble_with(element_values, row_count, prior_face, next_face):
    left_face = element_values[:, 0]
    right_face = element_values[:, -1]
    from_prior = jnp.concatenate([prior_face, right_face[..., :-row_count]], axis=-1)
    from_next = jnp.concatenate([left_face[..., row_count:], next_face], axis=-1)
    element_values = jnp.concatenate([(left_face + from_prior)[:, None], element_values[:, 1:-1], (right_face + from_next)[:, None]], axis=1)
    bottom_face = element_values[:, :, 0]
    top_face = element_values[:, :, -1]
    position = jnp.arange(element_values.shape[-1]) % row_count
    zero_column = jnp.zeros_like(bottom_face[..., :1])
    from_above = jnp.where(position != row_count - 1, jnp.concatenate([bottom_face[..., 1:], zero_column], axis=-1), 0.0)
    from_below = jnp.where(position != 0, jnp.concatenate([zero_column, top_face[..., :-1]], axis=-1), 0.0)
    return jnp.concatenate([(bottom_face + from_below)[:, :, None], element_values[:, :, 1:-1], (top_face + from_above)[:, :, None]], axis=2)

def boundary_tables(element_count, row_count, first_column, column_total):
    column = first_column + jnp.arange(element_count) // row_count
    row_index = jnp.arange(element_count) % row_count
    node_index = jnp.arange(7)
    west_side = (node_index == 0)[:, None, None]
    east_side = (node_index == 6)[:, None, None]
    south_side = (node_index == 0)[None, :, None]
    north_side = (node_index == 6)[None, :, None]
    fixed_node = south_side & (row_index == 0) | north_side & (row_index == row_count - 1) | west_side & (column == 0)
    dirichlet_keep = jnp.where(fixed_node, 0.0, 1.0)
    shared_horizontal = west_side & (column > 0) | east_side & (column < column_total - 1)
    shared_vertical = south_side & (row_index > 0) | north_side & (row_index < row_count - 1)
    weight = 1.0 / (jnp.where(shared_horizontal, 2.0, 1.0) * jnp.where(shared_vertical, 2.0, 1.0))
    return (dirichlet_keep, weight)

def reference(velocity, element_slot):
    block_size = EX * EY
    block_start = jnp.arange(ELEMS) // block_size * block_size
    gather_index = (block_start + element_slot).astype(jnp.int32)
    grid_field = jnp.take(velocity, gather_index, axis=4)
    quadrature, derivative, stiffness = gll_tables()
    inverse, slope, forward = fourier_tables(NCOEF)
    blocks = jnp.moveaxis(grid_field.reshape(3, NCOEF, 7, 7, N_MESH, block_size), 4, 0)

    def block_term(block_values):
        return nonlinear(block_values, inverse, slope, forward, derivative)
    terms = lax.map(block_term, blocks)
    nonlinear_modes = jnp.moveaxis(terms, 0, 4).reshape(3, NCOEF, 7, 7, ELEMS)
    mass_diag = 0.25 * quadrature[:, None] * quadrature[None, :]
    source = mass_diag[:, :, None] * (SIGMA_BASE * grid_field + STEP_TIME * nonlinear_modes)
    numbers = jnp.arange(NCOEF)
    wavenumber = jnp.where(numbers <= NCOEF // 2, numbers, numbers - NCOEF // 2).astype(jnp.float32)
    helmholtz = jnp.tile(SIGMA_BASE + (SPAN_WAVE * wavenumber) ** 2, 3)
    dirichlet_keep, weight = boundary_tables(ELEMS, EY, 0, ELEMS // EY)
    systems = source.reshape(3 * NCOEF // 8, 8, 7, 7, ELEMS)
    shifts = helmholtz.reshape(3 * NCOEF // 8, 8)

    def solve_group(group_pair):
        group_source, group_shift = group_pair
        edge_zeros = jnp.zeros((group_source.shape[0], 7, EY), group_source.dtype)

        def apply_operator(values):
            return dirichlet_keep * assemble_with(operate(values, group_shift, stiffness, quadrature), EY, edge_zeros, edge_zeros)

        def weighted_inner(left_values, right_values):
            return lax.optimization_barrier(jnp.sum(left_values * right_values * weight, axis=(1, 2, 3)))
        residual = dirichlet_keep * assemble_with(group_source, EY, edge_zeros, edge_zeros)
        direction = residual
        solution = jnp.zeros_like(residual)
        norm_now = weighted_inner(residual, residual)
        for iteration in range(ITERS):
            applied = apply_operator(direction)
            step_size = norm_now / weighted_inner(direction, applied)
            solution = solution + step_size[:, None, None, None] * direction
            residual = residual - step_size[:, None, None, None] * applied
            if iteration + 1 < ITERS:
                norm_next = weighted_inner(residual, residual)
                direction = residual + (norm_next / norm_now)[:, None, None, None] * direction
                norm_now = norm_next
        return solution
    solved = lax.map(solve_group, (systems, shifts))
    return solved.reshape(3, NCOEF, 7, 7, ELEMS)
```

```python
import functools

import jax
import jax.numpy as jnp
import numpy as np
from jax import lax
from jax.experimental import pallas as pl
from jax.experimental.pallas import tpu as pltpu
from jax.sharding import PartitionSpec as P

NODES = 7
FIELDS = 3
GROUPS = 8
LOCAL = 16
NCOEF = 128
LANES = 128
EY = 16
PLANES_PER_FIELD = NODES * NODES
SIGMA_BASE = 8.0
SPAN_WAVE = 0.25
STEP_TIME = 0.01
MOMENTS = 6


def gll_tables():
    inner_point = np.sqrt((5.0 - 2.0 * np.sqrt(5.0 / 3.0)) / 11.0)
    outer_point = np.sqrt((5.0 + 2.0 * np.sqrt(5.0 / 3.0)) / 11.0)
    points = np.array([-1.0, -outer_point, -inner_point, 0.0, inner_point, outer_point, 1.0])
    legendre_prev = points * 0.0 + 1.0
    legendre_now = points.copy()
    for degree in range(1, points.shape[0] - 1):
        legendre_next = ((2 * degree + 1) * points * legendre_now - degree * legendre_prev) / (
            degree + 1
        )
        legendre_prev = legendre_now
        legendre_now = legendre_next
    order_value = points.shape[0] - 1
    quadrature = 2.0 / (order_value * (order_value + 1) * legendre_now**2)
    counter = np.arange(points.shape[0])
    same_node = counter[:, None] == counter[None, :]
    distances = np.where(same_node, 1.0, points[:, None] - points[None, :])
    barycentric = 1.0 / np.prod(distances, axis=1)
    off_diagonal = np.where(same_node, 0.0, barycentric[None, :] / barycentric[:, None] / distances)
    derivative = np.where(same_node, -np.sum(off_diagonal, axis=1)[:, None], off_diagonal)
    stiffness = derivative.T @ (quadrature[:, None] * derivative)
    return quadrature, derivative, stiffness


def fourier_tables():
    half_count = NCOEF // 2
    planes = np.arange(NCOEF) * 2.0 * np.pi / NCOEF
    numbers = np.arange(NCOEF)
    wavenumber = np.where(numbers <= half_count, numbers, numbers - half_count)
    cosine_mask = (numbers <= half_count)[None, :]
    phase = planes[:, None] * wavenumber[None, :]
    inverse = np.where(cosine_mask, np.cos(phase), np.sin(phase))
    slope = SPAN_WAVE * wavenumber[None, :] * np.where(cosine_mask, -np.sin(phase), np.cos(phase))
    normaliser = np.where((numbers == 0) | (numbers == half_count), 1.0 / NCOEF, 2.0 / NCOEF)
    forward = normaliser[:, None] * inverse.T
    return inverse, slope, forward


QUAD, DERIV, STIFF = gll_tables()
SCALED_STIFF = STIFF / QUAD[:, None]
MASS = 0.25 * QUAD[:, None] * QUAD[None, :]


def split_table(table):
    high = np.asarray(table, np.float32).astype(jnp.bfloat16)
    low = (np.asarray(table, np.float64) - high.astype(np.float64)).astype(jnp.bfloat16)
    return high, low


def transform_tables():
    inverse, slope, forward = fourier_tables()
    t_high, t_low = split_table(np.concatenate([inverse, slope], axis=0))
    f_high, f_low = split_table(-STEP_TIME * forward)
    padded = np.zeros((8, 8))
    padded[:NODES, :NODES] = 2.0 * DERIV
    b_high, b_low = split_table(np.kron(padded.T, np.eye(EY)))
    return [
        np.concatenate([t_high, t_high], axis=1),
        t_low,
        np.concatenate([f_high, f_high], axis=1),
        f_low,
        np.concatenate([b_high, b_high], axis=0),
        b_low,
    ]


def split_value(value):
    high = value.astype(jnp.bfloat16)
    low = (value - high.astype(jnp.float32)).astype(jnp.bfloat16)
    return high, low


def dot(left, right):
    return jnp.dot(left, right, preferred_element_type=jnp.float32)


def swap_groups(tiles, group):
    tiles = list(tiles)
    for bit in (4, 2, 1):
        low = (group & bit) == 0
        new = list(tiles)
        for at in range(8):
            if at & bit:
                continue
            first, second = tiles[at], tiles[at + bit]
            if bit == 4:
                moved = pltpu.roll(jnp.where(low, second, first), 64, 1)
                new[at] = jnp.where(low, first, moved)
                new[at + bit] = jnp.where(low, moved, second)
            else:
                new[at] = jnp.where(low, first, pltpu.roll(second, EY * bit, 1))
                new[at + bit] = jnp.where(low, pltpu.roll(first, LANES - EY * bit, 1), second)
        tiles = new
    return tiles


def weighted_sum(coefficients, values):
    total = None
    for coefficient, value in zip(coefficients, values):
        term = float(coefficient) * value
        total = term if total is None else total + term
    return total


def line_product(matrix, line, sign):
    even = [line[k] + line[6 - k] for k in range(3)] + [line[3]]
    odd = [line[k] - line[6 - k] for k in range(3)]
    out = [None] * 7
    for i in range(3):
        even_row = [0.5 * (matrix[i, k] + matrix[i, 6 - k]) for k in range(3)] + [matrix[i, 3]]
        odd_row = [0.5 * (matrix[i, k] - matrix[i, 6 - k]) for k in range(3)]
        even_part = weighted_sum(even_row, even)
        odd_part = weighted_sum(odd_row, odd)
        out[i] = even_part + odd_part
        out[6 - i] = even_part - odd_part if sign > 0 else odd_part - even_part
    if sign > 0:
        out[3] = weighted_sum([matrix[3, k] for k in range(4)], even)
    else:
        out[3] = weighted_sum([matrix[3, k] for k in range(3)], odd)
    return out


def kernel(
    mesh_x,
    mesh_z,
    vel,
    slot,
    tt,
    tl,
    ff,
    fl,
    bb,
    bl,
    out,
    msg,
    recv1,
    phys,
    span,
    cross,
    send2,
    recv2,
    basis,
    moments,
    halo_send,
    halo_recv,
    red_x,
    red_z,
    send1_sem,
    recv1_sem,
    own1_sem,
    send2_sem,
    recv2_sem,
    own2_sem,
    halo_send_sem,
    halo_recv_sem,
    redx_send_sem,
    redx_recv_sem,
    redz_send_sem,
    redz_recv_sem,
):
    me = lax.axis_index("modes")
    strip = lax.axis_index("mesh")
    strips = mesh_x * mesh_z
    at_x = lax.rem(strip, mesh_x)
    at_z = strip // mesh_x
    following = lax.rem(strip + 1, strips)
    previous = lax.rem(strip + strips - 1, strips)

    def mode_peer(step):
        return lax.rem(me + step, GROUPS)

    def x_peer(step):
        return at_z * mesh_x + lax.rem(at_x + step, mesh_x)

    def z_peer(step):
        return lax.rem(at_z + step, mesh_z) * mesh_x + at_x

    barrier = pltpu.get_barrier_semaphore()
    greeted = [{"modes": mode_peer(step)} for step in range(1, GROUPS)]
    greeted += [{"mesh": following}, {"mesh": previous}]
    greeted += [{"mesh": x_peer(step)} for step in range(1, mesh_x)]
    greeted += [{"mesh": z_peer(step)} for step in range(1, mesh_z)]
    for device in greeted:
        pl.semaphore_signal(
            barrier, inc=1, device_id=device, device_id_type=pl.DeviceIdType.MESH
        )

    lane = lax.broadcasted_iota(jnp.int32, (8, LANES), 1)
    group = lane // EY
    row = lane % EY
    slots = jnp.broadcast_to(slot[...], (8, LANES))

    def remote(src, dst, send, recv, device):
        return pltpu.make_async_remote_copy(
            src_ref=src,
            dst_ref=dst,
            send_sem=send,
            recv_sem=recv,
            device_id=device,
            device_id_type=pl.DeviceIdType.MESH,
        )

    def out_copy(f, step):
        peer = mode_peer(step)
        return remote(
            msg.at[peer, pl.ds(f * NODES, NODES)],
            recv1.at[pl.ds(f * NODES, NODES), pl.ds(me * LOCAL, LOCAL)],
            send1_sem.at[f, step - 1],
            recv1_sem.at[f, step - 1],
            {"modes": peer},
        )

    def own_out(f):
        return pltpu.make_async_copy(
            msg.at[me, pl.ds(f * NODES, NODES)],
            recv1.at[pl.ds(f * NODES, NODES), pl.ds(me * LOCAL, LOCAL)],
            own1_sem.at[f],
        )

    def back_copy(f, step):
        peer = mode_peer(step)
        return remote(
            send2.at[pl.ds(f * NODES, NODES), pl.ds(peer * LOCAL, LOCAL)],
            recv2.at[me, pl.ds(f * NODES, NODES)],
            send2_sem.at[f, step - 1],
            recv2_sem.at[f, step - 1],
            {"modes": peer},
        )

    def own_back(f):
        return pltpu.make_async_copy(
            send2.at[pl.ds(f * NODES, NODES), pl.ds(me * LOCAL, LOCAL)],
            recv2.at[me, pl.ds(f * NODES, NODES)],
            own2_sem.at[f],
        )

    def spread_rows(f, i):
        for half in range(2):
            rows = pl.ds(8 * half, 8)
            tiles = []
            for j in range(NODES):
                at = f * PLANES_PER_FIELD + i * NODES + j
                tile = jnp.take_along_axis(vel[at, rows, :], slots, axis=1)
                out[at, rows, :] = SIGMA_BASE * tile
                tiles.append(tile)
            tiles = swap_groups(tiles + [jnp.zeros((8, LANES), jnp.float32)], group)
            for k in range(GROUPS):
                msg[k, f * NODES + i, rows, :] = tiles[k]

    for f in range(FIELDS):
        lax.fori_loop(0, NODES, lambda i, c, f=f: (spread_rows(f, i), c)[1], 0)
        if f == 0:
            pl.semaphore_wait(barrier, len(greeted))
        for step in range(1, GROUPS):
            out_copy(f, step).start()
        own_out(f).start()

    def to_planes(f, carry):
        for step in range(1, GROUPS):
            out_copy(f, step).wait_recv()
        own_out(f).wait()
        for i in range(NODES):
            at = f * NODES + i
            high, low = split_value(recv1[at])
            value = dot(tt[...], jnp.concatenate([high, low], axis=0)) + dot(tl[...], high)
            planes = value[:NCOEF]
            phys[at] = planes
            span[at] = value[NCOEF:]
            high, low = split_value(planes)
            cross[at] = dot(jnp.concatenate([high, low], axis=1), bb[...]) + dot(high, bl[...])
        return carry

    lax.fori_loop(0, FIELDS, to_planes, 0)

    def advect(f, carry):
        def rows_of(block, inner):
            rows = pl.ds(pl.multiple_of(block * 8, 8), 8)
            line = [phys[f * NODES + i, rows, :] for i in range(NODES)]
            stream = line_product(2.0 * DERIV, line, -1)
            for i in range(NODES):
                at = f * NODES + i
                send2[at, rows, :] = (
                    phys[i, rows, :] * stream[i]
                    + phys[NODES + i, rows, :] * cross[at, rows, :]
                    + phys[2 * NODES + i, rows, :] * span[at, rows, :]
                )
            return inner

        lax.fori_loop(0, NCOEF // 8, rows_of, 0)
        for i in range(NODES):
            at = f * NODES + i
            high, low = split_value(send2[at])
            send2[at] = dot(ff[...], jnp.concatenate([high, low], axis=0)) + dot(fl[...], high)
        for step in range(1, GROUPS):
            back_copy(f, step).start()
        own_back(f).start()
        return carry

    lax.fori_loop(0, FIELDS, advect, 0)

    def gather_source(f, carry):
        for step in range(1, GROUPS):
            back_copy(f, step).wait_recv()
        own_back(f).wait()
        for half in range(2):
            rows = pl.ds(8 * half, 8)
            for i in range(NODES):
                tiles = swap_groups(
                    [recv2[k, f * NODES + i, rows, :] for k in range(GROUPS)], group
                )
                for j in range(NODES):
                    at = f * PLANES_PER_FIELD + i * NODES + j
                    basis[0, at, rows, :] = float(MASS[i, j]) * (out[at, rows, :] + tiles[j])
        return carry

    lax.fori_loop(0, FIELDS, gather_source, 0)

    is_first = strip == 0
    is_last = strip == strips - 1
    inflow = jnp.logical_and(group == 0, is_first)
    not_inflow = jnp.logical_not(inflow)
    west = group == 0
    east = group == GROUPS - 1
    south = row != 0
    north = row != EY - 1
    has_previous = jnp.where(is_first, 0.0, 1.0)
    has_following = jnp.where(is_last, 0.0, 1.0)
    east_weight = jnp.where(jnp.logical_and(east, is_last), 1.0, 0.5)

    def halo_copies(level):
        return (
            remote(
                halo_send.at[level, 0],
                halo_recv.at[level, 0],
                halo_send_sem.at[level, 0],
                halo_recv_sem.at[level, 0],
                {"mesh": following},
            ),
            remote(
                halo_send.at[level, 1],
                halo_recv.at[level, 1],
                halo_send_sem.at[level, 1],
                halo_recv_sem.at[level, 1],
                {"mesh": previous},
            ),
        )

    def at_block(block):
        f = block // 2
        rows = pl.ds(pl.multiple_of((block % 2) * 8, 8), 8)
        return f, rows

    def send_faces(level):
        def pack(block, carry):
            f, rows = at_block(block)
            base = f * PLANES_PER_FIELD
            to_next = jnp.zeros((8, LANES), jnp.float32)
            to_prior = to_next
            for j in range(NODES):
                right = basis[level, base + 6 * NODES + j, rows, :]
                left = basis[level, base + j, rows, :]
                here = group == j
                to_next = jnp.where(here, pltpu.roll(right, (EY * (j + 1)) % LANES, 1), to_next)
                to_prior = jnp.where(
                    here, pltpu.roll(left, EY * j, 1) if j else left, to_prior
                )
            halo_send[level, 0, f, rows, :] = to_next
            halo_send[level, 1, f, rows, :] = to_prior
            return carry

        lax.fori_loop(0, 2 * FIELDS, pack, 0)
        for copy in halo_copies(level):
            copy.start()

    def along_rows(line):
        bottom, top = line[0], line[6]
        line[0] = jnp.where(south, bottom + pltpu.roll(top, 1, 1), 0.0)
        line[6] = jnp.where(north, top + pltpu.roll(bottom, LANES - 1, 1), 0.0)
        return line

    def squares(line, edge):
        total = line[1] * line[1]
        for j in range(2, 6):
            total = total + line[j] * line[j]
        return total + 0.5 * (line[0] * line[0] + line[6] * line[6])

    def finish_inside(level):
        def block_of(block, carry):
            f, rows = at_block(block)
            base = f * PLANES_PER_FIELD
            total = jnp.zeros((8, LANES), jnp.float32)
            for i in range(1, 6):
                line = [basis[level, base + i * NODES + j, rows, :] for j in range(NODES)]
                line = along_rows(line)
                basis[level, base + i * NODES, rows, :] = line[0]
                basis[level, base + i * NODES + 6, rows, :] = line[6]
                total = total + squares(line, None)
            moments[2 * level, f, rows, :] = total
            return carry

        lax.fori_loop(0, 2 * FIELDS, block_of, 0)

    def finish_faces(level):
        for copy in halo_copies(level):
            copy.wait_recv()

        def block_of(block, carry):
            f, rows = at_block(block)
            base = f * PLANES_PER_FIELD
            prior = halo_recv[level, 0, f, rows, :] * has_previous
            after = halo_recv[level, 1, f, rows, :] * has_following
            lefts, rights = [], []
            for j in range(NODES):
                left = basis[level, base + j, rows, :]
                right = basis[level, base + 6 * NODES + j, rows, :]
                from_prior = pltpu.roll(prior, LANES - EY * j, 1) if j else prior
                from_after = pltpu.roll(after, LANES - EY * (j + 1), 1) if j < 7 else after
                lefts.append(left + jnp.where(west, from_prior, pltpu.roll(right, EY, 1)))
                rights.append(
                    right + jnp.where(east, from_after, pltpu.roll(left, LANES - EY, 1))
                )
            lefts = [jnp.where(not_inflow, value, 0.0) for value in along_rows(lefts)]
            rights = along_rows(rights)
            for j in range(NODES):
                basis[level, base + j, rows, :] = lefts[j]
                basis[level, base + 6 * NODES + j, rows, :] = rights[j]
            moments[2 * level, f, rows, :] = (
                moments[2 * level, f, rows, :]
                + 0.5 * squares(lefts, None)
                + east_weight * squares(rights, None)
            )
            return carry

        lax.fori_loop(0, 2 * FIELDS, block_of, 0)

    def operate(level, keep_image):
        def block_of(block, carry):
            f, rows = at_block(block)
            base = f * PLANES_PER_FIELD
            number = (
                me * LOCAL
                + (block % 2) * 8
                + lax.broadcasted_iota(jnp.int32, (8, LANES), 0)
            )
            wave = SPAN_WAVE * jnp.where(number <= NCOEF // 2, number, number - NCOEF // 2).astype(
                jnp.float32
            )
            shift = 0.25 * (SIGMA_BASE + wave * wave)
            values = [basis[level, base + n, rows, :] for n in range(PLANES_PER_FIELD)]
            image = [None] * PLANES_PER_FIELD
            for j in range(NODES):
                line = line_product(SCALED_STIFF, [values[i * NODES + j] for i in range(NODES)], 1)
                for i in range(NODES):
                    image[i * NODES + j] = line[i]
            energy = jnp.zeros((8, LANES), jnp.float32)
            for i in range(NODES):
                line = line_product(SCALED_STIFF, values[i * NODES : (i + 1) * NODES], 1)
                for j in range(NODES):
                    n = i * NODES + j
                    result = float(QUAD[i] * QUAD[j]) * (image[n] + line[j] + shift * values[n])
                    energy = energy + result * values[n]
                    if keep_image:
                        basis[level + 1, base + n, rows, :] = result
            moments[2 * level + 1, f, rows, :] = energy
            return carry

        lax.fori_loop(0, 2 * FIELDS, block_of, 0)

    for level in range(3):
        send_faces(level)
        finish_inside(level)
        finish_faces(level)
        operate(level, level < 2)

    packed = jnp.zeros((8, LANES), jnp.float32)
    for m in range(MOMENTS):
        for block in range(2 * FIELDS):
            f, half = block // 2, block % 2
            total = jnp.sum(moments[m, f, 8 * half : 8 * half + 8, :], axis=1, keepdims=True)
            packed = jnp.where(lane == 8 * block + m, total, packed)

    def sum_over(value, slots_ref, mine, count, copies):
        slots_ref[mine] = value
        for copy in copies:
            copy.start()
        for copy in copies:
            copy.wait_recv()
        total = slots_ref[0]
        for k in range(1, count):
            total = total + slots_ref[k]
        return total

    x_copies = [
        remote(
            red_x.at[at_x],
            red_x.at[at_x],
            redx_send_sem.at[step - 1],
            redx_recv_sem.at[step - 1],
            {"mesh": x_peer(step)},
        )
        for step in range(1, mesh_x)
    ]
    z_copies = [
        remote(
            red_z.at[at_z],
            red_z.at[at_z],
            redz_send_sem.at[step - 1],
            redz_recv_sem.at[step - 1],
            {"mesh": z_peer(step)},
        )
        for step in range(1, mesh_z)
    ]
    packed = sum_over(packed, red_x, at_x, mesh_x, x_copies)
    packed = sum_over(packed, red_z, at_z, mesh_z, z_copies)

    m0, m1, m2, m3, m4, m5 = [
        packed if m == 0 else pltpu.roll(packed, LANES - m, 1) for m in range(MOMENTS)
    ]
    s0, s1, s2 = lax.rsqrt(m1), lax.rsqrt(m3), lax.rsqrt(m5)
    l10 = m2 * s0 * s1
    l20 = m3 * s0 * s2
    h21 = m4 * s1 * s2
    d1 = 1.0 - l10 * l10
    l21 = (h21 - l20 * l10) / d1
    d2 = 1.0 - l20 * l20 - l21 * l21 * d1
    y0 = m0 * s0
    y1 = m1 * s1 - l10 * y0
    y2 = m2 * s2 - l20 * y0 - l21 * y1
    c2 = y2 / d2
    c1 = y1 / d1 - l21 * c2
    c0 = y0 - l10 * c1 - l20 * c2
    c0, c1, c2 = c0 * s0, c1 * s1, c2 * s2

    for block in range(2 * FIELDS):
        f, half = block // 2, block % 2
        rows = pl.ds(8 * half, 8)
        f0, f1, f2 = [
            jnp.broadcast_to(c[:, 8 * block : 8 * block + 1], (8, LANES)) for c in (c0, c1, c2)
        ]

        def combine(n, carry, f=f, rows=rows, f0=f0, f1=f1, f2=f2):
            at = f * PLANES_PER_FIELD + n
            out[at, rows, :] = (
                f0 * basis[0, at, rows, :] + f1 * basis[1, at, rows, :] + f2 * basis[2, at, rows, :]
            )
            return carry

        lax.fori_loop(0, PLANES_PER_FIELD, combine, 0, unroll=7)

    for f in range(FIELDS):
        for step in range(1, GROUPS):
            out_copy(f, step).wait_send()
            back_copy(f, step).wait_send()
    for level in range(3):
        for copy in halo_copies(level):
            copy.wait_send()
    for copy in x_copies + z_copies:
        copy.wait_send()


def shards(mesh_x, mesh_z, velocity, element_slot):
    tables = [jnp.asarray(table) for table in transform_tables()]
    count = FIELDS * PLANES_PER_FIELD
    field = jnp.transpose(velocity, (0, 2, 3, 1, 4)).reshape(count, LOCAL, LANES)
    vmem = pl.BlockSpec(memory_space=pltpu.VMEM)
    lines = FIELDS * NODES
    f32 = jnp.float32
    dma = pltpu.SemaphoreType.DMA
    result = pl.pallas_call(
        functools.partial(kernel, mesh_x, mesh_z),
        out_shape=jax.ShapeDtypeStruct((count, LOCAL, LANES), f32),
        in_specs=[vmem] * 8,
        out_specs=vmem,
        scratch_shapes=[
            pltpu.VMEM((GROUPS, lines, LOCAL, LANES), f32),
            pltpu.VMEM((lines, NCOEF, LANES), f32),
            pltpu.VMEM((lines, NCOEF, LANES), f32),
            pltpu.VMEM((lines, NCOEF, LANES), f32),
            pltpu.VMEM((lines, NCOEF, LANES), f32),
            pltpu.VMEM((lines, NCOEF, LANES), f32),
            pltpu.VMEM((GROUPS, lines, LOCAL, LANES), f32),
            pltpu.VMEM((3, count, LOCAL, LANES), f32),
            pltpu.VMEM((MOMENTS, FIELDS, LOCAL, LANES), f32),
            pltpu.VMEM((3, 2, FIELDS, LOCAL, LANES), f32),
            pltpu.VMEM((3, 2, FIELDS, LOCAL, LANES), f32),
            pltpu.VMEM((mesh_x, 8, LANES), f32),
            pltpu.VMEM((mesh_z, 8, LANES), f32),
            dma((FIELDS, GROUPS - 1)),
            dma((FIELDS, GROUPS - 1)),
            dma((FIELDS,)),
            dma((FIELDS, GROUPS - 1)),
            dma((FIELDS, GROUPS - 1)),
            dma((FIELDS,)),
            dma((3, 2)),
            dma((3, 2)),
            dma((mesh_x - 1,)),
            dma((mesh_x - 1,)),
            dma((mesh_z - 1,)),
            dma((mesh_z - 1,)),
        ],
        compiler_params=pltpu.CompilerParams(
            collective_id=0, has_side_effects=True, vmem_limit_bytes=40 * 1024 * 1024
        ),
    )(field, element_slot.reshape(1, LANES), *tables)
    return jnp.transpose(
        result.reshape(FIELDS, NODES, NODES, LOCAL, LANES), (0, 3, 1, 2, 4)
    )


def solution(mesh):
    strips = mesh.shape["mesh"]
    mesh_x = 4 if strips % 4 == 0 else 1
    placed = (P(None, "modes", None, None, "mesh"), P("mesh"))
    return jax.shard_map(
        functools.partial(shards, mesh_x, strips // mesh_x),
        mesh=mesh,
        in_specs=placed,
        out_specs=P(None, "modes", None, None, "mesh"),
        check_vma=False,
    )
```

```python
import functools

import jax
import jax.numpy as jnp
import numpy as np
from jax import lax
from jax.experimental import pallas as pl
from jax.experimental.pallas import tpu as pltpu
from jax.sharding import PartitionSpec as P

NODES = 7
FIELDS = 3
GROUPS = 8
LOCAL = 16
NCOEF = 128
LANES = 128
EY = 16
PLANES_PER_FIELD = NODES * NODES
SIGMA_BASE = 8.0
SPAN_WAVE = 0.25
STEP_TIME = 0.01
MOMENTS = 6
TILES = 19
OUT_PARTS = ((0, 7), (7, 6), (13, 6))
BACK_PARTS = ((0, 6), (6, 6), (12, 7))


def gll_tables():
    inner_point = np.sqrt((5.0 - 2.0 * np.sqrt(5.0 / 3.0)) / 11.0)
    outer_point = np.sqrt((5.0 + 2.0 * np.sqrt(5.0 / 3.0)) / 11.0)
    points = np.array([-1.0, -outer_point, -inner_point, 0.0, inner_point, outer_point, 1.0])
    legendre_prev = points * 0.0 + 1.0
    legendre_now = points.copy()
    for degree in range(1, points.shape[0] - 1):
        legendre_next = ((2 * degree + 1) * points * legendre_now - degree * legendre_prev) / (
            degree + 1
        )
        legendre_prev = legendre_now
        legendre_now = legendre_next
    order_value = points.shape[0] - 1
    quadrature = 2.0 / (order_value * (order_value + 1) * legendre_now**2)
    counter = np.arange(points.shape[0])
    same_node = counter[:, None] == counter[None, :]
    distances = np.where(same_node, 1.0, points[:, None] - points[None, :])
    barycentric = 1.0 / np.prod(distances, axis=1)
    off_diagonal = np.where(same_node, 0.0, barycentric[None, :] / barycentric[:, None] / distances)
    derivative = np.where(same_node, -np.sum(off_diagonal, axis=1)[:, None], off_diagonal)
    stiffness = derivative.T @ (quadrature[:, None] * derivative)
    return quadrature, derivative, stiffness


def fourier_tables():
    half_count = NCOEF // 2
    planes = np.arange(NCOEF) * 2.0 * np.pi / NCOEF
    numbers = np.arange(NCOEF)
    wavenumber = np.where(numbers <= half_count, numbers, numbers - half_count)
    cosine_mask = (numbers <= half_count)[None, :]
    phase = planes[:, None] * wavenumber[None, :]
    inverse = np.where(cosine_mask, np.cos(phase), np.sin(phase))
    slope = SPAN_WAVE * wavenumber[None, :] * np.where(cosine_mask, -np.sin(phase), np.cos(phase))
    normaliser = np.where((numbers == 0) | (numbers == half_count), 1.0 / NCOEF, 2.0 / NCOEF)
    forward = normaliser[:, None] * inverse.T
    return inverse, slope, forward


QUAD, DERIV, STIFF = gll_tables()
SCALED_STIFF = STIFF / QUAD[:, None]
MASS = 0.25 * QUAD[:, None] * QUAD[None, :]


def split_table(table):
    high = np.asarray(table, np.float32).astype(jnp.bfloat16)
    low = (np.asarray(table, np.float64) - high.astype(np.float64)).astype(jnp.bfloat16)
    return high, low


def transform_tables():
    inverse, slope, forward = fourier_tables()
    t_high, t_low = split_table(np.concatenate([inverse, slope], axis=0))
    f_high, f_low = split_table(-STEP_TIME * forward)
    padded = np.zeros((8, 8))
    padded[:NODES, :NODES] = 2.0 * DERIV
    b_high, b_low = split_table(np.kron(padded.T, np.eye(EY)))
    return np.concatenate(
        [
            np.concatenate([t_high, t_high], axis=1),
            np.concatenate([t_low, np.concatenate([b_high, b_high], axis=0)], axis=1),
            np.concatenate([f_high, f_high], axis=1),
            np.concatenate([f_low, b_low], axis=1),
        ],
        axis=0,
    )


def split_value(value):
    high = value.astype(jnp.bfloat16)
    low = (value - high.astype(jnp.float32)).astype(jnp.bfloat16)
    return high, low


def dot(left, right):
    return jnp.dot(left, right, preferred_element_type=jnp.float32)


def swap_groups(tiles, group):
    tiles = list(tiles)
    for bit in (4, 2, 1):
        low = (group & bit) == 0
        new = list(tiles)
        for at in range(8):
            if at & bit:
                continue
            first, second = tiles[at], tiles[at + bit]
            if bit == 4:
                moved = pltpu.roll(jnp.where(low, second, first), 64, 1)
                new[at] = jnp.where(low, first, moved)
                new[at + bit] = jnp.where(low, moved, second)
            else:
                new[at] = jnp.where(low, first, pltpu.roll(second, EY * bit, 1))
                new[at + bit] = jnp.where(low, pltpu.roll(first, LANES - EY * bit, 1), second)
        tiles = new
    return tiles


def weighted_sum(coefficients, values):
    total = None
    for coefficient, value in zip(coefficients, values):
        if value is None:
            continue
        term = float(coefficient) * value
        total = term if total is None else total + term
    return total


def line_product(matrix, line, sign):
    pairs = [(line[k], line[6 - k]) for k in range(3)]
    even = [None if a is None else a + b for a, b in pairs] + [line[3]]
    odd = [None if a is None else a - b for a, b in pairs]
    out = [None] * 7
    for i in range(3):
        even_row = [0.5 * (matrix[i, k] + matrix[i, 6 - k]) for k in range(3)] + [matrix[i, 3]]
        odd_row = [0.5 * (matrix[i, k] - matrix[i, 6 - k]) for k in range(3)]
        even_part = weighted_sum(even_row, even)
        odd_part = weighted_sum(odd_row, odd)
        out[i] = even_part + odd_part
        out[6 - i] = even_part - odd_part if sign > 0 else odd_part - even_part
    if sign > 0:
        out[3] = weighted_sum([matrix[3, k] for k in range(4)], even)
    else:
        out[3] = weighted_sum([matrix[3, k] for k in range(3)], odd)
    return out


def kernel(
    mesh_x,
    mesh_z,
    vel_hbm,
    slot_hbm,
    table_hbm,
    out,
    vel,
    slot,
    table,
    msg,
    recv1,
    phys,
    span,
    cross,
    send2,
    recv2,
    basis,
    last_faces,
    edge_tile,
    edge_recv,
    moments,
    halo_send,
    halo_recv,
    red_x,
    red_z,
    send1_sem,
    recv1_sem,
    own1_sem,
    send2_sem,
    recv2_sem,
    own2_sem,
    halo_send_sem,
    halo_recv_sem,
    redx_send_sem,
    redx_recv_sem,
    redz_send_sem,
    redz_recv_sem,
    load_sem,
    edge_send_sem,
    edge_recv_sem,
):
    def vel_load(f):
        part = pl.ds(f * PLANES_PER_FIELD, PLANES_PER_FIELD)
        return pltpu.make_async_copy(vel_hbm.at[part], vel.at[part], load_sem.at[f])

    slot_load = pltpu.make_async_copy(slot_hbm, slot, load_sem.at[FIELDS])
    table_load = pltpu.make_async_copy(table_hbm, table, load_sem.at[FIELDS + 1])
    slot_load.start()
    for f in range(FIELDS):
        vel_load(f).start()
    table_load.start()

    me = lax.axis_index("modes")
    strip = lax.axis_index("mesh")
    strips = mesh_x * mesh_z
    at_x = lax.rem(strip, mesh_x)
    at_z = strip // mesh_x
    following = lax.rem(strip + 1, strips)
    previous = lax.rem(strip + strips - 1, strips)

    def mode_peer(step):
        return lax.rem(me + step, GROUPS)

    def x_peer(step):
        return at_z * mesh_x + lax.rem(at_x + step, mesh_x)

    def z_peer(step):
        return lax.rem(at_z + step, mesh_z) * mesh_x + at_x

    barrier = pltpu.get_barrier_semaphore()
    greeted = [{"modes": mode_peer(step)} for step in range(1, GROUPS)]
    greeted += [{"mesh": following}, {"mesh": previous}]
    greeted += [{"mesh": x_peer(step)} for step in range(1, mesh_x)]
    greeted += [{"mesh": z_peer(step)} for step in range(1, mesh_z)]
    greeted += [{"modes": 0, "mesh": following}, {"modes": GROUPS - 1, "mesh": previous}]
    greetings = len(greeted) - 2
    greetings += jnp.where(jnp.logical_or(me == 0, me == GROUPS - 1), GROUPS, 0)
    for device in greeted:
        pl.semaphore_signal(
            barrier, inc=1, device_id=device, device_id_type=pl.DeviceIdType.MESH
        )

    lane = lax.broadcasted_iota(jnp.int32, (8, LANES), 1)
    group = lane // EY
    row = lane % EY
    slot_load.wait()
    slots = jnp.broadcast_to(slot[...], (8, LANES))

    def remote(src, dst, send, recv, device):
        return pltpu.make_async_remote_copy(
            src_ref=src,
            dst_ref=dst,
            send_sem=send,
            recv_sem=recv,
            device_id=device,
            device_id_type=pl.DeviceIdType.MESH,
        )

    def out_copy(f, step):
        peer = mode_peer(step)
        part = pl.ds(*OUT_PARTS[f])
        return remote(
            msg.at[peer, part],
            recv1.at[part, pl.ds(me * LOCAL, LOCAL)],
            send1_sem.at[f, step - 1],
            recv1_sem.at[f, step - 1],
            {"modes": peer},
        )

    def own_out(f):
        part = pl.ds(*OUT_PARTS[f])
        return pltpu.make_async_copy(
            msg.at[me, part], recv1.at[part, pl.ds(me * LOCAL, LOCAL)], own1_sem.at[f]
        )

    def back_copy(f, step):
        peer = mode_peer(step)
        part = pl.ds(*BACK_PARTS[f])
        return remote(
            send2.at[part, pl.ds(peer * LOCAL, LOCAL)],
            recv2.at[me, part],
            send2_sem.at[f, step - 1],
            recv2_sem.at[f, step - 1],
            {"modes": peer},
        )

    def own_back(f):
        part = pl.ds(*BACK_PARTS[f])
        return pltpu.make_async_copy(
            send2.at[part, pl.ds(me * LOCAL, LOCAL)], recv2.at[me, part], own2_sem.at[f]
        )

    def edge_copy(side, f, owner):
        return remote(
            (edge_tile if side == 0 else send2).at[
                f if side == 0 else f * 6, pl.ds(pl.multiple_of(owner * LOCAL, LOCAL), LOCAL)
            ],
            edge_recv.at[side, f],
            edge_send_sem.at[side, f, owner],
            edge_recv_sem.at[side, f],
            {"modes": owner, "mesh": following if side == 0 else previous},
        )

    def for_edges(action):
        for side, worker in ((0, GROUPS - 1), (1, 0)):

            @pl.when(me == worker)
            def _(side=side):
                def each(owner, carry):
                    action(side, owner)
                    return carry

                lax.fori_loop(0, GROUPS, each, 0)

    def halo_copies(level):
        return (
            remote(
                halo_send.at[level, 0],
                halo_recv.at[level, 0],
                halo_send_sem.at[level, 0],
                halo_recv_sem.at[level, 0],
                {"mesh": following},
            ),
            remote(
                halo_send.at[level, 1],
                halo_recv.at[level, 1],
                halo_send_sem.at[level, 1],
                halo_recv_sem.at[level, 1],
                {"mesh": previous},
            ),
        )

    def pack_faces(level, f, rows, lefts, rights):
        to_next = pltpu.roll(rights[0], EY, 1)
        to_prior = lefts[0]
        for j in range(1, NODES):
            here = group == j
            right = pltpu.roll(rights[j], EY * (j + 1), 1)
            to_next = jnp.where(here, right, to_next)
            to_prior = jnp.where(here, pltpu.roll(lefts[j], EY * j, 1), to_prior)
        halo_send[level, 0, f, rows, :] = to_next
        halo_send[level, 1, f, rows, :] = to_prior

    def order_line(f, i):
        for half in range(2):
            rows = pl.ds(8 * half, 8)
            for j in range(NODES):
                at = f * PLANES_PER_FIELD + i * NODES + j
                vel[at, rows, :] = jnp.take_along_axis(vel[at, rows, :], slots, axis=1)

    def spread_line(f, i):
        for half in range(2):
            rows = pl.ds(8 * half, 8)
            base = f * PLANES_PER_FIELD
            tiles = [vel[base + i * NODES + j, rows, :] for j in range(NODES)]
            tiles = swap_groups(tiles + [vel[base + 42 + i, rows, :]], group)
            for k in range(GROUPS):
                msg[k, 1 + f * 6 + i, rows, :] = tiles[k]

    for f in range(FIELDS):
        vel_load(f).wait()
        order_line(f, 6)
    for half in range(2):
        rows = pl.ds(8 * half, 8)
        zero = jnp.zeros((8, LANES), jnp.float32)
        tiles = [vel[f * PLANES_PER_FIELD + 48, rows, :] for f in range(FIELDS)]
        tiles = swap_groups(tiles + [zero] * 5, group)
        for k in range(GROUPS):
            msg[k, 0, rows, :] = tiles[k]
    for f in range(FIELDS):

        def one_line(i, carry, f=f):
            order_line(f, i)
            spread_line(f, i)
            return carry

        lax.fori_loop(0, NODES - 1, one_line, 0)
        if f == 0:
            pl.semaphore_wait(barrier, greetings)
        for step in range(1, GROUPS):
            out_copy(f, step).start()
        own_out(f).start()

    for f in range(FIELDS):
        base = f * PLANES_PER_FIELD
        for half in range(2):
            rows = pl.ds(8 * half, 8)
            lefts = [vel[base + j, rows, :] for j in range(NODES)]
            rights = [vel[base + 42 + j, rows, :] for j in range(NODES)]
            pack_faces(0, f, rows, lefts, rights)
    for copy in halo_copies(0):
        copy.start()

    table_load.wait()
    tt, tl, bb = table.at[0:256, :], table.at[256:512, 0:128], table.at[256:512, 128:256]
    ff, fl, bl = table.at[512:640, :], table.at[640:768, 0:128], table.at[640:768, 128:256]
    group_all = lax.broadcasted_iota(jnp.int32, (NCOEF, LANES), 1) // EY

    def shifted(value, slots_up):
        return pltpu.roll(value, (EY * slots_up) % LANES, 1) if slots_up % GROUPS else value

    for f in range(FIELDS):
        for step in range(1, GROUPS):
            out_copy(f, step).wait_recv()
        own_out(f).wait()
        last = jnp.where(group_all == 6, shifted(recv1[0], 6 - f), 0.0)
        for i in range(6):
            last = jnp.where(group_all == i, shifted(recv1[1 + f * 6 + i], i - 7), last)
        for i in range(NODES):
            at = f * NODES + i
            high, low = split_value(recv1[1 + f * 6 + i] if i < 6 else last)
            value = dot(tt[...], jnp.concatenate([high, low], axis=0)) + dot(tl[...], high)
            planes = value[:NCOEF]
            phys[at] = planes
            span[at] = value[NCOEF:]
            high, low = split_value(planes)
            cross[at] = dot(jnp.concatenate([high, low], axis=1), bb[...]) + dot(high, bl[...])

    rest = jnp.zeros((NCOEF, LANES), jnp.float32)
    for f in range(FIELDS):

        def rows_of(block, inner, f=f):
            rows = pl.ds(pl.multiple_of(block * 8, 8), 8)
            line = [phys[f * NODES + i, rows, :] for i in range(NODES)]
            stream = line_product(2.0 * DERIV, line, -1)
            for i in range(NODES):
                at = f * NODES + i
                cross[at, rows, :] = (
                    phys[i, rows, :] * stream[i]
                    + phys[NODES + i, rows, :] * cross[at, rows, :]
                    + phys[2 * NODES + i, rows, :] * span[at, rows, :]
                )
            return inner

        lax.fori_loop(0, NCOEF // 8, rows_of, 0)
        for i in (6, 0, 1, 2, 3, 4, 5):
            high, low = split_value(cross[f * NODES + i])
            value = dot(ff[...], jnp.concatenate([high, low], axis=0)) + dot(fl[...], high)
            if i == 6:
                last = value
                edge_tile[f] = value
                rest = jnp.where(group_all == f, shifted(value, f - 6), rest)
            else:
                send2[f * 6 + i] = jnp.where(group_all == 7, shifted(last, 7 - i), value)
        if f == FIELDS - 1:
            send2[TILES - 1] = rest
        for_edges(lambda side, owner, f=f: edge_copy(side, f, owner).start())
        for step in range(1, GROUPS):
            back_copy(f, step).start()
        own_back(f).start()

    is_first = strip == 0
    is_last = strip == strips - 1
    not_inflow = jnp.logical_not(jnp.logical_and(group == 0, is_first))
    west = group == 0
    east = group == GROUPS - 1
    south = row != 0
    north = row != EY - 1
    has_previous = jnp.where(is_first, 0.0, 1.0)
    has_following = jnp.where(is_last, 0.0, 1.0)
    east_weight = jnp.where(jnp.logical_and(east, is_last), 1.0, 0.5)

    def at_block(block):
        f = block // 2
        rows = pl.ds(pl.multiple_of((block % 2) * 8, 8), 8)
        return f, rows

    def over_blocks(body, first=0, last=2 * FIELDS):
        lax.fori_loop(first, last, lambda block, c: (body(block), c)[1], 0, unroll=2)

    def gather_source(f):
        for step in range(1, GROUPS):
            back_copy(f, step).wait_recv()
        own_back(f).wait()
        base = f * PLANES_PER_FIELD
        for half in range(2):
            rows = pl.ds(8 * half, 8)
            for i in range(6):
                tiles = swap_groups([recv2[k, f * 6 + i, rows, :] for k in range(GROUPS)], group)
                for j in range(8):
                    a, b = (i, j) if j < 7 else (6, i)
                    at = base + a * NODES + b
                    basis[0, at, rows, :] = float(MASS[a, b]) * (
                        SIGMA_BASE * vel[at, rows, :] + tiles[j]
                    )

    def gather_rest():
        for half in range(2):
            rows = pl.ds(8 * half, 8)
            tiles = swap_groups([recv2[k, TILES - 1, rows, :] for k in range(GROUPS)], group)
            for f in range(FIELDS):
                at = f * PLANES_PER_FIELD + 48
                basis[0, at, rows, :] = float(MASS[6, 6]) * (
                    SIGMA_BASE * vel[at, rows, :] + tiles[f]
                )

    def along_rows(line):
        bottom, top = line[0], line[6]
        first = jnp.where(south, bottom + pltpu.roll(top, 1, 1), 0.0)
        last = jnp.where(north, top + pltpu.roll(bottom, LANES - 1, 1), 0.0)
        return [first] + list(line[1:6]) + [last]

    def squares(line):
        total = line[1] * line[1]
        for j in range(2, 6):
            total = total + line[j] * line[j]
        return total + 0.5 * (line[0] * line[0] + line[6] * line[6])

    def shift_of(block):
        number = (
            me * LOCAL + (block % 2) * 8 + lax.broadcasted_iota(jnp.int32, (8, LANES), 0)
        )
        wave = jnp.where(number <= NCOEF // 2, number, number - NCOEF // 2).astype(jnp.float32)
        wave = SPAN_WAVE * wave
        return 0.25 * (SIGMA_BASE + wave * wave)

    def finish_inside(level, first=0, last=2 * FIELDS):
        def block_of(block):
            f, rows = at_block(block)
            base = f * PLANES_PER_FIELD
            shift = shift_of(block)
            total = jnp.zeros((8, LANES), jnp.float32)
            inside = []
            for i in range(1, 6):
                line = []
                for j in range(NODES):
                    value = basis[level, base + i * NODES + j, rows, :]
                    if level:
                        value = float(QUAD[i] * QUAD[j]) * (
                            value
                            + float(SCALED_STIFF[i, 0]) * basis[level - 1, base + j, rows, :]
                            + float(SCALED_STIFF[i, 6]) * basis[level - 1, base + 42 + j, rows, :]
                        )
                    line.append(value)
                line = along_rows(line)
                for j in range(NODES):
                    if level or j in (0, 6):
                        basis[level, base + i * NODES + j, rows, :] = line[j]
                total = total + squares(line)
                inside.append(line)
            image = [None] * PLANES_PER_FIELD
            for j in range(NODES):
                column = [None] + [line[j] for line in inside] + [None]
                column = line_product(SCALED_STIFF, column, 1)
                for i in range(NODES):
                    image[i * NODES + j] = column[i]
            energy = jnp.zeros((8, LANES), jnp.float32)
            for i in range(1, 6):
                line = line_product(SCALED_STIFF, inside[i - 1], 1)
                for j in range(NODES):
                    n = i * NODES + j
                    image[n] = image[n] + line[j] + shift * inside[i - 1][j]
                    energy = energy + float(QUAD[i] * QUAD[j]) * (image[n] * inside[i - 1][j])
            for n in range(PLANES_PER_FIELD):
                if level < 2:
                    basis[level + 1, base + n, rows, :] = image[n]
                elif n < 7:
                    last_faces[0, f, n, rows, :] = image[n]
                elif n >= 42:
                    last_faces[1, f, n - 42, rows, :] = image[n]
            moments[2 * level, f, rows, :] = total
            moments[2 * level + 1, f, rows, :] = energy

        over_blocks(block_of, first, last)

    def finish_faces(level):
        def block_of(block):
            f, rows = at_block(block)
            base = f * PLANES_PER_FIELD
            shift = shift_of(block)
            prior = halo_recv[level, 0, f, rows, :]
            after = halo_recv[level, 1, f, rows, :]
            if level == 0:
                prior = SIGMA_BASE * prior + edge_recv[0, f, rows, :]
                after = SIGMA_BASE * after + edge_recv[1, f, rows, :]
            prior = prior * has_previous
            after = after * has_following
            lefts, rights = [], []
            for j in range(NODES):
                left = basis[level, base + j, rows, :]
                right = basis[level, base + 42 + j, rows, :]
                from_prior = pltpu.roll(prior, LANES - EY * j, 1) if j else prior
                from_after = pltpu.roll(after, LANES - EY * (j + 1), 1)
                if level == 0:
                    from_prior = float(MASS[6, j]) * from_prior
                    from_after = float(MASS[0, j]) * from_after
                lefts.append(left + jnp.where(west, from_prior, pltpu.roll(right, EY, 1)))
                rights.append(
                    right + jnp.where(east, from_after, pltpu.roll(left, LANES - EY, 1))
                )
            lefts = [jnp.where(not_inflow, value, 0.0) for value in along_rows(lefts)]
            rights = along_rows(rights)
            moments[2 * level, f, rows, :] = (
                moments[2 * level, f, rows, :]
                + 0.5 * squares(lefts)
                + east_weight * squares(rights)
            )
            energy = moments[2 * level + 1, f, rows, :]
            images = []
            for i, line in ((0, lefts), (6, rights)):
                across = line_product(SCALED_STIFF, line, 1)
                image = []
                for j in range(NODES):
                    basis[level, base + i * NODES + j, rows, :] = line[j]
                    if level < 2:
                        part = basis[level + 1, base + i * NODES + j, rows, :]
                    else:
                        part = last_faces[i // 6, f, j, rows, :]
                    whole = (
                        part
                        + float(SCALED_STIFF[i, 0]) * lefts[j]
                        + float(SCALED_STIFF[i, 6]) * rights[j]
                        + across[j]
                        + shift * line[j]
                    )
                    weight = float(QUAD[i] * QUAD[j])
                    energy = energy + weight * ((whole + part) * line[j])
                    if level < 2:
                        whole = weight * whole
                        basis[level + 1, base + i * NODES + j, rows, :] = whole
                        image.append(whole)
                images.append(image)
            moments[2 * level + 1, f, rows, :] = energy
            if level < 2:
                pack_faces(level + 1, f, rows, images[0], images[1])

        over_blocks(block_of)

    def pack_moments(packed, which):
        for m in which:
            for block in range(2 * FIELDS):
                f, half = block // 2, block % 2
                total = jnp.sum(moments[m, f, 8 * half : 8 * half + 8, :], axis=1, keepdims=True)
                packed = jnp.where(lane == 8 * block + m, total, packed)
        return packed

    packed = jnp.zeros((8, LANES), jnp.float32)
    for level in range(3):
        if level == 0:
            for f in range(FIELDS):
                gather_source(f)
                finish_inside(0, 2 * f, 2 * f + 2)
                for side in range(2):
                    edge_copy(side, f, 0).wait_recv()
            gather_rest()
        else:
            finish_inside(level)
            packed = pack_moments(packed, (2 * level - 2, 2 * level - 1))
        for copy in halo_copies(level):
            copy.wait_recv()
        finish_faces(level)
        if level < 2:
            for copy in halo_copies(level + 1):
                copy.start()
    packed = pack_moments(packed, (4, 5))

    def sum_over(value, slots_ref, mine, count, copies):
        slots_ref[mine] = value
        for copy in copies:
            copy.start()
        for copy in copies:
            copy.wait_recv()
        total = slots_ref[0]
        for k in range(1, count):
            total = total + slots_ref[k]
        return total

    x_copies = [
        remote(
            red_x.at[at_x],
            red_x.at[at_x],
            redx_send_sem.at[step - 1],
            redx_recv_sem.at[step - 1],
            {"mesh": x_peer(step)},
        )
        for step in range(1, mesh_x)
    ]
    z_copies = [
        remote(
            red_z.at[at_z],
            red_z.at[at_z],
            redz_send_sem.at[step - 1],
            redz_recv_sem.at[step - 1],
            {"mesh": z_peer(step)},
        )
        for step in range(1, mesh_z)
    ]
    packed = sum_over(packed, red_x, at_x, mesh_x, x_copies)
    packed = sum_over(packed, red_z, at_z, mesh_z, z_copies)

    m0, m1, m2, m3, m4, m5 = [
        packed if m == 0 else pltpu.roll(packed, LANES - m, 1) for m in range(MOMENTS)
    ]
    s0, s1, s2 = lax.rsqrt(m1), lax.rsqrt(m3), lax.rsqrt(m5)
    l10 = m2 * s0 * s1
    l20 = m3 * s0 * s2
    h21 = m4 * s1 * s2
    d1 = 1.0 - l10 * l10
    l21 = (h21 - l20 * l10) / d1
    d2 = 1.0 - l20 * l20 - l21 * l21 * d1
    y0 = m0 * s0
    y1 = m1 * s1 - l10 * y0
    y2 = m2 * s2 - l20 * y0 - l21 * y1
    c2 = y2 / d2
    c1 = y1 / d1 - l21 * c2
    c0 = y0 - l10 * c1 - l20 * c2
    c0, c1, c2 = c0 * s0, c1 * s1, c2 * s2

    for block in range(2 * FIELDS):
        f, half = block // 2, block % 2
        rows = pl.ds(8 * half, 8)
        f0, f1, f2 = [
            jnp.broadcast_to(c[:, 8 * block : 8 * block + 1], (8, LANES)) for c in (c0, c1, c2)
        ]

        def combine(n, carry, f=f, rows=rows, f0=f0, f1=f1, f2=f2):
            at = f * PLANES_PER_FIELD + n
            out[at, rows, :] = (
                f0 * basis[0, at, rows, :] + f1 * basis[1, at, rows, :] + f2 * basis[2, at, rows, :]
            )
            return carry

        lax.fori_loop(0, PLANES_PER_FIELD, combine, 0, unroll=7)

    for f in range(FIELDS):
        for step in range(1, GROUPS):
            out_copy(f, step).wait_send()
            back_copy(f, step).wait_send()
        for_edges(lambda side, owner, f=f: edge_copy(side, f, owner).wait_send())
    for level in range(3):
        for copy in halo_copies(level):
            copy.wait_send()
    for copy in x_copies + z_copies:
        copy.wait_send()


def shards(mesh_x, mesh_z, velocity, element_slot):
    count = FIELDS * PLANES_PER_FIELD
    field = jnp.transpose(velocity, (0, 2, 3, 1, 4)).reshape(count, LOCAL, LANES)
    vmem = pl.BlockSpec(memory_space=pltpu.VMEM)
    lines = FIELDS * NODES
    f32 = jnp.float32
    dma = pltpu.SemaphoreType.DMA
    result = pl.pallas_call(
        functools.partial(kernel, mesh_x, mesh_z),
        out_shape=jax.ShapeDtypeStruct((count, LOCAL, LANES), f32),
        in_specs=[pl.BlockSpec(memory_space=pl.ANY)] * 3,
        out_specs=vmem,
        scratch_shapes=[
            pltpu.VMEM((count, LOCAL, LANES), f32),
            pltpu.VMEM((1, LANES), jnp.int32),
            pltpu.VMEM((768, 256), jnp.bfloat16),
            pltpu.VMEM((GROUPS, TILES, LOCAL, LANES), f32),
            pltpu.VMEM((TILES, NCOEF, LANES), f32),
            pltpu.VMEM((lines, NCOEF, LANES), f32),
            pltpu.VMEM((lines, NCOEF, LANES), f32),
            pltpu.VMEM((lines, NCOEF, LANES), f32),
            pltpu.VMEM((TILES, NCOEF, LANES), f32),
            pltpu.VMEM((GROUPS, TILES, LOCAL, LANES), f32),
            pltpu.VMEM((3, count, LOCAL, LANES), f32),
            pltpu.VMEM((2, FIELDS, NODES, LOCAL, LANES), f32),
            pltpu.VMEM((FIELDS, NCOEF, LANES), f32),
            pltpu.VMEM((2, FIELDS, LOCAL, LANES), f32),
            pltpu.VMEM((MOMENTS, FIELDS, LOCAL, LANES), f32),
            pltpu.VMEM((3, 2, FIELDS, LOCAL, LANES), f32),
            pltpu.VMEM((3, 2, FIELDS, LOCAL, LANES), f32),
            pltpu.VMEM((mesh_x, 8, LANES), f32),
            pltpu.VMEM((mesh_z, 8, LANES), f32),
            dma((FIELDS, GROUPS - 1)),
            dma((FIELDS, GROUPS - 1)),
            dma((FIELDS,)),
            dma((FIELDS, GROUPS - 1)),
            dma((FIELDS, GROUPS - 1)),
            dma((FIELDS,)),
            dma((3, 2)),
            dma((3, 2)),
            dma((mesh_x - 1,)),
            dma((mesh_x - 1,)),
            dma((mesh_z - 1,)),
            dma((mesh_z - 1,)),
            dma((FIELDS + 2,)),
            dma((2, FIELDS, GROUPS)),
            dma((2, FIELDS)),
        ],
        compiler_params=pltpu.CompilerParams(
            collective_id=0, has_side_effects=True, vmem_limit_bytes=40 * 1024 * 1024
        ),
    )(field, element_slot.reshape(1, LANES), jnp.asarray(transform_tables()))
    return jnp.transpose(
        result.reshape(FIELDS, NODES, NODES, LOCAL, LANES), (0, 3, 1, 2, 4)
    )


def solution(mesh):
    strips = mesh.shape["mesh"]
    mesh_x = 4 if strips % 4 == 0 else 1
    placed = (P(None, "modes", None, None, "mesh"), P("mesh"))
    return jax.shard_map(
        functools.partial(shards, mesh_x, strips // mesh_x),
        mesh=mesh,
        in_specs=placed,
        out_specs=P(None, "modes", None, None, "mesh"),
        check_vma=False,
    )
```

```python
import functools

import jax
import jax.numpy as jnp
import numpy as np
from jax import lax
from jax.experimental import pallas as pl
from jax.experimental.pallas import tpu as pltpu
from jax.sharding import PartitionSpec as P

NODES = 7
FIELDS = 3
GROUPS = 8
LOCAL = 16
NCOEF = 128
LANES = 128
EY = 16
PLANES_PER_FIELD = NODES * NODES
SIGMA_BASE = 8.0
SPAN_WAVE = 0.25
STEP_TIME = 0.01
MOMENTS = 6
HALVES = 2
TILES = 10
SLOT = 8
OUT_PARTS = (((0, 4), (4, 3), (7, 3)), ((1, 3), (4, 3), (7, 3)))
BACK_PARTS = (((0, 3), (3, 3), (6, 3)), ((0, 3), (3, 3), (6, 4)))


def gll_tables():
    inner_point = np.sqrt((5.0 - 2.0 * np.sqrt(5.0 / 3.0)) / 11.0)
    outer_point = np.sqrt((5.0 + 2.0 * np.sqrt(5.0 / 3.0)) / 11.0)
    points = np.array([-1.0, -outer_point, -inner_point, 0.0, inner_point, outer_point, 1.0])
    legendre_prev = points * 0.0 + 1.0
    legendre_now = points.copy()
    for degree in range(1, points.shape[0] - 1):
        legendre_next = ((2 * degree + 1) * points * legendre_now - degree * legendre_prev) / (
            degree + 1
        )
        legendre_prev = legendre_now
        legendre_now = legendre_next
    order_value = points.shape[0] - 1
    quadrature = 2.0 / (order_value * (order_value + 1) * legendre_now**2)
    counter = np.arange(points.shape[0])
    same_node = counter[:, None] == counter[None, :]
    distances = np.where(same_node, 1.0, points[:, None] - points[None, :])
    barycentric = 1.0 / np.prod(distances, axis=1)
    off_diagonal = np.where(same_node, 0.0, barycentric[None, :] / barycentric[:, None] / distances)
    derivative = np.where(same_node, -np.sum(off_diagonal, axis=1)[:, None], off_diagonal)
    stiffness = derivative.T @ (quadrature[:, None] * derivative)
    return quadrature, derivative, stiffness


def fourier_tables():
    half_count = NCOEF // 2
    planes = np.arange(NCOEF) * 2.0 * np.pi / NCOEF
    numbers = np.arange(NCOEF)
    wavenumber = np.where(numbers <= half_count, numbers, numbers - half_count)
    cosine_mask = (numbers <= half_count)[None, :]
    phase = planes[:, None] * wavenumber[None, :]
    inverse = np.where(cosine_mask, np.cos(phase), np.sin(phase))
    slope = SPAN_WAVE * wavenumber[None, :] * np.where(cosine_mask, -np.sin(phase), np.cos(phase))
    normaliser = np.where((numbers == 0) | (numbers == half_count), 1.0 / NCOEF, 2.0 / NCOEF)
    forward = normaliser[:, None] * inverse.T
    return inverse, slope, forward


QUAD, DERIV, STIFF = gll_tables()
SCALED_STIFF = STIFF / QUAD[:, None]
MASS = 0.25 * QUAD[:, None] * QUAD[None, :]


def split_table(table):
    high = np.asarray(table, np.float32).astype(jnp.bfloat16)
    low = (np.asarray(table, np.float64) - high.astype(np.float64)).astype(jnp.bfloat16)
    return high, low


def transform_tables():
    inverse, slope, forward = fourier_tables()
    t_high, t_low = split_table(np.concatenate([inverse, slope], axis=0))
    f_high, f_low = split_table(-STEP_TIME * forward)
    padded = np.zeros((8, 8))
    padded[:NODES, :NODES] = 2.0 * DERIV
    b_high, b_low = split_table(np.kron(np.eye(2), np.kron(padded.T, np.eye(SLOT))))
    return np.concatenate(
        [
            np.concatenate([t_high, t_high], axis=1),
            np.concatenate([t_low, np.concatenate([b_high, b_high], axis=0)], axis=1),
            np.concatenate([f_high, f_high], axis=1),
            np.concatenate([f_low, b_low], axis=1),
        ],
        axis=0,
    )


def split_value(value):
    high = value.astype(jnp.bfloat16)
    low = (value - high.astype(jnp.float32)).astype(jnp.bfloat16)
    return high, low


def dot(left, right):
    return jnp.dot(left, right, preferred_element_type=jnp.float32)


def swap_groups(tiles, lane):
    tiles = list(tiles)
    for bit in (8, 4, 2, 1):
        low = (lane & (SLOT * bit)) == 0
        new = list(tiles)
        for at in range(16):
            if at & bit:
                continue
            first, second = tiles[at], tiles[at + bit]
            if bit == 8:
                moved = pltpu.roll(jnp.where(low, second, first), 64, 1)
                new[at] = jnp.where(low, first, moved)
                new[at + bit] = jnp.where(low, moved, second)
            else:
                new[at] = jnp.where(low, first, pltpu.roll(second, SLOT * bit, 1))
                new[at + bit] = jnp.where(low, pltpu.roll(first, LANES - SLOT * bit, 1), second)
        tiles = new
    return tiles


def weighted_sum(coefficients, values):
    total = None
    for coefficient, value in zip(coefficients, values):
        if value is None:
            continue
        term = float(coefficient) * value
        total = term if total is None else total + term
    return total


def line_product(matrix, line, sign):
    pairs = [(line[k], line[6 - k]) for k in range(3)]
    even = [None if a is None else a + b for a, b in pairs] + [line[3]]
    odd = [None if a is None else a - b for a, b in pairs]
    out = [None] * 7
    for i in range(3):
        even_row = [0.5 * (matrix[i, k] + matrix[i, 6 - k]) for k in range(3)] + [matrix[i, 3]]
        odd_row = [0.5 * (matrix[i, k] - matrix[i, 6 - k]) for k in range(3)]
        even_part = weighted_sum(even_row, even)
        odd_part = weighted_sum(odd_row, odd)
        out[i] = even_part + odd_part
        out[6 - i] = even_part - odd_part if sign > 0 else odd_part - even_part
    if sign > 0:
        out[3] = weighted_sum([matrix[3, k] for k in range(4)], even)
    else:
        out[3] = weighted_sum([matrix[3, k] for k in range(3)], odd)
    return out


class Levels:
    def __init__(self, *buffers):
        self.buffers = buffers

    def __getitem__(self, at):
        return self.buffers[at[0]][at[1:]]

    def __setitem__(self, at, value):
        self.buffers[at[0]][at[1:]] = value


def kernel(
    mesh_x,
    mesh_z,
    vel_hbm,
    slot_hbm,
    table_hbm,
    basis0,
    basis1,
    basis2,
    factor0,
    factor1,
    factor2,
    vel,
    slot,
    table,
    msg,
    recv1,
    phys,
    span,
    cross,
    send2,
    recv2,
    last_faces,
    edge_tile,
    edge_recv,
    moments,
    halo_send,
    halo_recv,
    red_x,
    red_z,
    send1_sem,
    recv1_sem,
    own1_sem,
    send2_sem,
    recv2_sem,
    own2_sem,
    halo_send_sem,
    halo_recv_sem,
    redx_send_sem,
    redx_recv_sem,
    redz_send_sem,
    redz_recv_sem,
    load_sem,
    edge_send_sem,
    edge_recv_sem,
):
    def vel_load(f):
        part = pl.ds(f * PLANES_PER_FIELD, PLANES_PER_FIELD)
        return pltpu.make_async_copy(vel_hbm.at[part], vel.at[part], load_sem.at[f])

    slot_load = pltpu.make_async_copy(slot_hbm, slot, load_sem.at[FIELDS])
    table_load = pltpu.make_async_copy(table_hbm, table, load_sem.at[FIELDS + 1])
    slot_load.start()
    for f in range(FIELDS):
        vel_load(f).start()
    table_load.start()

    basis = Levels(basis0, basis1, basis2)
    factor = Levels(factor0, factor1, factor2)
    me = lax.axis_index("modes")
    strip = lax.axis_index("mesh")
    strips = mesh_x * mesh_z
    at_x = lax.rem(strip, mesh_x)
    at_z = strip // mesh_x
    following = lax.rem(strip + 1, strips)
    previous = lax.rem(strip + strips - 1, strips)

    def mode_peer(step):
        return lax.rem(me + step, GROUPS)

    def x_peer(step):
        return at_z * mesh_x + lax.rem(at_x + step, mesh_x)

    def z_peer(step):
        return lax.rem(at_z + step, mesh_z) * mesh_x + at_x

    barrier = pltpu.get_barrier_semaphore()
    greeted = [{"modes": mode_peer(step)} for step in range(1, GROUPS)]
    greeted += [{"mesh": following}, {"mesh": previous}]
    greeted += [{"mesh": x_peer(step)} for step in range(1, mesh_x)]
    greeted += [{"mesh": z_peer(step)} for step in range(1, mesh_z)]
    greeted += [{"modes": 0, "mesh": following}, {"modes": GROUPS - 1, "mesh": previous}]
    greetings = len(greeted) - 2
    greetings += jnp.where(jnp.logical_or(me == 0, me == GROUPS - 1), GROUPS, 0)
    for device in greeted:
        pl.semaphore_signal(
            barrier, inc=1, device_id=device, device_id_type=pl.DeviceIdType.MESH
        )

    lane = lax.broadcasted_iota(jnp.int32, (8, LANES), 1)
    group = lane // EY
    row = lane % EY
    slot_load.wait()
    slots = jnp.broadcast_to(slot[...], (8, LANES))

    def remote(src, dst, send, recv, device):
        return pltpu.make_async_remote_copy(
            src_ref=src,
            dst_ref=dst,
            send_sem=send,
            recv_sem=recv,
            device_id=device,
            device_id_type=pl.DeviceIdType.MESH,
        )

    def out_copy(h, f, step):
        peer = mode_peer(step)
        part = pl.ds(*OUT_PARTS[h][f])
        return remote(
            msg.at[h, peer, part],
            recv1.at[h, part, pl.ds(me * LOCAL, LOCAL)],
            send1_sem.at[h, f, step - 1],
            recv1_sem.at[h, f, step - 1],
            {"modes": peer},
        )

    def own_out(h, f):
        part = pl.ds(*OUT_PARTS[h][f])
        return pltpu.make_async_copy(
            msg.at[h, me, part], recv1.at[h, part, pl.ds(me * LOCAL, LOCAL)], own1_sem.at[h, f]
        )

    def start_out(h, f):
        for step in range(1, GROUPS):
            out_copy(h, f, step).start()
        own_out(h, f).start()

    def back_copy(h, f, step):
        peer = mode_peer(step)
        part = pl.ds(*BACK_PARTS[h][f])
        return remote(
            send2.at[h, part, pl.ds(peer * LOCAL, LOCAL)],
            recv2.at[h, me, part],
            send2_sem.at[h, f, step - 1],
            recv2_sem.at[h, f, step - 1],
            {"modes": peer},
        )

    def own_back(h, f):
        part = pl.ds(*BACK_PARTS[h][f])
        return pltpu.make_async_copy(
            send2.at[h, part, pl.ds(me * LOCAL, LOCAL)], recv2.at[h, me, part], own2_sem.at[h, f]
        )

    def edge_copy(side, f, owner):
        return remote(
            edge_tile.at[side, f, pl.ds(pl.multiple_of(owner * LOCAL, LOCAL), LOCAL)],
            edge_recv.at[side, f],
            edge_send_sem.at[side, f, owner],
            edge_recv_sem.at[side, f],
            {"modes": owner, "mesh": following if side == 0 else previous},
        )

    def for_edges(action):
        for side, worker in ((0, GROUPS - 1), (1, 0)):

            @pl.when(me == worker)
            def _(side=side):
                def each(owner, carry):
                    action(side, owner)
                    return carry

                lax.fori_loop(0, GROUPS, each, 0)

    def halo_copies(level):
        return (
            remote(
                halo_send.at[level, 0],
                halo_recv.at[level, 0],
                halo_send_sem.at[level, 0],
                halo_recv_sem.at[level, 0],
                {"mesh": following},
            ),
            remote(
                halo_send.at[level, 1],
                halo_recv.at[level, 1],
                halo_send_sem.at[level, 1],
                halo_recv_sem.at[level, 1],
                {"mesh": previous},
            ),
        )

    def pack_faces(level, f, rows, lefts, rights):
        to_next = pltpu.roll(rights[0], EY, 1)
        to_prior = lefts[0]
        for j in range(1, NODES):
            here = group == j
            right = pltpu.roll(rights[j], EY * (j + 1), 1)
            to_next = jnp.where(here, right, to_next)
            to_prior = jnp.where(here, pltpu.roll(lefts[j], EY * j, 1), to_prior)
        halo_send[level, 0, f, rows, :] = to_next
        halo_send[level, 1, f, rows, :] = to_prior

    def order_line(f, i):
        for half in range(2):
            rows = pl.ds(8 * half, 8)
            for j in range(NODES):
                at = f * PLANES_PER_FIELD + i * NODES + j
                vel[at, rows, :] = jnp.take_along_axis(vel[at, rows, :], slots, axis=1)

    def store_message(tiles, at, rows):
        tiles = swap_groups(tiles, lane)
        for k in range(GROUPS):
            for h in range(HALVES):
                msg[h, k, at, rows, :] = tiles[2 * k + h]

    def spread_lines(f, p):
        base = f * PLANES_PER_FIELD
        for half in range(2):
            rows = pl.ds(8 * half, 8)
            tiles = []
            for i in (2 * p, 2 * p + 1):
                tiles += [vel[base + i * NODES + j, rows, :] for j in range(NODES)]
                tiles.append(vel[base + 42 + i, rows, :])
            store_message(tiles, 1 + f * 3 + p, rows)

    for f in range(FIELDS):
        vel_load(f).wait()
        order_line(f, 6)
    for half in range(2):
        rows = pl.ds(8 * half, 8)
        zero = jnp.zeros((8, LANES), jnp.float32)
        tiles = [vel[f * PLANES_PER_FIELD + 48, rows, :] for f in range(FIELDS)]
        tiles = swap_groups(tiles + [zero] * 13, lane)
        for k in range(GROUPS):
            msg[0, k, 0, rows, :] = tiles[2 * k] + pltpu.roll(tiles[2 * k + 1], 3 * SLOT, 1)
    for f in range(FIELDS):

        def two_lines(p, carry, f=f):
            order_line(f, 2 * p)
            order_line(f, 2 * p + 1)
            spread_lines(f, p)
            return carry

        lax.fori_loop(0, 3, two_lines, 0)
        if f == 0:
            pl.semaphore_wait(barrier, greetings)
        start_out(0, f)

    for f in range(FIELDS):
        base = f * PLANES_PER_FIELD
        for half in range(2):
            rows = pl.ds(8 * half, 8)
            lefts = [vel[base + j, rows, :] for j in range(NODES)]
            rights = [vel[base + 42 + j, rows, :] for j in range(NODES)]
            pack_faces(0, f, rows, lefts, rights)
    for copy in halo_copies(0):
        copy.start()

    table_load.wait()
    tt, tl, bb = table.at[0:256, :], table.at[256:512, 0:128], table.at[256:512, 128:256]
    ff, fl, bl = table.at[512:640, :], table.at[640:768, 0:128], table.at[640:768, 128:256]
    slot_all = lax.broadcasted_iota(jnp.int32, (NCOEF, LANES), 1) // SLOT
    low_half = lane < 64

    def shifted(value, slots_up):
        return pltpu.roll(value, (SLOT * slots_up) % LANES, 1) if slots_up % 16 else value

    def to_planes(h, f):
        tiles = [recv1[h, 1 + 3 * f + p] for p in range(3)]
        last = jnp.where(slot_all == 6, shifted(recv1[0, 0], 6 - f - 3 * h), 0.0)
        for j in range(6):
            last = jnp.where(
                slot_all == j, shifted(tiles[j // 2], j - 7 - 8 * (j % 2)), last
            )
        tiles.append(last)
        planes = []
        for p in (0, 2):
            high, low = split_value(jnp.concatenate(tiles[p : p + 2], axis=1))
            value = dot(tt[...], jnp.concatenate([high, low], axis=0)) + dot(tl[...], high)
            for q in range(2):
                at = 4 * f + p + q
                planes.append(value[:NCOEF, q * LANES : (q + 1) * LANES])
                phys[at] = planes[-1]
                span[at] = value[NCOEF:, q * LANES : (q + 1) * LANES]
        high, low = split_value(jnp.concatenate(planes, axis=0))
        value = dot(jnp.concatenate([high, low], axis=1), bb[...]) + dot(high, bl[...])
        for p in range(4):
            cross[4 * f + p] = value[p * NCOEF : (p + 1) * NCOEF]

    def derivative_at(i, a):
        return float(2.0 * DERIV[i, a]) if i < NODES and a < NODES else 0.0

    def advect(h, f):
        def rows_of(block, inner):
            rows = pl.ds(pl.multiple_of(block * 8, 8), 8)
            tiles = [phys[4 * f + p, rows, :] for p in range(4)]
            swapped = [pltpu.roll(tile, 64, 1) for tile in tiles]
            both = tiles[3] + swapped[3]
            for p in range(4):
                i = 2 * p
                stream = both * jnp.where(low_half, derivative_at(i, 6), derivative_at(i + 1, 6))
                for q in range(3):
                    a = 2 * q
                    stream = (
                        stream
                        + tiles[q]
                        * jnp.where(low_half, derivative_at(i, a), derivative_at(i + 1, a + 1))
                        + swapped[q]
                        * jnp.where(low_half, derivative_at(i, a + 1), derivative_at(i + 1, a))
                    )
                at = 4 * f + p
                cross[at, rows, :] = (
                    phys[p, rows, :] * stream
                    + phys[4 + p, rows, :] * cross[at, rows, :]
                    + phys[8 + p, rows, :] * span[at, rows, :]
                )
            return inner

        lax.fori_loop(0, NCOEF // 8, rows_of, 0, unroll=2)
        last = None
        for p in (2, 0):
            pair = jnp.concatenate([cross[4 * f + p], cross[4 * f + p + 1]], axis=1)
            high, low = split_value(pair)
            value = dot(ff[...], jnp.concatenate([high, low], axis=0)) + dot(fl[...], high)
            parts = [value[:, :LANES], value[:, LANES:]]
            if p == 2:
                last = parts.pop()
            for q, part in reversed(list(enumerate(parts))):
                i = 2 * (p + q)
                part = jnp.where(slot_all == 7, shifted(last, 7 - i), part)
                send2[h, 3 * f + p + q] = jnp.where(slot_all == 15, shifted(last, 14 - i), part)
        at = 3 * h + f
        rest = send2[1, TILES - 1] if at else jnp.zeros((NCOEF, LANES), jnp.float32)
        send2[1, TILES - 1] = jnp.where(slot_all == at, shifted(last, at - 6), rest)
        for side, tile in ((0, last), (1, part)):
            if h:
                tile = jnp.where(slot_all < 8, edge_tile[side, f], shifted(tile, 8))
            edge_tile[side, f] = tile
        if h:
            for_edges(lambda side, owner: edge_copy(side, f, owner).start())
        for step in range(1, GROUPS):
            back_copy(h, f, step).start()
        own_back(h, f).start()

    for h in range(HALVES):
        for f in range(FIELDS):
            for step in range(1, GROUPS):
                out_copy(h, f, step).wait_recv()
            own_out(h, f).wait()
            if h == 0:
                start_out(1, f)
            to_planes(h, f)
        for f in range(FIELDS):
            advect(h, f)

    is_first = strip == 0
    is_last = strip == strips - 1
    not_inflow = jnp.logical_not(jnp.logical_and(group == 0, is_first))
    west = group == 0
    east = group == GROUPS - 1
    south = row != 0
    north = row != EY - 1
    has_previous = jnp.where(is_first, 0.0, 1.0)
    has_following = jnp.where(is_last, 0.0, 1.0)
    east_weight = jnp.where(jnp.logical_and(east, is_last), 1.0, 0.5)

    def at_block(block):
        f = block // 2
        rows = pl.ds(pl.multiple_of((block % 2) * 8, 8), 8)
        return f, rows

    def over_blocks(body, first=0, last=2 * FIELDS, unroll=2):
        lax.fori_loop(first, last, lambda block, c: (body(block), c)[1], 0, unroll=unroll)

    def gather_source(f):
        for h in range(HALVES):
            for step in range(1, GROUPS):
                back_copy(h, f, step).wait_recv()
            own_back(h, f).wait()
        base = f * PLANES_PER_FIELD
        for half in range(2):
            rows = pl.ds(8 * half, 8)
            for p in range(3):
                tiles = swap_groups(
                    [recv2[g % 2, g // 2, 3 * f + p, rows, :] for g in range(16)], lane
                )
                for s in range(16):
                    i, j = 2 * p + s // 8, s % 8
                    a, b = (i, j) if j < 7 else (6, i)
                    at = base + a * NODES + b
                    basis[0, at, rows, :] = float(MASS[a, b]) * (
                        SIGMA_BASE * vel[at, rows, :] + tiles[s]
                    )

    def gather_rest():
        for half in range(2):
            rows = pl.ds(8 * half, 8)
            tiles = []
            for k in range(GROUPS):
                tile = recv2[1, k, TILES - 1, rows, :]
                tiles += [tile, shifted(tile, -3)]
            tiles = swap_groups(tiles, lane)
            for f in range(FIELDS):
                at = f * PLANES_PER_FIELD + 48
                basis[0, at, rows, :] = float(MASS[6, 6]) * (
                    SIGMA_BASE * vel[at, rows, :] + tiles[f]
                )

    def along_rows(line):
        bottom, top = line[0], line[6]
        first = jnp.where(south, bottom + pltpu.roll(top, 1, 1), 0.0)
        last = jnp.where(north, top + pltpu.roll(bottom, LANES - 1, 1), 0.0)
        return [first] + list(line[1:6]) + [last]

    def squares(line):
        total = line[1] * line[1]
        for j in range(2, 6):
            total = total + line[j] * line[j]
        return total + 0.5 * (line[0] * line[0] + line[6] * line[6])

    def shift_of(block):
        number = (
            me * LOCAL + (block % 2) * 8 + lax.broadcasted_iota(jnp.int32, (8, LANES), 0)
        )
        wave = jnp.where(number <= NCOEF // 2, number, number - NCOEF // 2).astype(jnp.float32)
        wave = SPAN_WAVE * wave
        return 0.25 * (SIGMA_BASE + wave * wave)

    def finish_inside(level, first=0, last=2 * FIELDS):
        def block_of(block):
            f, rows = at_block(block)
            base = f * PLANES_PER_FIELD
            shift = shift_of(block)
            total = jnp.zeros((8, LANES), jnp.float32)
            inside = []
            for i in range(1, 6):
                line = []
                for j in range(NODES):
                    value = basis[level, base + i * NODES + j, rows, :]
                    if level:
                        value = float(QUAD[i] * QUAD[j]) * (
                            value
                            + float(SCALED_STIFF[i, 0]) * basis[level - 1, base + j, rows, :]
                            + float(SCALED_STIFF[i, 6]) * basis[level - 1, base + 42 + j, rows, :]
                        )
                    line.append(value)
                line = along_rows(line)
                for j in range(NODES):
                    if level or j in (0, 6):
                        basis[level, base + i * NODES + j, rows, :] = line[j]
                total = total + squares(line)
                inside.append(line)
            image = [None] * PLANES_PER_FIELD
            for j in range(NODES):
                column = [None] + [line[j] for line in inside] + [None]
                column = line_product(SCALED_STIFF, column, 1)
                for i in range(NODES):
                    image[i * NODES + j] = column[i]
            energy = jnp.zeros((8, LANES), jnp.float32)
            for i in range(1, 6):
                line = line_product(SCALED_STIFF, inside[i - 1], 1)
                for j in range(NODES):
                    n = i * NODES + j
                    image[n] = image[n] + line[j] + shift * inside[i - 1][j]
                    energy = energy + float(QUAD[i] * QUAD[j]) * (image[n] * inside[i - 1][j])
            for n in range(PLANES_PER_FIELD):
                if level < 2:
                    basis[level + 1, base + n, rows, :] = image[n]
                elif n < 7:
                    last_faces[0, f, n, rows, :] = image[n]
                elif n >= 42:
                    last_faces[1, f, n - 42, rows, :] = image[n]
            moments[2 * level, f, rows, :] = total
            moments[2 * level + 1, f, rows, :] = energy

        over_blocks(block_of, first, last)

    def finish_faces(level):
        def block_of(block):
            f, rows = at_block(block)
            base = f * PLANES_PER_FIELD
            shift = shift_of(block)
            prior = halo_recv[level, 0, f, rows, :]
            after = halo_recv[level, 1, f, rows, :]
            if level == 0:
                prior = SIGMA_BASE * prior
                after = SIGMA_BASE * after
                prior_edge = edge_recv[0, f, rows, :] * has_previous
                after_edge = edge_recv[1, f, rows, :] * has_following
            prior = prior * has_previous
            after = after * has_following
            lefts, rights = [], []
            for j in range(NODES):
                left = basis[level, base + j, rows, :]
                right = basis[level, base + 42 + j, rows, :]
                from_prior = pltpu.roll(prior, LANES - EY * j, 1) if j else prior
                from_after = pltpu.roll(after, LANES - EY * (j + 1), 1)
                if level == 0:
                    from_prior = float(MASS[6, j]) * (
                        from_prior
                        + jnp.where(
                            lane < 8, shifted(prior_edge, -j), shifted(prior_edge, -7 - j)
                        )
                    )
                    from_after = float(MASS[0, j]) * (
                        from_after
                        + jnp.where(
                            lane < 120, shifted(after_edge, 14 - j), shifted(after_edge, 7 - j)
                        )
                    )
                lefts.append(left + jnp.where(west, from_prior, pltpu.roll(right, EY, 1)))
                rights.append(
                    right + jnp.where(east, from_after, pltpu.roll(left, LANES - EY, 1))
                )
            lefts = [jnp.where(not_inflow, value, 0.0) for value in along_rows(lefts)]
            rights = along_rows(rights)
            moments[2 * level, f, rows, :] = (
                moments[2 * level, f, rows, :]
                + 0.5 * squares(lefts)
                + east_weight * squares(rights)
            )
            energy = moments[2 * level + 1, f, rows, :]
            images = []
            for i, line in ((0, lefts), (6, rights)):
                across = line_product(SCALED_STIFF, line, 1)
                image = []
                for j in range(NODES):
                    basis[level, base + i * NODES + j, rows, :] = line[j]
                    if level < 2:
                        part = basis[level + 1, base + i * NODES + j, rows, :]
                    else:
                        part = last_faces[i // 6, f, j, rows, :]
                    whole = (
                        part
                        + float(SCALED_STIFF[i, 0]) * lefts[j]
                        + float(SCALED_STIFF[i, 6]) * rights[j]
                        + across[j]
                        + shift * line[j]
                    )
                    weight = float(QUAD[i] * QUAD[j])
                    energy = energy + weight * ((whole + part) * line[j])
                    if level < 2:
                        whole = weight * whole
                        basis[level + 1, base + i * NODES + j, rows, :] = whole
                        image.append(whole)
                images.append(image)
            moments[2 * level + 1, f, rows, :] = energy
            if level < 2:
                pack_faces(level + 1, f, rows, images[0], images[1])

        over_blocks(block_of, unroll=6)

    def pack_moments(packed, which):
        for m in which:
            for block in range(2 * FIELDS):
                f, half = block // 2, block % 2
                total = jnp.sum(moments[m, f, 8 * half : 8 * half + 8, :], axis=1, keepdims=True)
                packed = jnp.where(lane == 8 * block + m, total, packed)
        return packed

    packed = jnp.zeros((8, LANES), jnp.float32)
    for level in range(3):
        if level == 0:
            for f in range(FIELDS):
                gather_source(f)
                finish_inside(0, 2 * f, 2 * f + 2)
                for side in range(2):
                    edge_copy(side, f, 0).wait_recv()
            gather_rest()
        else:
            finish_inside(level)
            packed = pack_moments(packed, (2 * level - 2, 2 * level - 1))
        for copy in halo_copies(level):
            copy.wait_recv()
        finish_faces(level)
        if level < 2:
            for copy in halo_copies(level + 1):
                copy.start()
    packed = pack_moments(packed, (4, 5))

    def sum_over(value, slots_ref, mine, count, copies):
        slots_ref[mine] = value
        for copy in copies:
            copy.start()
        for copy in copies:
            copy.wait_recv()
        total = slots_ref[0]
        for k in range(1, count):
            total = total + slots_ref[k]
        return total

    x_copies = [
        remote(
            red_x.at[at_x],
            red_x.at[at_x],
            redx_send_sem.at[step - 1],
            redx_recv_sem.at[step - 1],
            {"mesh": x_peer(step)},
        )
        for step in range(1, mesh_x)
    ]
    z_copies = [
        remote(
            red_z.at[at_z],
            red_z.at[at_z],
            redz_send_sem.at[step - 1],
            redz_recv_sem.at[step - 1],
            {"mesh": z_peer(step)},
        )
        for step in range(1, mesh_z)
    ]
    packed = sum_over(packed, red_x, at_x, mesh_x, x_copies)
    packed = sum_over(packed, red_z, at_z, mesh_z, z_copies)

    m0, m1, m2, m3, m4, m5 = [
        packed if m == 0 else pltpu.roll(packed, LANES - m, 1) for m in range(MOMENTS)
    ]
    s0, s1, s2 = lax.rsqrt(m1), lax.rsqrt(m3), lax.rsqrt(m5)
    l10 = m2 * s0 * s1
    l20 = m3 * s0 * s2
    h21 = m4 * s1 * s2
    d1 = 1.0 - l10 * l10
    l21 = (h21 - l20 * l10) / d1
    d2 = 1.0 - l20 * l20 - l21 * l21 * d1
    y0 = m0 * s0
    y1 = m1 * s1 - l10 * y0
    y2 = m2 * s2 - l20 * y0 - l21 * y1
    c2 = y2 / d2
    c1 = y1 / d1 - l21 * c2
    c0 = y0 - l10 * c1 - l20 * c2
    c0, c1, c2 = c0 * s0, c1 * s1, c2 * s2

    for block in range(2 * FIELDS):
        f, half = block // 2, block % 2
        for k, c in enumerate((c0, c1, c2)):
            factor[k, f, 8 * half : 8 * half + 8, :] = jnp.broadcast_to(
                c[:, 8 * block : 8 * block + 1], (8, LANES)
            )

    for h in range(HALVES):
        for f in range(FIELDS):
            for step in range(1, GROUPS):
                out_copy(h, f, step).wait_send()
                back_copy(h, f, step).wait_send()
    for f in range(FIELDS):
        for_edges(lambda side, owner, f=f: edge_copy(side, f, owner).wait_send())
    for level in range(3):
        for copy in halo_copies(level):
            copy.wait_send()
    for copy in x_copies + z_copies:
        copy.wait_send()


def shards(mesh_x, mesh_z, velocity, element_slot):
    count = FIELDS * PLANES_PER_FIELD
    field = jnp.transpose(velocity, (0, 2, 3, 1, 4)).reshape(count, LOCAL, LANES)
    vmem = pl.BlockSpec(memory_space=pltpu.VMEM)
    f32 = jnp.float32
    dma = pltpu.SemaphoreType.DMA
    *basis, factor0, factor1, factor2 = pl.pallas_call(
        functools.partial(kernel, mesh_x, mesh_z),
        out_shape=[
            jax.ShapeDtypeStruct((count, LOCAL, LANES), f32),
        ]
        * 3
        + [
            jax.ShapeDtypeStruct((FIELDS, LOCAL, LANES), f32),
        ]
        * 3,
        in_specs=[pl.BlockSpec(memory_space=pltpu.HBM)] * 3,
        out_specs=[vmem] * 6,
        scratch_shapes=[
            pltpu.VMEM((count, LOCAL, LANES), f32),
            pltpu.VMEM((1, LANES), jnp.int32),
            pltpu.VMEM((768, 256), jnp.bfloat16),
            pltpu.VMEM((HALVES, GROUPS, TILES, LOCAL, LANES), f32),
            pltpu.VMEM((HALVES, TILES, NCOEF, LANES), f32),
            pltpu.VMEM((4 * FIELDS, NCOEF, LANES), f32),
            pltpu.VMEM((4 * FIELDS, NCOEF, LANES), f32),
            pltpu.VMEM((4 * FIELDS, NCOEF, LANES), f32),
            pltpu.VMEM((HALVES, TILES, NCOEF, LANES), f32),
            pltpu.VMEM((HALVES, GROUPS, TILES, LOCAL, LANES), f32),
            pltpu.VMEM((2, FIELDS, NODES, LOCAL, LANES), f32),
            pltpu.VMEM((2, FIELDS, NCOEF, LANES), f32),
            pltpu.VMEM((2, FIELDS, LOCAL, LANES), f32),
            pltpu.VMEM((MOMENTS, FIELDS, LOCAL, LANES), f32),
            pltpu.VMEM((3, 2, FIELDS, LOCAL, LANES), f32),
            pltpu.VMEM((3, 2, FIELDS, LOCAL, LANES), f32),
            pltpu.VMEM((mesh_x, 8, LANES), f32),
            pltpu.VMEM((mesh_z, 8, LANES), f32),
            dma((HALVES, FIELDS, GROUPS - 1)),
            dma((HALVES, FIELDS, GROUPS - 1)),
            dma((HALVES, FIELDS)),
            dma((HALVES, FIELDS, GROUPS - 1)),
            dma((HALVES, FIELDS, GROUPS - 1)),
            dma((HALVES, FIELDS)),
            dma((3, 2)),
            dma((3, 2)),
            dma((mesh_x - 1,)),
            dma((mesh_x - 1,)),
            dma((mesh_z - 1,)),
            dma((mesh_z - 1,)),
            dma((FIELDS + 2,)),
            dma((2, FIELDS, GROUPS)),
            dma((2, FIELDS)),
        ],
        compiler_params=pltpu.CompilerParams(
            collective_id=0, has_side_effects=True, vmem_limit_bytes=50688 * 1024
        ),
    )(field, element_slot.reshape(1, LANES), jnp.asarray(transform_tables()))
    terms = [
        factor[:, None, None] * level.reshape(FIELDS, NODES, NODES, LOCAL, LANES)
        for level, factor in zip(basis, (factor0, factor1, factor2))
    ]
    result = terms[0] + terms[1] + terms[2]
    return jnp.transpose(result, (0, 3, 1, 2, 4))


def solution(mesh):
    strips = mesh.shape["mesh"]
    mesh_x = 4 if strips % 4 == 0 else 1
    placed = (P(None, "modes", None, None, "mesh"), P("mesh"))
    return jax.shard_map(
        functools.partial(shards, mesh_x, strips // mesh_x),
        mesh=mesh,
        in_specs=placed,
        out_specs=P(None, "modes", None, None, "mesh"),
        check_vma=False,
    )
```

```python
import functools

import jax
import jax.numpy as jnp
import numpy as np
from jax import lax
from jax.experimental import pallas as pl
from jax.experimental.pallas import tpu as pltpu
from jax.sharding import PartitionSpec as P

NODES = 7
FIELDS = 3
GROUPS = 8
LOCAL = 16
NCOEF = 128
LANES = 128
EY = 16
PLANES_PER_FIELD = NODES * NODES
SIGMA_BASE = 8.0
SPAN_WAVE = 0.25
STEP_TIME = 0.01
MOMENTS = 6
TABLE_ROWS = 768
TABLE_HELD = 4096
HALVES = 2
TILES = 10
SLOT = 8
OUT_PARTS = (((0, 4), (4, 3), (7, 3)), ((1, 3), (4, 3), (7, 3)))
BACK_PARTS = (((0, 3), (3, 3), (6, 3)), ((0, 3), (3, 3), (6, 4)))


def gll_tables():
    inner_point = np.sqrt((5.0 - 2.0 * np.sqrt(5.0 / 3.0)) / 11.0)
    outer_point = np.sqrt((5.0 + 2.0 * np.sqrt(5.0 / 3.0)) / 11.0)
    points = np.array([-1.0, -outer_point, -inner_point, 0.0, inner_point, outer_point, 1.0])
    legendre_prev = points * 0.0 + 1.0
    legendre_now = points.copy()
    for degree in range(1, points.shape[0] - 1):
        legendre_next = ((2 * degree + 1) * points * legendre_now - degree * legendre_prev) / (
            degree + 1
        )
        legendre_prev = legendre_now
        legendre_now = legendre_next
    order_value = points.shape[0] - 1
    quadrature = 2.0 / (order_value * (order_value + 1) * legendre_now**2)
    counter = np.arange(points.shape[0])
    same_node = counter[:, None] == counter[None, :]
    distances = np.where(same_node, 1.0, points[:, None] - points[None, :])
    barycentric = 1.0 / np.prod(distances, axis=1)
    off_diagonal = np.where(same_node, 0.0, barycentric[None, :] / barycentric[:, None] / distances)
    derivative = np.where(same_node, -np.sum(off_diagonal, axis=1)[:, None], off_diagonal)
    stiffness = derivative.T @ (quadrature[:, None] * derivative)
    return quadrature, derivative, stiffness


def fourier_tables():
    half_count = NCOEF // 2
    planes = np.arange(NCOEF) * 2.0 * np.pi / NCOEF
    numbers = np.arange(NCOEF)
    wavenumber = np.where(numbers <= half_count, numbers, numbers - half_count)
    cosine_mask = (numbers <= half_count)[None, :]
    phase = planes[:, None] * wavenumber[None, :]
    inverse = np.where(cosine_mask, np.cos(phase), np.sin(phase))
    slope = SPAN_WAVE * wavenumber[None, :] * np.where(cosine_mask, -np.sin(phase), np.cos(phase))
    normaliser = np.where((numbers == 0) | (numbers == half_count), 1.0 / NCOEF, 2.0 / NCOEF)
    forward = normaliser[:, None] * inverse.T
    return inverse, slope, forward


QUAD, DERIV, STIFF = gll_tables()
SCALED_STIFF = STIFF / QUAD[:, None]
MASS = 0.25 * QUAD[:, None] * QUAD[None, :]


def split_table(table):
    high = np.asarray(table, np.float32).astype(jnp.bfloat16)
    low = (np.asarray(table, np.float64) - high.astype(np.float64)).astype(jnp.bfloat16)
    return high, low


def transform_tables():
    inverse, slope, forward = fourier_tables()
    t_high, t_low = split_table(np.concatenate([inverse, slope], axis=0))
    f_high, f_low = split_table(-STEP_TIME * forward)
    padded = np.zeros((8, 8))
    padded[:NODES, :NODES] = 2.0 * DERIV
    b_high, b_low = split_table(np.kron(np.eye(2), np.kron(padded.T, np.eye(SLOT))))
    return np.concatenate(
        [
            np.concatenate([t_high, t_high], axis=1),
            np.concatenate([t_low, np.concatenate([b_high, b_high], axis=0)], axis=1),
            np.concatenate([f_high, f_high], axis=1),
            np.concatenate([f_low, b_low], axis=1),
            np.zeros((TABLE_HELD - TABLE_ROWS, 256), jnp.bfloat16),
        ],
        axis=0,
    )


def split_value(value):
    high = value.astype(jnp.bfloat16)
    low = (value - high.astype(jnp.float32)).astype(jnp.bfloat16)
    return high, low


def dot(left, right):
    return jnp.dot(left, right, preferred_element_type=jnp.float32)


def swap_groups(tiles, lane):
    tiles = list(tiles)
    for bit in (8, 4, 2, 1):
        low = (lane & (SLOT * bit)) == 0
        new = list(tiles)
        for at in range(16):
            if at & bit:
                continue
            first, second = tiles[at], tiles[at + bit]
            if bit == 8:
                moved = pltpu.roll(jnp.where(low, second, first), 64, 1)
                new[at] = jnp.where(low, first, moved)
                new[at + bit] = jnp.where(low, moved, second)
            else:
                new[at] = jnp.where(low, first, pltpu.roll(second, SLOT * bit, 1))
                new[at + bit] = jnp.where(low, pltpu.roll(first, LANES - SLOT * bit, 1), second)
        tiles = new
    return tiles


def weighted_sum(coefficients, values):
    total = None
    for coefficient, value in zip(coefficients, values):
        if value is None:
            continue
        term = float(coefficient) * value
        total = term if total is None else total + term
    return total


def line_product(matrix, line, sign):
    pairs = [(line[k], line[6 - k]) for k in range(3)]
    even = [None if a is None else a + b for a, b in pairs] + [line[3]]
    odd = [None if a is None else a - b for a, b in pairs]
    out = [None] * 7
    for i in range(3):
        even_row = [0.5 * (matrix[i, k] + matrix[i, 6 - k]) for k in range(3)] + [matrix[i, 3]]
        odd_row = [0.5 * (matrix[i, k] - matrix[i, 6 - k]) for k in range(3)]
        even_part = weighted_sum(even_row, even)
        odd_part = weighted_sum(odd_row, odd)
        out[i] = even_part + odd_part
        out[6 - i] = even_part - odd_part if sign > 0 else odd_part - even_part
    if sign > 0:
        out[3] = weighted_sum([matrix[3, k] for k in range(4)], even)
    else:
        out[3] = weighted_sum([matrix[3, k] for k in range(3)], odd)
    return out


class Levels:
    def __init__(self, *buffers):
        self.buffers = buffers

    def __getitem__(self, at):
        return self.buffers[at[0]][at[1:]]

    def __setitem__(self, at, value):
        self.buffers[at[0]][at[1:]] = value


def kernel(
    mesh_x,
    mesh_z,
    vel_hbm,
    slot_hbm,
    table_hbm,
    basis0,
    basis1,
    basis2,
    factor0,
    factor1,
    factor2,
    vel,
    slot,
    table,
    msg,
    recv1,
    phys,
    span,
    cross,
    send2,
    recv2,
    last_faces,
    beside,
    edge_tile,
    edge_recv,
    moments,
    halo_send,
    halo_recv,
    red_x,
    red_z,
    send1_sem,
    recv1_sem,
    own1_sem,
    send2_sem,
    recv2_sem,
    own2_sem,
    halo_send_sem,
    halo_recv_sem,
    redx_send_sem,
    redx_recv_sem,
    redz_send_sem,
    redz_recv_sem,
    load_sem,
    edge_send_sem,
    edge_recv_sem,
):
    def vel_load(f):
        part = pl.ds(f * PLANES_PER_FIELD, PLANES_PER_FIELD)
        return pltpu.make_async_copy(vel_hbm.at[part], vel.at[part], load_sem.at[f])

    slot_load = pltpu.make_async_copy(slot_hbm, slot, load_sem.at[FIELDS])
    table_load = pltpu.make_async_copy(
        table_hbm.at[0:TABLE_ROWS], table, load_sem.at[FIELDS + 1]
    )
    slot_load.start()
    for f in range(FIELDS):
        vel_load(f).start()
    table_load.start()

    basis = Levels(basis0, basis1, basis2)
    factor = Levels(factor0, factor1, factor2)
    me = lax.axis_index("modes")
    strip = lax.axis_index("mesh")
    strips = mesh_x * mesh_z
    at_x = lax.rem(strip, mesh_x)
    at_z = strip // mesh_x
    following = lax.rem(strip + 1, strips)
    previous = lax.rem(strip + strips - 1, strips)

    def mode_peer(step):
        return lax.rem(me + step, GROUPS)

    def x_peer(step):
        return at_z * mesh_x + lax.rem(at_x + step, mesh_x)

    def z_peer(step):
        return lax.rem(at_z + step, mesh_z) * mesh_x + at_x

    barrier = pltpu.get_barrier_semaphore()
    greeted = [{"modes": mode_peer(step)} for step in range(1, GROUPS)]
    greeted += [{"mesh": following}, {"mesh": previous}]
    greeted += [{"mesh": x_peer(step)} for step in range(1, mesh_x)]
    greeted += [{"mesh": z_peer(step)} for step in range(1, mesh_z)]
    greeted += [{"modes": 0, "mesh": following}, {"modes": GROUPS - 1, "mesh": previous}]
    greetings = len(greeted) - 2
    greetings += jnp.where(jnp.logical_or(me == 0, me == GROUPS - 1), GROUPS, 0)
    for device in greeted:
        pl.semaphore_signal(
            barrier, inc=1, device_id=device, device_id_type=pl.DeviceIdType.MESH
        )

    lane = lax.broadcasted_iota(jnp.int32, (8, LANES), 1)
    group = lane // EY
    row = lane % EY
    slot_load.wait()
    slots = jnp.broadcast_to(slot[...], (8, LANES))

    def remote(src, dst, send, recv, device):
        return pltpu.make_async_remote_copy(
            src_ref=src,
            dst_ref=dst,
            send_sem=send,
            recv_sem=recv,
            device_id=device,
            device_id_type=pl.DeviceIdType.MESH,
        )

    def out_copy(h, f, step):
        peer = mode_peer(step)
        part = pl.ds(*OUT_PARTS[h][f])
        return remote(
            msg.at[h, peer, part],
            recv1.at[h, part, pl.ds(me * LOCAL, LOCAL)],
            send1_sem.at[h, f, step - 1],
            recv1_sem.at[h, f, step - 1],
            {"modes": peer},
        )

    def own_out(h, f):
        part = pl.ds(*OUT_PARTS[h][f])
        return pltpu.make_async_copy(
            msg.at[h, me, part], recv1.at[h, part, pl.ds(me * LOCAL, LOCAL)], own1_sem.at[h, f]
        )

    def start_out(h, f):
        for step in range(1, GROUPS):
            out_copy(h, f, step).start()
        own_out(h, f).start()

    def back_copy(h, f, step):
        peer = mode_peer(step)
        part = pl.ds(*BACK_PARTS[h][f])
        return remote(
            send2.at[h, part, pl.ds(peer * LOCAL, LOCAL)],
            recv2.at[h, me, part],
            send2_sem.at[h, f, step - 1],
            recv2_sem.at[h, f, step - 1],
            {"modes": peer},
        )

    def own_back(h, f):
        part = pl.ds(*BACK_PARTS[h][f])
        return pltpu.make_async_copy(
            send2.at[h, part, pl.ds(me * LOCAL, LOCAL)], recv2.at[h, me, part], own2_sem.at[h, f]
        )

    def edge_copy(side, f, owner):
        return remote(
            edge_tile.at[side, f, pl.ds(pl.multiple_of(owner * LOCAL, LOCAL), LOCAL)],
            edge_recv.at[side, f],
            edge_send_sem.at[side, f, owner],
            edge_recv_sem.at[side, f],
            {"modes": owner, "mesh": following if side == 0 else previous},
        )

    def for_edges(action):
        for side, worker in ((0, GROUPS - 1), (1, 0)):

            @pl.when(me == worker)
            def _(side=side):
                def each(owner, carry):
                    action(side, owner)
                    return carry

                lax.fori_loop(0, GROUPS, each, 0)

    def halo_copies(level):
        return (
            remote(
                halo_send.at[level, 0],
                halo_recv.at[level, 0],
                halo_send_sem.at[level, 0],
                halo_recv_sem.at[level, 0],
                {"mesh": following},
            ),
            remote(
                halo_send.at[level, 1],
                halo_recv.at[level, 1],
                halo_send_sem.at[level, 1],
                halo_recv_sem.at[level, 1],
                {"mesh": previous},
            ),
        )

    def pack_faces(level, f, rows, lefts, rights):
        to_next = pltpu.roll(rights[0], EY, 1)
        to_prior = lefts[0]
        for j in range(1, NODES):
            here = group == j
            right = pltpu.roll(rights[j], EY * (j + 1), 1)
            to_next = jnp.where(here, right, to_next)
            to_prior = jnp.where(here, pltpu.roll(lefts[j], EY * j, 1), to_prior)
        halo_send[level, 0, f, rows, :] = to_next
        halo_send[level, 1, f, rows, :] = to_prior

    def order_line(f, i):
        for half in range(2):
            rows = pl.ds(8 * half, 8)
            for j in range(NODES):
                at = f * PLANES_PER_FIELD + i * NODES + j
                vel[at, rows, :] = jnp.take_along_axis(vel[at, rows, :], slots, axis=1)

    def store_message(tiles, at, rows):
        tiles = swap_groups(tiles, lane)
        for k in range(GROUPS):
            for h in range(HALVES):
                msg[h, k, at, rows, :] = tiles[2 * k + h]

    def spread_lines(f, p):
        base = f * PLANES_PER_FIELD
        for half in range(2):
            rows = pl.ds(8 * half, 8)
            tiles = []
            for i in (2 * p, 2 * p + 1):
                tiles += [vel[base + i * NODES + j, rows, :] for j in range(NODES)]
                tiles.append(vel[base + 42 + i, rows, :])
            store_message(tiles, 1 + f * 3 + p, rows)

    for f in range(FIELDS):
        vel_load(f).wait()
        order_line(f, 6)
    for half in range(2):
        rows = pl.ds(8 * half, 8)
        zero = jnp.zeros((8, LANES), jnp.float32)
        tiles = [vel[f * PLANES_PER_FIELD + 48, rows, :] for f in range(FIELDS)]
        tiles = swap_groups(tiles + [zero] * 13, lane)
        for k in range(GROUPS):
            msg[0, k, 0, rows, :] = tiles[2 * k] + pltpu.roll(tiles[2 * k + 1], 3 * SLOT, 1)
    for f in range(FIELDS):

        def two_lines(p, carry, f=f):
            order_line(f, 2 * p)
            order_line(f, 2 * p + 1)
            spread_lines(f, p)
            return carry

        lax.fori_loop(0, 3, two_lines, 0)
        if f == 0:
            pl.semaphore_wait(barrier, greetings)
        start_out(0, f)

    for f in range(FIELDS):
        base = f * PLANES_PER_FIELD
        for half in range(2):
            rows = pl.ds(8 * half, 8)
            lefts = [vel[base + j, rows, :] for j in range(NODES)]
            rights = [vel[base + 42 + j, rows, :] for j in range(NODES)]
            pack_faces(0, f, rows, lefts, rights)
    for copy in halo_copies(0):
        copy.start()

    table_load.wait()
    tt, tl, bb = table.at[0:256, :], table.at[256:512, 0:128], table.at[256:512, 128:256]
    ff, fl, bl = table.at[512:640, :], table.at[640:768, 0:128], table.at[640:768, 128:256]
    slot_all = lax.broadcasted_iota(jnp.int32, (NCOEF, LANES), 1) // SLOT
    low_half = lane < 64

    def shifted(value, slots_up):
        return pltpu.roll(value, (SLOT * slots_up) % LANES, 1) if slots_up % 16 else value

    def to_planes(h, f):
        tiles = [recv1[h, 1 + 3 * f + p] for p in range(3)]
        last = jnp.where(slot_all == 6, shifted(recv1[0, 0], 6 - f - 3 * h), 0.0)
        for j in range(6):
            last = jnp.where(
                slot_all == j, shifted(tiles[j // 2], j - 7 - 8 * (j % 2)), last
            )
        tiles.append(last)
        planes = []
        for p in (0, 2):
            high, low = split_value(jnp.concatenate(tiles[p : p + 2], axis=1))
            value = dot(tt[...], jnp.concatenate([high, low], axis=0)) + dot(tl[...], high)
            for q in range(2):
                at = 4 * f + p + q
                planes.append(value[:NCOEF, q * LANES : (q + 1) * LANES])
                phys[at] = planes[-1]
                span[at] = value[NCOEF:, q * LANES : (q + 1) * LANES]
        high, low = split_value(jnp.concatenate(planes, axis=0))
        value = dot(jnp.concatenate([high, low], axis=1), bb[...]) + dot(high, bl[...])
        for p in range(4):
            cross[4 * f + p] = value[p * NCOEF : (p + 1) * NCOEF]

    def derivative_at(i, a):
        return float(2.0 * DERIV[i, a]) if i < NODES and a < NODES else 0.0

    def advect(h, f):
        def rows_of(block, inner):
            rows = pl.ds(pl.multiple_of(block * 8, 8), 8)
            tiles = [phys[4 * f + p, rows, :] for p in range(4)]
            swapped = [pltpu.roll(tile, 64, 1) for tile in tiles]
            both = tiles[3] + swapped[3]
            for p in range(4):
                i = 2 * p
                stream = both * jnp.where(low_half, derivative_at(i, 6), derivative_at(i + 1, 6))
                for q in range(3):
                    a = 2 * q
                    stream = (
                        stream
                        + tiles[q]
                        * jnp.where(low_half, derivative_at(i, a), derivative_at(i + 1, a + 1))
                        + swapped[q]
                        * jnp.where(low_half, derivative_at(i, a + 1), derivative_at(i + 1, a))
                    )
                at = 4 * f + p
                cross[at, rows, :] = (
                    phys[p, rows, :] * stream
                    + phys[4 + p, rows, :] * cross[at, rows, :]
                    + phys[8 + p, rows, :] * span[at, rows, :]
                )
            return inner

        lax.fori_loop(0, NCOEF // 8, rows_of, 0, unroll=2)
        last = None
        for p in (2, 0):
            pair = jnp.concatenate([cross[4 * f + p], cross[4 * f + p + 1]], axis=1)
            high, low = split_value(pair)
            value = dot(ff[...], jnp.concatenate([high, low], axis=0)) + dot(fl[...], high)
            parts = [value[:, :LANES], value[:, LANES:]]
            if p == 2:
                last = parts.pop()
            for q, part in reversed(list(enumerate(parts))):
                i = 2 * (p + q)
                part = jnp.where(slot_all == 7, shifted(last, 7 - i), part)
                send2[h, 3 * f + p + q] = jnp.where(slot_all == 15, shifted(last, 14 - i), part)
        at = 3 * h + f
        rest = send2[1, TILES - 1] if at else jnp.zeros((NCOEF, LANES), jnp.float32)
        send2[1, TILES - 1] = jnp.where(slot_all == at, shifted(last, at - 6), rest)
        for side, tile in ((0, last), (1, part)):
            if h:
                tile = jnp.where(slot_all < 8, edge_tile[side, f], shifted(tile, 8))
            edge_tile[side, f] = tile
        if h:
            for_edges(lambda side, owner: edge_copy(side, f, owner).start())
        for step in range(1, GROUPS):
            back_copy(h, f, step).start()
        own_back(h, f).start()

    for h in range(HALVES):
        for f in range(FIELDS):
            for step in range(1, GROUPS):
                out_copy(h, f, step).wait_recv()
            own_out(h, f).wait()
            if h == 0:
                start_out(1, f)
            to_planes(h, f)
        for f in range(FIELDS):
            advect(h, f)

    is_first = strip == 0
    is_last = strip == strips - 1
    not_inflow = jnp.logical_not(jnp.logical_and(group == 0, is_first))
    west = group == 0
    east = group == GROUPS - 1
    south = row != 0
    north = row != EY - 1
    has_previous = jnp.where(is_first, 0.0, 1.0)
    has_following = jnp.where(is_last, 0.0, 1.0)
    east_weight = jnp.where(jnp.logical_and(east, is_last), 1.0, 0.5)

    def at_block(block):
        f = block // 2
        rows = pl.ds(pl.multiple_of((block % 2) * 8, 8), 8)
        return f, rows

    def over_blocks(body, first=0, last=2 * FIELDS, unroll=2):
        lax.fori_loop(first, last, lambda block, c: (body(block), c)[1], 0, unroll=unroll)

    def gather_source(f):
        for h in range(HALVES):
            for step in range(1, GROUPS):
                back_copy(h, f, step).wait_recv()
            own_back(h, f).wait()
        base = f * PLANES_PER_FIELD
        for half in range(2):
            rows = pl.ds(8 * half, 8)
            for p in range(3):
                tiles = swap_groups(
                    [recv2[g % 2, g // 2, 3 * f + p, rows, :] for g in range(16)], lane
                )
                for s in range(16):
                    i, j = 2 * p + s // 8, s % 8
                    a, b = (i, j) if j < 7 else (6, i)
                    at = base + a * NODES + b
                    basis[0, at, rows, :] = float(MASS[a, b]) * (
                        SIGMA_BASE * vel[at, rows, :] + tiles[s]
                    )

    def gather_rest():
        for half in range(2):
            rows = pl.ds(8 * half, 8)
            tiles = []
            for k in range(GROUPS):
                tile = recv2[1, k, TILES - 1, rows, :]
                tiles += [tile, shifted(tile, -3)]
            tiles = swap_groups(tiles, lane)
            for f in range(FIELDS):
                at = f * PLANES_PER_FIELD + 48
                basis[0, at, rows, :] = float(MASS[6, 6]) * (
                    SIGMA_BASE * vel[at, rows, :] + tiles[f]
                )

    def along_rows(line):
        bottom, top = line[0], line[6]
        first = jnp.where(south, bottom + pltpu.roll(top, 1, 1), 0.0)
        last = jnp.where(north, top + pltpu.roll(bottom, LANES - 1, 1), 0.0)
        return [first] + list(line[1:6]) + [last]

    def squares(line):
        total = line[1] * line[1]
        for j in range(2, 6):
            total = total + line[j] * line[j]
        return total + 0.5 * (line[0] * line[0] + line[6] * line[6])

    def shift_of(block):
        number = (
            me * LOCAL + (block % 2) * 8 + lax.broadcasted_iota(jnp.int32, (8, LANES), 0)
        )
        wave = jnp.where(number <= NCOEF // 2, number, number - NCOEF // 2).astype(jnp.float32)
        wave = SPAN_WAVE * wave
        return 0.25 * (SIGMA_BASE + wave * wave)

    def finish_inside(level, first=0, last=2 * FIELDS):
        def block_of(block):
            f, rows = at_block(block)
            base = f * PLANES_PER_FIELD
            shift = shift_of(block)
            total = jnp.zeros((8, LANES), jnp.float32)
            inside = []
            for i in range(1, 6):
                line = []
                for j in range(NODES):
                    value = basis[level, base + i * NODES + j, rows, :]
                    if level:
                        value = float(QUAD[i] * QUAD[j]) * (
                            value
                            + float(SCALED_STIFF[i, 0]) * basis[level - 1, base + j, rows, :]
                            + float(SCALED_STIFF[i, 6]) * basis[level - 1, base + 42 + j, rows, :]
                        )
                    line.append(value)
                line = along_rows(line)
                for j in range(NODES):
                    if level or j in (0, 6):
                        basis[level, base + i * NODES + j, rows, :] = line[j]
                total = total + squares(line)
                inside.append(line)
            image = [None] * PLANES_PER_FIELD
            for j in range(NODES):
                column = [None] + [line[j] for line in inside] + [None]
                column = line_product(SCALED_STIFF, column, 1)
                for i in range(NODES):
                    image[i * NODES + j] = column[i]
            energy = jnp.zeros((8, LANES), jnp.float32)
            for i in range(1, 6):
                line = line_product(SCALED_STIFF, inside[i - 1], 1)
                for j in range(NODES):
                    n = i * NODES + j
                    image[n] = image[n] + line[j] + shift * inside[i - 1][j]
                    energy = energy + float(QUAD[i] * QUAD[j]) * (image[n] * inside[i - 1][j])
            for n in range(PLANES_PER_FIELD):
                if level < 2:
                    basis[level + 1, base + n, rows, :] = image[n]
                elif n < 7:
                    last_faces[0, f, n, rows, :] = image[n]
                elif n >= 42:
                    last_faces[1, f, n - 42, rows, :] = image[n]
            moments[2 * level, f, rows, :] = total
            moments[2 * level + 1, f, rows, :] = energy
            if level == 1:
                lefts = [basis[1, base + j, rows, :] for j in range(NODES)]
                rights = [basis[1, base + 42 + j, rows, :] for j in range(NODES)]
                inner_rights = along_rows(
                    [b + pltpu.roll(a, LANES - EY, 1) for a, b in zip(lefts, rights)]
                )
                inner_lefts = along_rows([a + pltpu.roll(b, EY, 1) for a, b in zip(lefts, rights)])
                pack_faces(
                    2,
                    f,
                    rows,
                    [image[j] + float(SCALED_STIFF[0, 6]) * inner_rights[j] for j in range(NODES)],
                    [
                        image[42 + j] + float(SCALED_STIFF[6, 0]) * inner_lefts[j]
                        for j in range(NODES)
                    ],
                )

        over_blocks(block_of, first, last, unroll=6 if last - first > 2 else 2)

    def finish_faces(level):
        def block_of(block):
            f, rows = at_block(block)
            base = f * PLANES_PER_FIELD
            shift = shift_of(block)
            prior = halo_recv[level, 0, f, rows, :]
            after = halo_recv[level, 1, f, rows, :]
            if level == 0:
                prior = SIGMA_BASE * prior
                after = SIGMA_BASE * after
                prior_edge = edge_recv[0, f, rows, :] * has_previous
                after_edge = edge_recv[1, f, rows, :] * has_following
            prior = prior * has_previous
            after = after * has_following
            lefts, rights = [], []
            for j in range(NODES):
                left = basis[level, base + j, rows, :]
                right = basis[level, base + 42 + j, rows, :]
                from_prior = pltpu.roll(prior, LANES - EY * j, 1) if j else prior
                from_after = pltpu.roll(after, LANES - EY * (j + 1), 1)
                if level == 0:
                    from_prior = float(MASS[6, j]) * (
                        from_prior
                        + jnp.where(
                            lane < 8, shifted(prior_edge, -j), shifted(prior_edge, -7 - j)
                        )
                    )
                    from_after = float(MASS[0, j]) * (
                        from_after
                        + jnp.where(
                            lane < 120, shifted(after_edge, 14 - j), shifted(after_edge, 7 - j)
                        )
                    )
                if level == 2:
                    weight = float(QUAD[0] * QUAD[j])
                    from_prior = weight * (from_prior + beside[0, f, j, rows, :])
                    from_after = weight * (from_after + beside[1, f, j, rows, :])
                lefts.append(left + jnp.where(west, from_prior, pltpu.roll(right, EY, 1)))
                rights.append(
                    right + jnp.where(east, from_after, pltpu.roll(left, LANES - EY, 1))
                )
            lefts = [jnp.where(not_inflow, value, 0.0) for value in along_rows(lefts)]
            rights = along_rows(rights)
            moments[2 * level, f, rows, :] = (
                moments[2 * level, f, rows, :]
                + 0.5 * squares(lefts)
                + east_weight * squares(rights)
            )
            energy = moments[2 * level + 1, f, rows, :]
            images = []
            for i, line in ((0, lefts), (6, rights)):
                across = line_product(SCALED_STIFF, line, 1)
                image = []
                for j in range(NODES):
                    basis[level, base + i * NODES + j, rows, :] = line[j]
                    if level < 2:
                        part = basis[level + 1, base + i * NODES + j, rows, :]
                    else:
                        part = last_faces[i // 6, f, j, rows, :]
                    whole = (
                        part
                        + float(SCALED_STIFF[i, 0]) * lefts[j]
                        + float(SCALED_STIFF[i, 6]) * rights[j]
                        + across[j]
                        + shift * line[j]
                    )
                    if level == 1:
                        has_side = has_previous if i == 0 else has_following
                        beside[i // 6, f, j, rows, :] = has_side * (
                            float(SCALED_STIFF[0, 0]) * line[j] + across[j] + shift * line[j]
                        )
                    weight = float(QUAD[i] * QUAD[j])
                    energy = energy + weight * ((whole + part) * line[j])
                    if level < 2:
                        whole = weight * whole
                        basis[level + 1, base + i * NODES + j, rows, :] = whole
                        image.append(whole)
                images.append(image)
            moments[2 * level + 1, f, rows, :] = energy
            if level == 0:
                pack_faces(1, f, rows, images[0], images[1])

        over_blocks(block_of, unroll=6)

    def wait_sent():
        for h in range(HALVES):
            for f in range(FIELDS):
                for step in range(1, GROUPS):
                    out_copy(h, f, step).wait_send()
                    back_copy(h, f, step).wait_send()
        for f in range(FIELDS):
            for_edges(lambda side, owner, f=f: edge_copy(side, f, owner).wait_send())

    def pack_moments(packed, which):
        for m in which:
            for block in range(2 * FIELDS):
                f, half = block // 2, block % 2
                total = jnp.sum(moments[m, f, 8 * half : 8 * half + 8, :], axis=1, keepdims=True)
                packed = jnp.where(lane == 8 * block + m, total, packed)
        return packed

    packed = jnp.zeros((8, LANES), jnp.float32)
    for level in range(3):
        if level == 0:
            for f in range(FIELDS):
                gather_source(f)
                finish_inside(0, 2 * f, 2 * f + 2)
                for side in range(2):
                    edge_copy(side, f, 0).wait_recv()
            gather_rest()
        else:
            finish_inside(level)
            if level == 1:
                for copy in halo_copies(2):
                    copy.start()
            packed = pack_moments(packed, (2 * level - 2, 2 * level - 1))
            if level == 1:
                wait_sent()
        for copy in halo_copies(level):
            copy.wait_recv()
        finish_faces(level)
        if level == 0:
            for copy in halo_copies(1):
                copy.start()
    packed = pack_moments(packed, (4, 5))

    def sum_over(value, slots_ref, mine, count, copies):
        slots_ref[mine] = value
        for copy in copies:
            copy.start()
        for copy in copies:
            copy.wait_recv()
        total = slots_ref[0]
        for k in range(1, count):
            total = total + slots_ref[k]
        return total

    x_copies = [
        remote(
            red_x.at[at_x],
            red_x.at[at_x],
            redx_send_sem.at[step - 1],
            redx_recv_sem.at[step - 1],
            {"mesh": x_peer(step)},
        )
        for step in range(1, mesh_x)
    ]
    z_copies = [
        remote(
            red_z.at[at_z],
            red_z.at[at_z],
            redz_send_sem.at[step - 1],
            redz_recv_sem.at[step - 1],
            {"mesh": z_peer(step)},
        )
        for step in range(1, mesh_z)
    ]
    packed = sum_over(packed, red_x, at_x, mesh_x, x_copies)
    packed = sum_over(packed, red_z, at_z, mesh_z, z_copies)

    m0, m1, m2, m3, m4, m5 = [
        packed if m == 0 else pltpu.roll(packed, LANES - m, 1) for m in range(MOMENTS)
    ]
    s0, s1, s2 = lax.rsqrt(m1), lax.rsqrt(m3), lax.rsqrt(m5)
    l10 = m2 * s0 * s1
    l20 = m3 * s0 * s2
    h21 = m4 * s1 * s2
    d1 = 1.0 - l10 * l10
    l21 = (h21 - l20 * l10) / d1
    d2 = 1.0 - l20 * l20 - l21 * l21 * d1
    y0 = m0 * s0
    y1 = m1 * s1 - l10 * y0
    y2 = m2 * s2 - l20 * y0 - l21 * y1
    c2 = y2 / d2
    c1 = y1 / d1 - l21 * c2
    c0 = y0 - l10 * c1 - l20 * c2
    c0, c1, c2 = c0 * s0, c1 * s1, c2 * s2

    for block in range(2 * FIELDS):
        f, half = block // 2, block % 2
        for k, c in enumerate((c0, c1, c2)):
            factor[k, f, 8 * half : 8 * half + 8, :] = jnp.broadcast_to(
                c[:, 8 * block : 8 * block + 1], (8, LANES)
            )

    for level in range(3):
        for copy in halo_copies(level):
            copy.wait_send()
    for copy in x_copies + z_copies:
        copy.wait_send()


def shards(mesh_x, mesh_z, velocity, element_slot):
    count = FIELDS * PLANES_PER_FIELD
    field = jnp.transpose(velocity, (0, 2, 3, 1, 4)).reshape(count, LOCAL, LANES)
    vmem = pl.BlockSpec(memory_space=pltpu.VMEM)
    f32 = jnp.float32
    dma = pltpu.SemaphoreType.DMA
    *basis, factor0, factor1, factor2 = pl.pallas_call(
        functools.partial(kernel, mesh_x, mesh_z),
        out_shape=[
            jax.ShapeDtypeStruct((count, LOCAL, LANES), f32),
        ]
        * 3
        + [
            jax.ShapeDtypeStruct((FIELDS, LOCAL, LANES), f32),
        ]
        * 3,
        in_specs=[pl.BlockSpec(memory_space=pltpu.HBM)] * 3,
        out_specs=[vmem] * 6,
        scratch_shapes=[
            pltpu.VMEM((count, LOCAL, LANES), f32),
            pltpu.VMEM((1, LANES), jnp.int32),
            pltpu.VMEM((TABLE_ROWS, 256), jnp.bfloat16),
            pltpu.VMEM((HALVES, GROUPS, TILES, LOCAL, LANES), f32),
            pltpu.VMEM((HALVES, TILES, NCOEF, LANES), f32),
            pltpu.VMEM((4 * FIELDS, NCOEF, LANES), f32),
            pltpu.VMEM((4 * FIELDS, NCOEF, LANES), f32),
            pltpu.VMEM((4 * FIELDS, NCOEF, LANES), f32),
            pltpu.VMEM((HALVES, TILES, NCOEF, LANES), f32),
            pltpu.VMEM((HALVES, GROUPS, TILES, LOCAL, LANES), f32),
            pltpu.VMEM((2, FIELDS, NODES, LOCAL, LANES), f32),
            pltpu.VMEM((2, FIELDS, NODES, LOCAL, LANES), f32),
            pltpu.VMEM((2, FIELDS, NCOEF, LANES), f32),
            pltpu.VMEM((2, FIELDS, LOCAL, LANES), f32),
            pltpu.VMEM((MOMENTS, FIELDS, LOCAL, LANES), f32),
            pltpu.VMEM((3, 2, FIELDS, LOCAL, LANES), f32),
            pltpu.VMEM((3, 2, FIELDS, LOCAL, LANES), f32),
            pltpu.VMEM((mesh_x, 8, LANES), f32),
            pltpu.VMEM((mesh_z, 8, LANES), f32),
            dma((HALVES, FIELDS, GROUPS - 1)),
            dma((HALVES, FIELDS, GROUPS - 1)),
            dma((HALVES, FIELDS)),
            dma((HALVES, FIELDS, GROUPS - 1)),
            dma((HALVES, FIELDS, GROUPS - 1)),
            dma((HALVES, FIELDS)),
            dma((3, 2)),
            dma((3, 2)),
            dma((mesh_x - 1,)),
            dma((mesh_x - 1,)),
            dma((mesh_z - 1,)),
            dma((mesh_z - 1,)),
            dma((FIELDS + 2,)),
            dma((2, FIELDS, GROUPS)),
            dma((2, FIELDS)),
        ],
        compiler_params=pltpu.CompilerParams(
            collective_id=0, has_side_effects=True, vmem_limit_bytes=50688 * 1024
        ),
    )(field, element_slot.reshape(1, LANES), jnp.asarray(transform_tables()))
    terms = [
        factor[:, None, None] * level.reshape(FIELDS, NODES, NODES, LOCAL, LANES)
        for level, factor in zip(basis, (factor0, factor1, factor2))
    ]
    result = terms[0] + terms[1] + terms[2]
    return jnp.transpose(result, (0, 3, 1, 2, 4))


def solution(mesh):
    strips = mesh.shape["mesh"]
    mesh_x = 4 if strips % 4 == 0 else 1
    placed = (P(None, "modes", None, None, "mesh"), P("mesh"))
    return jax.shard_map(
        functools.partial(shards, mesh_x, strips // mesh_x),
        mesh=mesh,
        in_specs=placed,
        out_specs=P(None, "modes", None, None, "mesh"),
        check_vma=False,
    )
```

```python
import functools

import jax
import jax.numpy as jnp
import numpy as np
from jax import lax
from jax.experimental import pallas as pl
from jax.experimental.pallas import tpu as pltpu
from jax.sharding import PartitionSpec as P

NODES = 7
FIELDS = 3
GROUPS = 8
LOCAL = 16
NCOEF = 128
LANES = 128
EY = 16
PLANES_PER_FIELD = NODES * NODES
SIGMA_BASE = 8.0
SPAN_WAVE = 0.25
STEP_TIME = 0.01
MOMENTS = 6
TABLE_ROWS = 768
TABLE_HELD = 4096
HALVES = 2
TILES = 10
SLOT = 8
OUT_PARTS = (((0, 4), (4, 3), (7, 3)), ((1, 3), (4, 3), (7, 3)))
BACK_PARTS = (((0, 3), (3, 3), (6, 3)), ((0, 3), (3, 3), (6, 4)))


def gll_tables():
    inner_point = np.sqrt((5.0 - 2.0 * np.sqrt(5.0 / 3.0)) / 11.0)
    outer_point = np.sqrt((5.0 + 2.0 * np.sqrt(5.0 / 3.0)) / 11.0)
    points = np.array([-1.0, -outer_point, -inner_point, 0.0, inner_point, outer_point, 1.0])
    legendre_prev = points * 0.0 + 1.0
    legendre_now = points.copy()
    for degree in range(1, points.shape[0] - 1):
        legendre_next = ((2 * degree + 1) * points * legendre_now - degree * legendre_prev) / (
            degree + 1
        )
        legendre_prev = legendre_now
        legendre_now = legendre_next
    order_value = points.shape[0] - 1
    quadrature = 2.0 / (order_value * (order_value + 1) * legendre_now**2)
    counter = np.arange(points.shape[0])
    same_node = counter[:, None] == counter[None, :]
    distances = np.where(same_node, 1.0, points[:, None] - points[None, :])
    barycentric = 1.0 / np.prod(distances, axis=1)
    off_diagonal = np.where(same_node, 0.0, barycentric[None, :] / barycentric[:, None] / distances)
    derivative = np.where(same_node, -np.sum(off_diagonal, axis=1)[:, None], off_diagonal)
    stiffness = derivative.T @ (quadrature[:, None] * derivative)
    return quadrature, derivative, stiffness


def fourier_tables():
    half_count = NCOEF // 2
    planes = np.arange(NCOEF) * 2.0 * np.pi / NCOEF
    numbers = np.arange(NCOEF)
    wavenumber = np.where(numbers <= half_count, numbers, numbers - half_count)
    cosine_mask = (numbers <= half_count)[None, :]
    phase = planes[:, None] * wavenumber[None, :]
    inverse = np.where(cosine_mask, np.cos(phase), np.sin(phase))
    slope = SPAN_WAVE * wavenumber[None, :] * np.where(cosine_mask, -np.sin(phase), np.cos(phase))
    normaliser = np.where((numbers == 0) | (numbers == half_count), 1.0 / NCOEF, 2.0 / NCOEF)
    forward = normaliser[:, None] * inverse.T
    return inverse, slope, forward


QUAD, DERIV, STIFF = gll_tables()
SCALED_STIFF = STIFF / QUAD[:, None]
MASS = 0.25 * QUAD[:, None] * QUAD[None, :]


def split_table(table):
    high = np.asarray(table, np.float32).astype(jnp.bfloat16)
    low = (np.asarray(table, np.float64) - high.astype(np.float64)).astype(jnp.bfloat16)
    return high, low


def transform_tables():
    inverse, slope, forward = fourier_tables()
    t_high, t_low = split_table(np.concatenate([inverse, slope], axis=0))
    f_high, f_low = split_table(-STEP_TIME * forward)
    padded = np.zeros((8, 8))
    padded[:NODES, :NODES] = 2.0 * DERIV
    b_high, b_low = split_table(np.kron(np.eye(2), np.kron(padded.T, np.eye(SLOT))))
    return np.concatenate(
        [
            np.concatenate([t_high, t_high], axis=1),
            np.concatenate([t_low, np.concatenate([b_high, b_high], axis=0)], axis=1),
            np.concatenate([f_high, f_high], axis=1),
            np.concatenate([f_low, b_low], axis=1),
            np.zeros((TABLE_HELD - TABLE_ROWS, 256), jnp.bfloat16),
        ],
        axis=0,
    )


def split_value(value):
    high = value.astype(jnp.bfloat16)
    low = (value - high.astype(jnp.float32)).astype(jnp.bfloat16)
    return high, low


def dot(left, right):
    return jnp.dot(left, right, preferred_element_type=jnp.float32)


def swap_groups(tiles, lane):
    tiles = list(tiles)
    for bit in (8, 4, 2, 1):
        low = (lane & (SLOT * bit)) == 0
        new = list(tiles)
        for at in range(16):
            if at & bit:
                continue
            first, second = tiles[at], tiles[at + bit]
            if bit == 8:
                moved = pltpu.roll(jnp.where(low, second, first), 64, 1)
                new[at] = jnp.where(low, first, moved)
                new[at + bit] = jnp.where(low, moved, second)
            else:
                new[at] = jnp.where(low, first, pltpu.roll(second, SLOT * bit, 1))
                new[at + bit] = jnp.where(low, pltpu.roll(first, LANES - SLOT * bit, 1), second)
        tiles = new
    return tiles


def weighted_sum(coefficients, values):
    total = None
    for coefficient, value in zip(coefficients, values):
        if value is None:
            continue
        term = float(coefficient) * value
        total = term if total is None else total + term
    return total


def line_product(matrix, line, sign):
    pairs = [(line[k], line[6 - k]) for k in range(3)]
    even = [None if a is None else a + b for a, b in pairs] + [line[3]]
    odd = [None if a is None else a - b for a, b in pairs]
    out = [None] * 7
    for i in range(3):
        even_row = [0.5 * (matrix[i, k] + matrix[i, 6 - k]) for k in range(3)] + [matrix[i, 3]]
        odd_row = [0.5 * (matrix[i, k] - matrix[i, 6 - k]) for k in range(3)]
        even_part = weighted_sum(even_row, even)
        odd_part = weighted_sum(odd_row, odd)
        out[i] = even_part + odd_part
        out[6 - i] = even_part - odd_part if sign > 0 else odd_part - even_part
    if sign > 0:
        out[3] = weighted_sum([matrix[3, k] for k in range(4)], even)
    else:
        out[3] = weighted_sum([matrix[3, k] for k in range(3)], odd)
    return out


class Levels:
    def __init__(self, *buffers):
        self.buffers = buffers

    def __getitem__(self, at):
        return self.buffers[at[0]][at[1:]]

    def __setitem__(self, at, value):
        self.buffers[at[0]][at[1:]] = value


def kernel(
    mesh_x,
    mesh_z,
    vel_hbm,
    slot_hbm,
    table_hbm,
    basis0,
    basis1,
    basis2,
    factor0,
    factor1,
    factor2,
    vel,
    slot,
    table,
    msg,
    recv1,
    phys,
    span,
    cross,
    send2,
    recv2,
    last_faces,
    beside,
    edge_tile,
    edge_recv,
    moments,
    halo_send,
    halo_recv,
    red_x,
    red_z,
    send1_sem,
    recv1_sem,
    own1_sem,
    send2_sem,
    recv2_sem,
    own2_sem,
    halo_send_sem,
    halo_recv_sem,
    redx_send_sem,
    redx_recv_sem,
    redz_send_sem,
    redz_recv_sem,
    load_sem,
    edge_send_sem,
    edge_recv_sem,
):
    def vel_load(f):
        part = pl.ds(f * PLANES_PER_FIELD, PLANES_PER_FIELD)
        return pltpu.make_async_copy(vel_hbm.at[part], vel.at[part], load_sem.at[f])

    slot_load = pltpu.make_async_copy(slot_hbm, slot, load_sem.at[FIELDS])
    table_load = pltpu.make_async_copy(
        table_hbm.at[0:TABLE_ROWS], table, load_sem.at[FIELDS + 1]
    )
    basis = Levels(basis0, basis1, basis2)
    factor = Levels(factor0, factor1, factor2)
    me = lax.axis_index("modes")
    strip = lax.axis_index("mesh")
    strips = mesh_x * mesh_z
    at_x = lax.rem(strip, mesh_x)
    at_z = strip // mesh_x
    following = lax.rem(strip + 1, strips)
    previous = lax.rem(strip + strips - 1, strips)

    def mode_peer(step):
        return lax.rem(me + step, GROUPS)

    def x_peer(step):
        return at_z * mesh_x + lax.rem(at_x + step, mesh_x)

    def z_peer(step):
        return lax.rem(at_z + step, mesh_z) * mesh_x + at_x

    barrier = pltpu.get_barrier_semaphore()
    greeted = [{"modes": mode_peer(step)} for step in range(1, GROUPS)]
    greeted += [{"mesh": following}, {"mesh": previous}]
    greeted += [{"mesh": x_peer(step)} for step in range(1, mesh_x)]
    greeted += [{"mesh": z_peer(step)} for step in range(1, mesh_z)]
    greeted += [{"modes": 0, "mesh": following}, {"modes": GROUPS - 1, "mesh": previous}]
    greetings = len(greeted) - 2
    greetings += jnp.where(jnp.logical_or(me == 0, me == GROUPS - 1), GROUPS, 0)
    for device in greeted:
        pl.semaphore_signal(
            barrier, inc=1, device_id=device, device_id_type=pl.DeviceIdType.MESH
        )

    slot_load.start()
    for f in range(FIELDS):
        vel_load(f).start()
    table_load.start()

    lane = lax.broadcasted_iota(jnp.int32, (8, LANES), 1)
    group = lane // EY
    row = lane % EY
    slot_load.wait()
    slots = jnp.broadcast_to(slot[...], (8, LANES))

    def remote(src, dst, send, recv, device):
        return pltpu.make_async_remote_copy(
            src_ref=src,
            dst_ref=dst,
            send_sem=send,
            recv_sem=recv,
            device_id=device,
            device_id_type=pl.DeviceIdType.MESH,
        )

    def out_copy(h, f, step):
        peer = mode_peer(step)
        part = pl.ds(*OUT_PARTS[h][f])
        return remote(
            msg.at[h, peer, part],
            recv1.at[h, part, pl.ds(me * LOCAL, LOCAL)],
            send1_sem.at[h, f, step - 1],
            recv1_sem.at[h, f, step - 1],
            {"modes": peer},
        )

    def own_out(h, f):
        part = pl.ds(*OUT_PARTS[h][f])
        return pltpu.make_async_copy(
            msg.at[h, me, part], recv1.at[h, part, pl.ds(me * LOCAL, LOCAL)], own1_sem.at[h, f]
        )

    def start_out(h, f):
        for step in range(1, GROUPS):
            out_copy(h, f, step).start()
        own_out(h, f).start()

    def back_copy(h, f, step):
        peer = mode_peer(step)
        part = pl.ds(*BACK_PARTS[h][f])
        return remote(
            send2.at[h, part, pl.ds(peer * LOCAL, LOCAL)],
            recv2.at[h, me, part],
            send2_sem.at[h, f, step - 1],
            recv2_sem.at[h, f, step - 1],
            {"modes": peer},
        )

    def own_back(h, f):
        part = pl.ds(*BACK_PARTS[h][f])
        return pltpu.make_async_copy(
            send2.at[h, part, pl.ds(me * LOCAL, LOCAL)], recv2.at[h, me, part], own2_sem.at[h, f]
        )

    def edge_copy(side, f, owner):
        return remote(
            edge_tile.at[side, f, pl.ds(pl.multiple_of(owner * LOCAL, LOCAL), LOCAL)],
            edge_recv.at[side, f],
            edge_send_sem.at[side, f, owner],
            edge_recv_sem.at[side, f],
            {"modes": owner, "mesh": following if side == 0 else previous},
        )

    def for_edges(action):
        for side, worker in ((0, GROUPS - 1), (1, 0)):

            @pl.when(me == worker)
            def _(side=side):
                def each(owner, carry):
                    action(side, owner)
                    return carry

                lax.fori_loop(0, GROUPS, each, 0)

    def halo_copies(level):
        return (
            remote(
                halo_send.at[level, 0],
                halo_recv.at[level, 0],
                halo_send_sem.at[level, 0],
                halo_recv_sem.at[level, 0],
                {"mesh": following},
            ),
            remote(
                halo_send.at[level, 1],
                halo_recv.at[level, 1],
                halo_send_sem.at[level, 1],
                halo_recv_sem.at[level, 1],
                {"mesh": previous},
            ),
        )

    def pack_faces(level, f, rows, lefts, rights):
        to_next = pltpu.roll(rights[0], EY, 1)
        to_prior = lefts[0]
        for j in range(1, NODES):
            here = group == j
            right = pltpu.roll(rights[j], EY * (j + 1), 1)
            to_next = jnp.where(here, right, to_next)
            to_prior = jnp.where(here, pltpu.roll(lefts[j], EY * j, 1), to_prior)
        halo_send[level, 0, f, rows, :] = to_next
        halo_send[level, 1, f, rows, :] = to_prior

    def order_line(f, i):
        for half in range(2):
            rows = pl.ds(8 * half, 8)
            for j in range(NODES):
                at = f * PLANES_PER_FIELD + i * NODES + j
                vel[at, rows, :] = jnp.take_along_axis(vel[at, rows, :], slots, axis=1)

    def store_message(tiles, at, rows):
        tiles = swap_groups(tiles, lane)
        for k in range(GROUPS):
            for h in range(HALVES):
                msg[h, k, at, rows, :] = tiles[2 * k + h]

    def spread_lines(f, p):
        base = f * PLANES_PER_FIELD
        for half in range(2):
            rows = pl.ds(8 * half, 8)
            tiles = []
            for i in (2 * p, 2 * p + 1):
                tiles += [vel[base + i * NODES + j, rows, :] for j in range(NODES)]
                tiles.append(vel[base + 42 + i, rows, :])
            store_message(tiles, 1 + f * 3 + p, rows)

    for f in range(FIELDS):
        vel_load(f).wait()
        order_line(f, 6)
    for half in range(2):
        rows = pl.ds(8 * half, 8)
        zero = jnp.zeros((8, LANES), jnp.float32)
        tiles = [vel[f * PLANES_PER_FIELD + 48, rows, :] for f in range(FIELDS)]
        tiles = swap_groups(tiles + [zero] * 13, lane)
        for k in range(GROUPS):
            msg[0, k, 0, rows, :] = tiles[2 * k] + pltpu.roll(tiles[2 * k + 1], 3 * SLOT, 1)
    for f in range(FIELDS):

        def two_lines(p, carry, f=f):
            order_line(f, 2 * p)
            order_line(f, 2 * p + 1)
            spread_lines(f, p)
            return carry

        lax.fori_loop(0, 3, two_lines, 0)
        if f == 0:
            pl.semaphore_wait(barrier, greetings)
        start_out(0, f)

    for f in range(FIELDS):
        base = f * PLANES_PER_FIELD
        for half in range(2):
            rows = pl.ds(8 * half, 8)
            lefts = [vel[base + j, rows, :] for j in range(NODES)]
            rights = [vel[base + 42 + j, rows, :] for j in range(NODES)]
            pack_faces(0, f, rows, lefts, rights)
    for copy in halo_copies(0):
        copy.start()

    table_load.wait()
    tt, tl, bb = table.at[0:256, :], table.at[256:512, 0:128], table.at[256:512, 128:256]
    ff, fl, bl = table.at[512:640, :], table.at[640:768, 0:128], table.at[640:768, 128:256]
    slot_all = lax.broadcasted_iota(jnp.int32, (NCOEF, LANES), 1) // SLOT
    low_half = lane < 64

    def shifted(value, slots_up):
        return pltpu.roll(value, (SLOT * slots_up) % LANES, 1) if slots_up % 16 else value

    def to_planes(h, f):
        tiles = [recv1[h, 1 + 3 * f + p] for p in range(3)]
        last = jnp.where(slot_all == 6, shifted(recv1[0, 0], 6 - f - 3 * h), 0.0)
        for j in range(6):
            last = jnp.where(
                slot_all == j, shifted(tiles[j // 2], j - 7 - 8 * (j % 2)), last
            )
        tiles.append(last)
        planes = []
        for p in (0, 2):
            high, low = split_value(jnp.concatenate(tiles[p : p + 2], axis=1))
            value = dot(tt[...], jnp.concatenate([high, low], axis=0)) + dot(tl[...], high)
            for q in range(2):
                at = 4 * f + p + q
                planes.append(value[:NCOEF, q * LANES : (q + 1) * LANES])
                phys[at] = planes[-1]
                span[at] = value[NCOEF:, q * LANES : (q + 1) * LANES]
        high, low = split_value(jnp.concatenate(planes, axis=0))
        value = dot(jnp.concatenate([high, low], axis=1), bb[...]) + dot(high, bl[...])
        for p in range(4):
            cross[4 * f + p] = value[p * NCOEF : (p + 1) * NCOEF]

    def derivative_at(i, a):
        return float(2.0 * DERIV[i, a]) if i < NODES and a < NODES else 0.0

    def advect(h, f):
        def rows_of(block, inner):
            rows = pl.ds(pl.multiple_of(block * 8, 8), 8)
            tiles = [phys[4 * f + p, rows, :] for p in range(4)]
            swapped = [pltpu.roll(tile, 64, 1) for tile in tiles]
            both = tiles[3] + swapped[3]
            for p in range(4):
                i = 2 * p
                stream = both * jnp.where(low_half, derivative_at(i, 6), derivative_at(i + 1, 6))
                for q in range(3):
                    a = 2 * q
                    stream = (
                        stream
                        + tiles[q]
                        * jnp.where(low_half, derivative_at(i, a), derivative_at(i + 1, a + 1))
                        + swapped[q]
                        * jnp.where(low_half, derivative_at(i, a + 1), derivative_at(i + 1, a))
                    )
                at = 4 * f + p
                cross[at, rows, :] = (
                    phys[p, rows, :] * stream
                    + phys[4 + p, rows, :] * cross[at, rows, :]
                    + phys[8 + p, rows, :] * span[at, rows, :]
                )
            return inner

        lax.fori_loop(0, NCOEF // 8, rows_of, 0, unroll=2)
        last = None
        for p in (2, 0):
            pair = jnp.concatenate([cross[4 * f + p], cross[4 * f + p + 1]], axis=1)
            high, low = split_value(pair)
            value = dot(ff[...], jnp.concatenate([high, low], axis=0)) + dot(fl[...], high)
            parts = [value[:, :LANES], value[:, LANES:]]
            if p == 2:
                last = parts.pop()
            for q, part in reversed(list(enumerate(parts))):
                i = 2 * (p + q)
                part = jnp.where(slot_all == 7, shifted(last, 7 - i), part)
                send2[h, 3 * f + p + q] = jnp.where(slot_all == 15, shifted(last, 14 - i), part)
        at = 3 * h + f
        rest = send2[1, TILES - 1] if at else jnp.zeros((NCOEF, LANES), jnp.float32)
        send2[1, TILES - 1] = jnp.where(slot_all == at, shifted(last, at - 6), rest)
        for side, tile in ((0, last), (1, part)):
            if h:
                tile = jnp.where(slot_all < 8, edge_tile[side, f], shifted(tile, 8))
            edge_tile[side, f] = tile
        if h:
            for_edges(lambda side, owner: edge_copy(side, f, owner).start())
        for step in range(1, GROUPS):
            back_copy(h, f, step).start()
        own_back(h, f).start()

    for h in range(HALVES):
        for f in range(FIELDS):
            for step in range(1, GROUPS):
                out_copy(h, f, step).wait_recv()
            own_out(h, f).wait()
            if h == 0:
                start_out(1, f)
            to_planes(h, f)
        for f in range(FIELDS):
            advect(h, f)

    is_first = strip == 0
    is_last = strip == strips - 1
    not_inflow = jnp.logical_not(jnp.logical_and(group == 0, is_first))
    west = group == 0
    east = group == GROUPS - 1
    south = row != 0
    north = row != EY - 1
    has_previous = jnp.where(is_first, 0.0, 1.0)
    has_following = jnp.where(is_last, 0.0, 1.0)
    east_weight = jnp.where(jnp.logical_and(east, is_last), 1.0, 0.5)

    def at_block(block):
        f = block // 2
        rows = pl.ds(pl.multiple_of((block % 2) * 8, 8), 8)
        return f, rows

    def over_blocks(body, first=0, last=2 * FIELDS, unroll=2):
        lax.fori_loop(first, last, lambda block, c: (body(block), c)[1], 0, unroll=unroll)

    def gather_source(f):
        for h in range(HALVES):
            for step in range(1, GROUPS):
                back_copy(h, f, step).wait_recv()
            own_back(h, f).wait()
        base = f * PLANES_PER_FIELD
        for half in range(2):
            rows = pl.ds(8 * half, 8)
            for p in range(3):
                tiles = swap_groups(
                    [recv2[g % 2, g // 2, 3 * f + p, rows, :] for g in range(16)], lane
                )
                for s in range(16):
                    i, j = 2 * p + s // 8, s % 8
                    a, b = (i, j) if j < 7 else (6, i)
                    at = base + a * NODES + b
                    basis[0, at, rows, :] = float(MASS[a, b]) * (
                        SIGMA_BASE * vel[at, rows, :] + tiles[s]
                    )

    def gather_rest():
        for half in range(2):
            rows = pl.ds(8 * half, 8)
            tiles = []
            for k in range(GROUPS):
                tile = recv2[1, k, TILES - 1, rows, :]
                tiles += [tile, shifted(tile, -3)]
            tiles = swap_groups(tiles, lane)
            for f in range(FIELDS):
                at = f * PLANES_PER_FIELD + 48
                basis[0, at, rows, :] = float(MASS[6, 6]) * (
                    SIGMA_BASE * vel[at, rows, :] + tiles[f]
                )

    def along_rows(line):
        bottom, top = line[0], line[6]
        first = jnp.where(south, bottom + pltpu.roll(top, 1, 1), 0.0)
        last = jnp.where(north, top + pltpu.roll(bottom, LANES - 1, 1), 0.0)
        return [first] + list(line[1:6]) + [last]

    def squares(line):
        total = line[1] * line[1]
        for j in range(2, 6):
            total = total + line[j] * line[j]
        return total + 0.5 * (line[0] * line[0] + line[6] * line[6])

    def shift_of(block):
        number = (
            me * LOCAL + (block % 2) * 8 + lax.broadcasted_iota(jnp.int32, (8, LANES), 0)
        )
        wave = jnp.where(number <= NCOEF // 2, number, number - NCOEF // 2).astype(jnp.float32)
        wave = SPAN_WAVE * wave
        return 0.25 * (SIGMA_BASE + wave * wave)

    def finish_inside(level, first=0, last=2 * FIELDS):
        def block_of(block):
            f, rows = at_block(block)
            base = f * PLANES_PER_FIELD
            shift = shift_of(block)
            total = jnp.zeros((8, LANES), jnp.float32)
            inside = []
            for i in range(1, 6):
                line = []
                for j in range(NODES):
                    value = basis[level, base + i * NODES + j, rows, :]
                    if level:
                        value = float(QUAD[i] * QUAD[j]) * (
                            value
                            + float(SCALED_STIFF[i, 0]) * basis[level - 1, base + j, rows, :]
                            + float(SCALED_STIFF[i, 6]) * basis[level - 1, base + 42 + j, rows, :]
                        )
                    line.append(value)
                line = along_rows(line)
                for j in range(NODES):
                    if level or j in (0, 6):
                        basis[level, base + i * NODES + j, rows, :] = line[j]
                total = total + squares(line)
                inside.append(line)
            image = [None] * PLANES_PER_FIELD
            for j in range(NODES):
                column = [None] + [line[j] for line in inside] + [None]
                column = line_product(SCALED_STIFF, column, 1)
                for i in range(NODES):
                    image[i * NODES + j] = column[i]
            energy = jnp.zeros((8, LANES), jnp.float32)
            for i in range(1, 6):
                line = line_product(SCALED_STIFF, inside[i - 1], 1)
                for j in range(NODES):
                    n = i * NODES + j
                    image[n] = image[n] + line[j] + shift * inside[i - 1][j]
                    energy = energy + float(QUAD[i] * QUAD[j]) * (image[n] * inside[i - 1][j])
            for n in range(PLANES_PER_FIELD):
                if level < 2:
                    basis[level + 1, base + n, rows, :] = image[n]
                elif n < 7:
                    last_faces[0, f, n, rows, :] = image[n]
                elif n >= 42:
                    last_faces[1, f, n - 42, rows, :] = image[n]
            moments[2 * level, f, rows, :] = total
            moments[2 * level + 1, f, rows, :] = energy
            if level == 1:
                lefts = [basis[1, base + j, rows, :] for j in range(NODES)]
                rights = [basis[1, base + 42 + j, rows, :] for j in range(NODES)]
                inner_rights = along_rows(
                    [b + pltpu.roll(a, LANES - EY, 1) for a, b in zip(lefts, rights)]
                )
                inner_lefts = along_rows([a + pltpu.roll(b, EY, 1) for a, b in zip(lefts, rights)])
                pack_faces(
                    2,
                    f,
                    rows,
                    [image[j] + float(SCALED_STIFF[0, 6]) * inner_rights[j] for j in range(NODES)],
                    [
                        image[42 + j] + float(SCALED_STIFF[6, 0]) * inner_lefts[j]
                        for j in range(NODES)
                    ],
                )

        over_blocks(block_of, first, last, unroll=6 if last - first > 2 else 2)

    def finish_faces(level):
        def block_of(block):
            f, rows = at_block(block)
            base = f * PLANES_PER_FIELD
            shift = shift_of(block)
            prior = halo_recv[level, 0, f, rows, :]
            after = halo_recv[level, 1, f, rows, :]
            if level == 0:
                prior = SIGMA_BASE * prior
                after = SIGMA_BASE * after
                prior_edge = edge_recv[0, f, rows, :] * has_previous
                after_edge = edge_recv[1, f, rows, :] * has_following
            prior = prior * has_previous
            after = after * has_following
            lefts, rights = [], []
            for j in range(NODES):
                left = basis[level, base + j, rows, :]
                right = basis[level, base + 42 + j, rows, :]
                from_prior = pltpu.roll(prior, LANES - EY * j, 1) if j else prior
                from_after = pltpu.roll(after, LANES - EY * (j + 1), 1)
                if level == 0:
                    from_prior = float(MASS[6, j]) * (
                        from_prior
                        + jnp.where(
                            lane < 8, shifted(prior_edge, -j), shifted(prior_edge, -7 - j)
                        )
                    )
                    from_after = float(MASS[0, j]) * (
                        from_after
                        + jnp.where(
                            lane < 120, shifted(after_edge, 14 - j), shifted(after_edge, 7 - j)
                        )
                    )
                if level == 2:
                    weight = float(QUAD[0] * QUAD[j])
                    from_prior = weight * (from_prior + beside[0, f, j, rows, :])
                    from_after = weight * (from_after + beside[1, f, j, rows, :])
                lefts.append(left + jnp.where(west, from_prior, pltpu.roll(right, EY, 1)))
                rights.append(
                    right + jnp.where(east, from_after, pltpu.roll(left, LANES - EY, 1))
                )
            lefts = [jnp.where(not_inflow, value, 0.0) for value in along_rows(lefts)]
            rights = along_rows(rights)
            moments[2 * level, f, rows, :] = (
                moments[2 * level, f, rows, :]
                + 0.5 * squares(lefts)
                + east_weight * squares(rights)
            )
            energy = moments[2 * level + 1, f, rows, :]
            images = []
            for i, line in ((0, lefts), (6, rights)):
                across = line_product(SCALED_STIFF, line, 1)
                image = []
                for j in range(NODES):
                    basis[level, base + i * NODES + j, rows, :] = line[j]
                    if level < 2:
                        part = basis[level + 1, base + i * NODES + j, rows, :]
                    else:
                        part = last_faces[i // 6, f, j, rows, :]
                    whole = (
                        part
                        + float(SCALED_STIFF[i, 0]) * lefts[j]
                        + float(SCALED_STIFF[i, 6]) * rights[j]
                        + across[j]
                        + shift * line[j]
                    )
                    if level == 1:
                        has_side = has_previous if i == 0 else has_following
                        beside[i // 6, f, j, rows, :] = has_side * (
                            float(SCALED_STIFF[0, 0]) * line[j] + across[j] + shift * line[j]
                        )
                    weight = float(QUAD[i] * QUAD[j])
                    energy = energy + weight * ((whole + part) * line[j])
                    if level < 2:
                        whole = weight * whole
                        basis[level + 1, base + i * NODES + j, rows, :] = whole
                        image.append(whole)
                images.append(image)
            moments[2 * level + 1, f, rows, :] = energy
            if level == 0:
                pack_faces(1, f, rows, images[0], images[1])

        over_blocks(block_of, unroll=6)

    def wait_sent():
        for h in range(HALVES):
            for f in range(FIELDS):
                for step in range(1, GROUPS):
                    out_copy(h, f, step).wait_send()
                    back_copy(h, f, step).wait_send()
        for f in range(FIELDS):
            for_edges(lambda side, owner, f=f: edge_copy(side, f, owner).wait_send())

    def pack_moments(packed, which):
        for m in which:
            for block in range(2 * FIELDS):
                f, half = block // 2, block % 2
                total = jnp.sum(moments[m, f, 8 * half : 8 * half + 8, :], axis=1, keepdims=True)
                packed = jnp.where(lane == 8 * block + m, total, packed)
        return packed

    packed = jnp.zeros((8, LANES), jnp.float32)
    for level in range(3):
        if level == 0:
            for f in range(FIELDS):
                gather_source(f)
                finish_inside(0, 2 * f, 2 * f + 2)
                for side in range(2):
                    edge_copy(side, f, 0).wait_recv()
            gather_rest()
        else:
            finish_inside(level)
            if level == 1:
                for copy in halo_copies(2):
                    copy.start()
            packed = pack_moments(packed, (2 * level - 2, 2 * level - 1))
            if level == 1:
                wait_sent()
        for copy in halo_copies(level):
            copy.wait_recv()
        finish_faces(level)
        if level == 0:
            for copy in halo_copies(1):
                copy.start()
    packed = pack_moments(packed, (4, 5))

    def sum_over(value, slots_ref, mine, count, copies):
        slots_ref[mine] = value
        for copy in copies:
            copy.start()
        for copy in copies:
            copy.wait_recv()
        total = slots_ref[0]
        for k in range(1, count):
            total = total + slots_ref[k]
        return total

    x_copies = [
        remote(
            red_x.at[at_x],
            red_x.at[at_x],
            redx_send_sem.at[step - 1],
            redx_recv_sem.at[step - 1],
            {"mesh": x_peer(step)},
        )
        for step in range(1, mesh_x)
    ]
    z_copies = [
        remote(
            red_z.at[at_z],
            red_z.at[at_z],
            redz_send_sem.at[step - 1],
            redz_recv_sem.at[step - 1],
            {"mesh": z_peer(step)},
        )
        for step in range(1, mesh_z)
    ]
    packed = sum_over(packed, red_z, at_z, mesh_z, z_copies)
    packed = sum_over(packed, red_x, at_x, mesh_x, x_copies)

    m0, m1, m2, m3, m4, m5 = [
        packed if m == 0 else pltpu.roll(packed, LANES - m, 1) for m in range(MOMENTS)
    ]
    s0, s1, s2 = lax.rsqrt(m1), lax.rsqrt(m3), lax.rsqrt(m5)
    l10 = m2 * s0 * s1
    l20 = m3 * s0 * s2
    h21 = m4 * s1 * s2
    d1 = 1.0 - l10 * l10
    l21 = (h21 - l20 * l10) / d1
    d2 = 1.0 - l20 * l20 - l21 * l21 * d1
    y0 = m0 * s0
    y1 = m1 * s1 - l10 * y0
    y2 = m2 * s2 - l20 * y0 - l21 * y1
    c2 = y2 / d2
    c1 = y1 / d1 - l21 * c2
    c0 = y0 - l10 * c1 - l20 * c2
    c0, c1, c2 = c0 * s0, c1 * s1, c2 * s2

    for block in range(2 * FIELDS):
        f, half = block // 2, block % 2
        for k, c in enumerate((c0, c1, c2)):
            factor[k, f, 8 * half : 8 * half + 8, :] = jnp.broadcast_to(
                c[:, 8 * block : 8 * block + 1], (8, LANES)
            )

    for level in range(3):
        for copy in halo_copies(level):
            copy.wait_send()
    for copy in x_copies + z_copies:
        copy.wait_send()


def shards(mesh_x, mesh_z, velocity, element_slot):
    count = FIELDS * PLANES_PER_FIELD
    field = jnp.transpose(velocity, (0, 2, 3, 1, 4)).reshape(count, LOCAL, LANES)
    vmem = pl.BlockSpec(memory_space=pltpu.VMEM)
    f32 = jnp.float32
    dma = pltpu.SemaphoreType.DMA
    *basis, factor0, factor1, factor2 = pl.pallas_call(
        functools.partial(kernel, mesh_x, mesh_z),
        out_shape=[
            jax.ShapeDtypeStruct((count, LOCAL, LANES), f32),
        ]
        * 3
        + [
            jax.ShapeDtypeStruct((FIELDS, LOCAL, LANES), f32),
        ]
        * 3,
        in_specs=[pl.BlockSpec(memory_space=pltpu.HBM)] * 3,
        out_specs=[vmem] * 6,
        scratch_shapes=[
            pltpu.VMEM((count, LOCAL, LANES), f32),
            pltpu.VMEM((1, LANES), jnp.int32),
            pltpu.VMEM((TABLE_ROWS, 256), jnp.bfloat16),
            pltpu.VMEM((HALVES, GROUPS, TILES, LOCAL, LANES), f32),
            pltpu.VMEM((HALVES, TILES, NCOEF, LANES), f32),
            pltpu.VMEM((4 * FIELDS, NCOEF, LANES), f32),
            pltpu.VMEM((4 * FIELDS, NCOEF, LANES), f32),
            pltpu.VMEM((4 * FIELDS, NCOEF, LANES), f32),
            pltpu.VMEM((HALVES, TILES, NCOEF, LANES), f32),
            pltpu.VMEM((HALVES, GROUPS, TILES, LOCAL, LANES), f32),
            pltpu.VMEM((2, FIELDS, NODES, LOCAL, LANES), f32),
            pltpu.VMEM((2, FIELDS, NODES, LOCAL, LANES), f32),
            pltpu.VMEM((2, FIELDS, NCOEF, LANES), f32),
            pltpu.VMEM((2, FIELDS, LOCAL, LANES), f32),
            pltpu.VMEM((MOMENTS, FIELDS, LOCAL, LANES), f32),
            pltpu.VMEM((3, 2, FIELDS, LOCAL, LANES), f32),
            pltpu.VMEM((3, 2, FIELDS, LOCAL, LANES), f32),
            pltpu.VMEM((mesh_x, 8, LANES), f32),
            pltpu.VMEM((mesh_z, 8, LANES), f32),
            dma((HALVES, FIELDS, GROUPS - 1)),
            dma((HALVES, FIELDS, GROUPS - 1)),
            dma((HALVES, FIELDS)),
            dma((HALVES, FIELDS, GROUPS - 1)),
            dma((HALVES, FIELDS, GROUPS - 1)),
            dma((HALVES, FIELDS)),
            dma((3, 2)),
            dma((3, 2)),
            dma((mesh_x - 1,)),
            dma((mesh_x - 1,)),
            dma((mesh_z - 1,)),
            dma((mesh_z - 1,)),
            dma((FIELDS + 2,)),
            dma((2, FIELDS, GROUPS)),
            dma((2, FIELDS)),
        ],
        compiler_params=pltpu.CompilerParams(
            collective_id=0, has_side_effects=True, vmem_limit_bytes=50688 * 1024
        ),
    )(field, element_slot.reshape(1, LANES), jnp.asarray(transform_tables()))
    terms = [
        factor[:, None, None] * level.reshape(FIELDS, NODES, NODES, LOCAL, LANES)
        for level, factor in zip(basis, (factor0, factor1, factor2))
    ]
    result = terms[0] + terms[1] + terms[2]
    return jnp.transpose(result, (0, 3, 1, 2, 4))


def solution(mesh):
    strips = mesh.shape["mesh"]
    mesh_x = 4 if strips % 4 == 0 else 1
    placed = (P(None, "modes", None, None, "mesh"), P("mesh"))
    return jax.shard_map(
        functools.partial(shards, mesh_x, strips // mesh_x),
        mesh=mesh,
        in_specs=placed,
        out_specs=P(None, "modes", None, None, "mesh"),
        check_vma=False,
    )
```

```python
import functools

import jax
import jax.numpy as jnp
import numpy as np
from jax import lax
from jax.experimental import pallas as pl
from jax.experimental.pallas import tpu as pltpu
from jax.sharding import PartitionSpec as P

NODES = 7
FIELDS = 3
GROUPS = 8
LOCAL = 16
NCOEF = 128
LANES = 128
EY = 16
PLANES_PER_FIELD = NODES * NODES
SIGMA_BASE = 8.0
SPAN_WAVE = 0.25
STEP_TIME = 0.01
MOMENTS = 6
TABLE_ROWS = 768
TABLE_HELD = 4096
HALVES = 2
TILES = 10
SLOT = 8
OUT_PARTS = (((0, 4), (4, 3), (7, 3)), ((1, 3), (4, 3), (7, 3)))
BACK_PARTS = (((0, 3), (3, 3), (6, 3)), ((0, 3), (3, 3), (6, 4)))


def gll_tables():
    inner_point = np.sqrt((5.0 - 2.0 * np.sqrt(5.0 / 3.0)) / 11.0)
    outer_point = np.sqrt((5.0 + 2.0 * np.sqrt(5.0 / 3.0)) / 11.0)
    points = np.array([-1.0, -outer_point, -inner_point, 0.0, inner_point, outer_point, 1.0])
    legendre_prev = points * 0.0 + 1.0
    legendre_now = points.copy()
    for degree in range(1, points.shape[0] - 1):
        legendre_next = ((2 * degree + 1) * points * legendre_now - degree * legendre_prev) / (
            degree + 1
        )
        legendre_prev = legendre_now
        legendre_now = legendre_next
    order_value = points.shape[0] - 1
    quadrature = 2.0 / (order_value * (order_value + 1) * legendre_now**2)
    counter = np.arange(points.shape[0])
    same_node = counter[:, None] == counter[None, :]
    distances = np.where(same_node, 1.0, points[:, None] - points[None, :])
    barycentric = 1.0 / np.prod(distances, axis=1)
    off_diagonal = np.where(same_node, 0.0, barycentric[None, :] / barycentric[:, None] / distances)
    derivative = np.where(same_node, -np.sum(off_diagonal, axis=1)[:, None], off_diagonal)
    stiffness = derivative.T @ (quadrature[:, None] * derivative)
    return quadrature, derivative, stiffness


def fourier_tables():
    half_count = NCOEF // 2
    planes = np.arange(NCOEF) * 2.0 * np.pi / NCOEF
    numbers = np.arange(NCOEF)
    wavenumber = np.where(numbers <= half_count, numbers, numbers - half_count)
    cosine_mask = (numbers <= half_count)[None, :]
    phase = planes[:, None] * wavenumber[None, :]
    inverse = np.where(cosine_mask, np.cos(phase), np.sin(phase))
    slope = SPAN_WAVE * wavenumber[None, :] * np.where(cosine_mask, -np.sin(phase), np.cos(phase))
    normaliser = np.where((numbers == 0) | (numbers == half_count), 1.0 / NCOEF, 2.0 / NCOEF)
    forward = normaliser[:, None] * inverse.T
    return inverse, slope, forward


QUAD, DERIV, STIFF = gll_tables()
SCALED_STIFF = STIFF / QUAD[:, None]
MASS = 0.25 * QUAD[:, None] * QUAD[None, :]


def split_table(table):
    high = np.asarray(table, np.float32).astype(jnp.bfloat16)
    low = (np.asarray(table, np.float64) - high.astype(np.float64)).astype(jnp.bfloat16)
    return high, low


def transform_tables():
    inverse, slope, forward = fourier_tables()
    t_high, t_low = split_table(np.concatenate([inverse, slope], axis=0))
    f_high, f_low = split_table(-STEP_TIME * forward)
    padded = np.zeros((8, 8))
    padded[:NODES, :NODES] = 2.0 * DERIV
    b_high, b_low = split_table(np.kron(np.eye(2), np.kron(padded.T, np.eye(SLOT))))
    return np.concatenate(
        [
            np.concatenate([t_high, t_high], axis=1),
            np.concatenate([t_low, np.concatenate([b_high, b_high], axis=0)], axis=1),
            np.concatenate([f_high, f_high], axis=1),
            np.concatenate([f_low, b_low], axis=1),
            np.zeros((TABLE_HELD - TABLE_ROWS, 256), jnp.bfloat16),
        ],
        axis=0,
    )


def split_value(value):
    high = value.astype(jnp.bfloat16)
    low = (value - high.astype(jnp.float32)).astype(jnp.bfloat16)
    return high, low


def dot(left, right):
    return jnp.dot(left, right, preferred_element_type=jnp.float32)


def swap_groups(tiles, lane):
    tiles = list(tiles)
    for bit in (8, 4, 2, 1):
        low = (lane & (SLOT * bit)) == 0
        new = list(tiles)
        for at in range(16):
            if at & bit:
                continue
            first, second = tiles[at], tiles[at + bit]
            if bit == 8:
                moved = pltpu.roll(jnp.where(low, second, first), 64, 1)
                new[at] = jnp.where(low, first, moved)
                new[at + bit] = jnp.where(low, moved, second)
            else:
                new[at] = jnp.where(low, first, pltpu.roll(second, SLOT * bit, 1))
                new[at + bit] = jnp.where(low, pltpu.roll(first, LANES - SLOT * bit, 1), second)
        tiles = new
    return tiles


def weighted_sum(coefficients, values):
    total = None
    for coefficient, value in zip(coefficients, values):
        if value is None:
            continue
        term = float(coefficient) * value
        total = term if total is None else total + term
    return total


def line_product(matrix, line, sign):
    pairs = [(line[k], line[6 - k]) for k in range(3)]
    even = [None if a is None else a + b for a, b in pairs] + [line[3]]
    odd = [None if a is None else a - b for a, b in pairs]
    out = [None] * 7
    for i in range(3):
        even_row = [0.5 * (matrix[i, k] + matrix[i, 6 - k]) for k in range(3)] + [matrix[i, 3]]
        odd_row = [0.5 * (matrix[i, k] - matrix[i, 6 - k]) for k in range(3)]
        even_part = weighted_sum(even_row, even)
        odd_part = weighted_sum(odd_row, odd)
        out[i] = even_part + odd_part
        out[6 - i] = even_part - odd_part if sign > 0 else odd_part - even_part
    if sign > 0:
        out[3] = weighted_sum([matrix[3, k] for k in range(4)], even)
    else:
        out[3] = weighted_sum([matrix[3, k] for k in range(3)], odd)
    return out


class Levels:
    def __init__(self, *buffers):
        self.buffers = buffers

    def __getitem__(self, at):
        return self.buffers[at[0]][at[1:]]

    def __setitem__(self, at, value):
        self.buffers[at[0]][at[1:]] = value


def kernel(
    mesh_x,
    mesh_z,
    vel_hbm,
    slot_hbm,
    table_hbm,
    basis0,
    basis1,
    basis2,
    factor0,
    factor1,
    factor2,
    vel,
    slot,
    table,
    msg,
    recv1,
    phys,
    span,
    cross,
    send2,
    recv2,
    last_faces,
    beside,
    edge_tile,
    edge_recv,
    moments,
    halo_send,
    halo_recv,
    red_x,
    red_z,
    send1_sem,
    recv1_sem,
    own1_sem,
    send2_sem,
    recv2_sem,
    own2_sem,
    halo_send_sem,
    halo_recv_sem,
    redx_send_sem,
    redx_recv_sem,
    redz_send_sem,
    redz_recv_sem,
    load_sem,
    edge_send_sem,
    edge_recv_sem,
):
    def vel_load(f):
        part = pl.ds(f * PLANES_PER_FIELD, PLANES_PER_FIELD)
        return pltpu.make_async_copy(vel_hbm.at[part], vel.at[part], load_sem.at[f])

    slot_load = pltpu.make_async_copy(slot_hbm, slot, load_sem.at[FIELDS])
    table_load = pltpu.make_async_copy(
        table_hbm.at[0:TABLE_ROWS], table, load_sem.at[FIELDS + 1]
    )
    basis = Levels(basis0, basis1, basis2)
    factor = Levels(factor0, factor1, factor2)
    me = lax.axis_index("modes")
    strip = lax.axis_index("mesh")
    strips = mesh_x * mesh_z
    at_x = lax.rem(strip, mesh_x)
    at_z = strip // mesh_x
    following = lax.rem(strip + 1, strips)
    previous = lax.rem(strip + strips - 1, strips)

    def mode_peer(step):
        return lax.rem(me + step, GROUPS)

    def x_peer(step):
        return at_z * mesh_x + lax.rem(at_x + step, mesh_x)

    def z_peer(step):
        return lax.rem(at_z + step, mesh_z) * mesh_x + at_x

    barrier = pltpu.get_barrier_semaphore()
    greeted = [{"modes": mode_peer(step)} for step in range(1, GROUPS)]
    greeted += [{"mesh": following}, {"mesh": previous}]
    greeted += [{"mesh": x_peer(step)} for step in range(1, mesh_x)]
    greeted += [{"mesh": z_peer(step)} for step in range(1, mesh_z)]
    greeted += [{"modes": 0, "mesh": following}, {"modes": GROUPS - 1, "mesh": previous}]
    greetings = len(greeted) - 2
    greetings += jnp.where(jnp.logical_or(me == 0, me == GROUPS - 1), GROUPS, 0)
    for device in greeted:
        pl.semaphore_signal(
            barrier, inc=1, device_id=device, device_id_type=pl.DeviceIdType.MESH
        )

    slot_load.start()
    for f in range(FIELDS):
        vel_load(f).start()
    table_load.start()

    lane = lax.broadcasted_iota(jnp.int32, (8, LANES), 1)
    group = lane // EY
    row = lane % EY
    slot_load.wait()
    slots = jnp.broadcast_to(slot[...], (8, LANES))

    def remote(src, dst, send, recv, device):
        return pltpu.make_async_remote_copy(
            src_ref=src,
            dst_ref=dst,
            send_sem=send,
            recv_sem=recv,
            device_id=device,
            device_id_type=pl.DeviceIdType.MESH,
        )

    def out_copy(h, f, step):
        peer = mode_peer(step)
        part = pl.ds(*OUT_PARTS[h][f])
        return remote(
            msg.at[h, peer, part],
            recv1.at[h, part, pl.ds(me * LOCAL, LOCAL)],
            send1_sem.at[h, f, step - 1],
            recv1_sem.at[h, f, step - 1],
            {"modes": peer},
        )

    def own_out(h, f):
        part = pl.ds(*OUT_PARTS[h][f])
        return pltpu.make_async_copy(
            msg.at[h, me, part], recv1.at[h, part, pl.ds(me * LOCAL, LOCAL)], own1_sem.at[h, f]
        )

    def start_out(h, f):
        for step in range(1, GROUPS):
            out_copy(h, f, step).start()
        own_out(h, f).start()

    def back_copy(h, f, step):
        peer = mode_peer(step)
        part = pl.ds(*BACK_PARTS[h][f])
        return remote(
            send2.at[h, part, pl.ds(peer * LOCAL, LOCAL)],
            recv2.at[h, me, part],
            send2_sem.at[h, f, step - 1],
            recv2_sem.at[h, f, step - 1],
            {"modes": peer},
        )

    def own_back(h, f):
        part = pl.ds(*BACK_PARTS[h][f])
        return pltpu.make_async_copy(
            send2.at[h, part, pl.ds(me * LOCAL, LOCAL)], recv2.at[h, me, part], own2_sem.at[h, f]
        )

    def edge_copy(side, f, owner):
        return remote(
            edge_tile.at[side, f, pl.ds(pl.multiple_of(owner * LOCAL, LOCAL), LOCAL)],
            edge_recv.at[side, f],
            edge_send_sem.at[side, f, owner],
            edge_recv_sem.at[side, f],
            {"modes": owner, "mesh": following if side == 0 else previous},
        )

    def for_edges(action):
        for side, worker in ((0, GROUPS - 1), (1, 0)):

            @pl.when(me == worker)
            def _(side=side):
                def each(owner, carry):
                    action(side, owner)
                    return carry

                lax.fori_loop(0, GROUPS, each, 0)

    def halo_copies(level):
        return (
            remote(
                halo_send.at[level, 0],
                halo_recv.at[level, 0],
                halo_send_sem.at[level, 0],
                halo_recv_sem.at[level, 0],
                {"mesh": following},
            ),
            remote(
                halo_send.at[level, 1],
                halo_recv.at[level, 1],
                halo_send_sem.at[level, 1],
                halo_recv_sem.at[level, 1],
                {"mesh": previous},
            ),
        )

    def pack_faces(level, f, rows, lefts, rights):
        to_next = pltpu.roll(rights[0], EY, 1)
        to_prior = lefts[0]
        for j in range(1, NODES):
            here = group == j
            right = pltpu.roll(rights[j], EY * (j + 1), 1)
            to_next = jnp.where(here, right, to_next)
            to_prior = jnp.where(here, pltpu.roll(lefts[j], EY * j, 1), to_prior)
        halo_send[level, 0, f, rows, :] = to_next
        halo_send[level, 1, f, rows, :] = to_prior

    def order_line(f, i):
        for half in range(2):
            rows = pl.ds(8 * half, 8)
            for j in range(NODES):
                at = f * PLANES_PER_FIELD + i * NODES + j
                vel[at, rows, :] = jnp.take_along_axis(vel[at, rows, :], slots, axis=1)

    def store_message(tiles, at, rows):
        tiles = swap_groups(tiles, lane)
        for k in range(GROUPS):
            for h in range(HALVES):
                msg[h, k, at, rows, :] = tiles[2 * k + h]

    def spread_lines(f, p):
        base = f * PLANES_PER_FIELD
        for half in range(2):
            rows = pl.ds(8 * half, 8)
            tiles = []
            for i in (2 * p, 2 * p + 1):
                tiles += [vel[base + i * NODES + j, rows, :] for j in range(NODES)]
                tiles.append(vel[base + 42 + i, rows, :])
            store_message(tiles, 1 + f * 3 + p, rows)

    def spread_field(f):
        def two_lines(p, carry):
            order_line(f, 2 * p)
            order_line(f, 2 * p + 1)
            spread_lines(f, p)
            return carry

        lax.fori_loop(0, 3, two_lines, 0)

    vel_load(0).wait()
    order_line(0, 6)
    spread_field(0)
    for f in range(1, FIELDS):
        vel_load(f).wait()
        order_line(f, 6)
    for half in range(2):
        rows = pl.ds(8 * half, 8)
        zero = jnp.zeros((8, LANES), jnp.float32)
        tiles = [vel[f * PLANES_PER_FIELD + 48, rows, :] for f in range(FIELDS)]
        tiles = swap_groups(tiles + [zero] * 13, lane)
        for k in range(GROUPS):
            msg[0, k, 0, rows, :] = tiles[2 * k] + pltpu.roll(tiles[2 * k + 1], 3 * SLOT, 1)
    pl.semaphore_wait(barrier, greetings)
    for f in range(FIELDS):
        if f:
            spread_field(f)
        start_out(0, f)

    for f in range(FIELDS):
        base = f * PLANES_PER_FIELD
        for half in range(2):
            rows = pl.ds(8 * half, 8)
            lefts = [vel[base + j, rows, :] for j in range(NODES)]
            rights = [vel[base + 42 + j, rows, :] for j in range(NODES)]
            pack_faces(0, f, rows, lefts, rights)
    for copy in halo_copies(0):
        copy.start()

    table_load.wait()
    tt, tl, bb = table.at[0:256, :], table.at[256:512, 0:128], table.at[256:512, 128:256]
    ff, fl, bl = table.at[512:640, :], table.at[640:768, 0:128], table.at[640:768, 128:256]
    slot_all = lax.broadcasted_iota(jnp.int32, (NCOEF, LANES), 1) // SLOT
    low_half = lane < 64

    def shifted(value, slots_up):
        return pltpu.roll(value, (SLOT * slots_up) % LANES, 1) if slots_up % 16 else value

    def to_planes(h, f):
        tiles = [recv1[h, 1 + 3 * f + p] for p in range(3)]
        last = jnp.where(slot_all == 6, shifted(recv1[0, 0], 6 - f - 3 * h), 0.0)
        for j in range(6):
            last = jnp.where(
                slot_all == j, shifted(tiles[j // 2], j - 7 - 8 * (j % 2)), last
            )
        tiles.append(last)
        planes = []
        for p in (0, 2):
            high, low = split_value(jnp.concatenate(tiles[p : p + 2], axis=1))
            value = dot(tt[...], jnp.concatenate([high, low], axis=0)) + dot(tl[...], high)
            for q in range(2):
                at = 4 * f + p + q
                planes.append(value[:NCOEF, q * LANES : (q + 1) * LANES])
                phys[at] = planes[-1]
                span[at] = value[NCOEF:, q * LANES : (q + 1) * LANES]
        high, low = split_value(jnp.concatenate(planes, axis=0))
        value = dot(jnp.concatenate([high, low], axis=1), bb[...]) + dot(high, bl[...])
        for p in range(4):
            cross[4 * f + p] = value[p * NCOEF : (p + 1) * NCOEF]

    def derivative_at(i, a):
        return float(2.0 * DERIV[i, a]) if i < NODES and a < NODES else 0.0

    def advect(h, f):
        def rows_of(block, inner):
            rows = pl.ds(pl.multiple_of(block * 8, 8), 8)
            tiles = [phys[4 * f + p, rows, :] for p in range(4)]
            swapped = [pltpu.roll(tile, 64, 1) for tile in tiles]
            both = tiles[3] + swapped[3]
            for p in range(4):
                i = 2 * p
                stream = both * jnp.where(low_half, derivative_at(i, 6), derivative_at(i + 1, 6))
                for q in range(3):
                    a = 2 * q
                    stream = (
                        stream
                        + tiles[q]
                        * jnp.where(low_half, derivative_at(i, a), derivative_at(i + 1, a + 1))
                        + swapped[q]
                        * jnp.where(low_half, derivative_at(i, a + 1), derivative_at(i + 1, a))
                    )
                at = 4 * f + p
                cross[at, rows, :] = (
                    phys[p, rows, :] * stream
                    + phys[4 + p, rows, :] * cross[at, rows, :]
                    + phys[8 + p, rows, :] * span[at, rows, :]
                )
            return inner

        lax.fori_loop(0, NCOEF // 8, rows_of, 0, unroll=2)
        last = None
        for p in (2, 0):
            pair = jnp.concatenate([cross[4 * f + p], cross[4 * f + p + 1]], axis=1)
            high, low = split_value(pair)
            value = dot(ff[...], jnp.concatenate([high, low], axis=0)) + dot(fl[...], high)
            parts = [value[:, :LANES], value[:, LANES:]]
            if p == 2:
                last = parts.pop()
            for q, part in reversed(list(enumerate(parts))):
                i = 2 * (p + q)
                part = jnp.where(slot_all == 7, shifted(last, 7 - i), part)
                send2[h, 3 * f + p + q] = jnp.where(slot_all == 15, shifted(last, 14 - i), part)
        at = 3 * h + f
        rest = send2[1, TILES - 1] if at else jnp.zeros((NCOEF, LANES), jnp.float32)
        send2[1, TILES - 1] = jnp.where(slot_all == at, shifted(last, at - 6), rest)
        for side, tile in ((0, last), (1, part)):
            if h:
                tile = jnp.where(slot_all < 8, edge_tile[side, f], shifted(tile, 8))
            edge_tile[side, f] = tile
        if h:
            for_edges(lambda side, owner: edge_copy(side, f, owner).start())
        for step in range(1, GROUPS):
            back_copy(h, f, step).start()
        own_back(h, f).start()

    for h in range(HALVES):
        for f in range(FIELDS):
            for step in range(1, GROUPS):
                out_copy(h, f, step).wait_recv()
            own_out(h, f).wait()
            if h == 0:
                start_out(1, f)
            to_planes(h, f)
        for f in range(FIELDS):
            advect(h, f)

    is_first = strip == 0
    is_last = strip == strips - 1
    not_inflow = jnp.logical_not(jnp.logical_and(group == 0, is_first))
    west = group == 0
    east = group == GROUPS - 1
    south = row != 0
    north = row != EY - 1
    has_previous = jnp.where(is_first, 0.0, 1.0)
    has_following = jnp.where(is_last, 0.0, 1.0)
    east_weight = jnp.where(jnp.logical_and(east, is_last), 1.0, 0.5)

    def at_block(block):
        f = block // 2
        rows = pl.ds(pl.multiple_of((block % 2) * 8, 8), 8)
        return f, rows

    def over_blocks(body, first=0, last=2 * FIELDS, unroll=2):
        lax.fori_loop(first, last, lambda block, c: (body(block), c)[1], 0, unroll=unroll)

    def gather_source(f):
        for h in range(HALVES):
            for step in range(1, GROUPS):
                back_copy(h, f, step).wait_recv()
            own_back(h, f).wait()
        base = f * PLANES_PER_FIELD
        for half in range(2):
            rows = pl.ds(8 * half, 8)
            for p in range(3):
                tiles = swap_groups(
                    [recv2[g % 2, g // 2, 3 * f + p, rows, :] for g in range(16)], lane
                )
                for s in range(16):
                    i, j = 2 * p + s // 8, s % 8
                    a, b = (i, j) if j < 7 else (6, i)
                    at = base + a * NODES + b
                    basis[0, at, rows, :] = float(MASS[a, b]) * (
                        SIGMA_BASE * vel[at, rows, :] + tiles[s]
                    )

    def gather_rest():
        for half in range(2):
            rows = pl.ds(8 * half, 8)
            tiles = []
            for k in range(GROUPS):
                tile = recv2[1, k, TILES - 1, rows, :]
                tiles += [tile, shifted(tile, -3)]
            tiles = swap_groups(tiles, lane)
            for f in range(FIELDS):
                at = f * PLANES_PER_FIELD + 48
                basis[0, at, rows, :] = float(MASS[6, 6]) * (
                    SIGMA_BASE * vel[at, rows, :] + tiles[f]
                )

    def along_rows(line):
        bottom, top = line[0], line[6]
        first = jnp.where(south, bottom + pltpu.roll(top, 1, 1), 0.0)
        last = jnp.where(north, top + pltpu.roll(bottom, LANES - 1, 1), 0.0)
        return [first] + list(line[1:6]) + [last]

    def squares(line):
        total = line[1] * line[1]
        for j in range(2, 6):
            total = total + line[j] * line[j]
        return total + 0.5 * (line[0] * line[0] + line[6] * line[6])

    def shift_of(block):
        number = (
            me * LOCAL + (block % 2) * 8 + lax.broadcasted_iota(jnp.int32, (8, LANES), 0)
        )
        wave = jnp.where(number <= NCOEF // 2, number, number - NCOEF // 2).astype(jnp.float32)
        wave = SPAN_WAVE * wave
        return 0.25 * (SIGMA_BASE + wave * wave)

    def finish_inside(level, first=0, last=2 * FIELDS):
        def block_of(block):
            f, rows = at_block(block)
            base = f * PLANES_PER_FIELD
            shift = shift_of(block)
            total = jnp.zeros((8, LANES), jnp.float32)
            inside = []
            for i in range(1, 6):
                line = []
                for j in range(NODES):
                    value = basis[level, base + i * NODES + j, rows, :]
                    if level:
                        value = float(QUAD[i] * QUAD[j]) * (
                            value
                            + float(SCALED_STIFF[i, 0]) * basis[level - 1, base + j, rows, :]
                            + float(SCALED_STIFF[i, 6]) * basis[level - 1, base + 42 + j, rows, :]
                        )
                    line.append(value)
                line = along_rows(line)
                for j in range(NODES):
                    if level or j in (0, 6):
                        basis[level, base + i * NODES + j, rows, :] = line[j]
                total = total + squares(line)
                inside.append(line)
            image = [None] * PLANES_PER_FIELD
            for j in range(NODES):
                column = [None] + [line[j] for line in inside] + [None]
                column = line_product(SCALED_STIFF, column, 1)
                for i in range(NODES):
                    image[i * NODES + j] = column[i]
            energy = jnp.zeros((8, LANES), jnp.float32)
            for i in range(1, 6):
                line = line_product(SCALED_STIFF, inside[i - 1], 1)
                for j in range(NODES):
                    n = i * NODES + j
                    image[n] = image[n] + line[j] + shift * inside[i - 1][j]
                    energy = energy + float(QUAD[i] * QUAD[j]) * (image[n] * inside[i - 1][j])
            for n in range(PLANES_PER_FIELD):
                if level < 2:
                    basis[level + 1, base + n, rows, :] = image[n]
                elif n < 7:
                    last_faces[0, f, n, rows, :] = image[n]
                elif n >= 42:
                    last_faces[1, f, n - 42, rows, :] = image[n]
            moments[2 * level, f, rows, :] = total
            moments[2 * level + 1, f, rows, :] = energy
            if level == 1:
                lefts = [basis[1, base + j, rows, :] for j in range(NODES)]
                rights = [basis[1, base + 42 + j, rows, :] for j in range(NODES)]
                inner_rights = along_rows(
                    [b + pltpu.roll(a, LANES - EY, 1) for a, b in zip(lefts, rights)]
                )
                inner_lefts = along_rows([a + pltpu.roll(b, EY, 1) for a, b in zip(lefts, rights)])
                pack_faces(
                    2,
                    f,
                    rows,
                    [image[j] + float(SCALED_STIFF[0, 6]) * inner_rights[j] for j in range(NODES)],
                    [
                        image[42 + j] + float(SCALED_STIFF[6, 0]) * inner_lefts[j]
                        for j in range(NODES)
                    ],
                )

        over_blocks(block_of, first, last, unroll=6 if last - first > 2 else 2)

    def finish_faces(level):
        def block_of(block):
            f, rows = at_block(block)
            base = f * PLANES_PER_FIELD
            shift = shift_of(block)
            prior = halo_recv[level, 0, f, rows, :]
            after = halo_recv[level, 1, f, rows, :]
            if level == 0:
                prior = SIGMA_BASE * prior
                after = SIGMA_BASE * after
                prior_edge = edge_recv[0, f, rows, :] * has_previous
                after_edge = edge_recv[1, f, rows, :] * has_following
            prior = prior * has_previous
            after = after * has_following
            lefts, rights = [], []
            for j in range(NODES):
                left = basis[level, base + j, rows, :]
                right = basis[level, base + 42 + j, rows, :]
                from_prior = pltpu.roll(prior, LANES - EY * j, 1) if j else prior
                from_after = pltpu.roll(after, LANES - EY * (j + 1), 1)
                if level == 0:
                    from_prior = float(MASS[6, j]) * (
                        from_prior
                        + jnp.where(
                            lane < 8, shifted(prior_edge, -j), shifted(prior_edge, -7 - j)
                        )
                    )
                    from_after = float(MASS[0, j]) * (
                        from_after
                        + jnp.where(
                            lane < 120, shifted(after_edge, 14 - j), shifted(after_edge, 7 - j)
                        )
                    )
                if level == 2:
                    weight = float(QUAD[0] * QUAD[j])
                    from_prior = weight * (from_prior + beside[0, f, j, rows, :])
                    from_after = weight * (from_after + beside[1, f, j, rows, :])
                lefts.append(left + jnp.where(west, from_prior, pltpu.roll(right, EY, 1)))
                rights.append(
                    right + jnp.where(east, from_after, pltpu.roll(left, LANES - EY, 1))
                )
            lefts = [jnp.where(not_inflow, value, 0.0) for value in along_rows(lefts)]
            rights = along_rows(rights)
            moments[2 * level, f, rows, :] = (
                moments[2 * level, f, rows, :]
                + 0.5 * squares(lefts)
                + east_weight * squares(rights)
            )
            energy = moments[2 * level + 1, f, rows, :]
            images = []
            for i, line in ((0, lefts), (6, rights)):
                across = line_product(SCALED_STIFF, line, 1)
                image = []
                for j in range(NODES):
                    basis[level, base + i * NODES + j, rows, :] = line[j]
                    if level < 2:
                        part = basis[level + 1, base + i * NODES + j, rows, :]
                    else:
                        part = last_faces[i // 6, f, j, rows, :]
                    whole = (
                        part
                        + float(SCALED_STIFF[i, 0]) * lefts[j]
                        + float(SCALED_STIFF[i, 6]) * rights[j]
                        + across[j]
                        + shift * line[j]
                    )
                    if level == 1:
                        has_side = has_previous if i == 0 else has_following
                        beside[i // 6, f, j, rows, :] = has_side * (
                            float(SCALED_STIFF[0, 0]) * line[j] + across[j] + shift * line[j]
                        )
                    weight = float(QUAD[i] * QUAD[j])
                    energy = energy + weight * ((whole + part) * line[j])
                    if level < 2:
                        whole = weight * whole
                        basis[level + 1, base + i * NODES + j, rows, :] = whole
                        image.append(whole)
                images.append(image)
            moments[2 * level + 1, f, rows, :] = energy
            if level == 0:
                pack_faces(1, f, rows, images[0], images[1])

        over_blocks(block_of, unroll=6)

    def wait_sent():
        for h in range(HALVES):
            for f in range(FIELDS):
                for step in range(1, GROUPS):
                    out_copy(h, f, step).wait_send()
                    back_copy(h, f, step).wait_send()
        for f in range(FIELDS):
            for_edges(lambda side, owner, f=f: edge_copy(side, f, owner).wait_send())

    def pack_moments(packed, which):
        for m in which:
            for block in range(2 * FIELDS):
                f, half = block // 2, block % 2
                total = jnp.sum(moments[m, f, 8 * half : 8 * half + 8, :], axis=1, keepdims=True)
                packed = jnp.where(lane == 8 * block + m, total, packed)
        return packed

    packed = jnp.zeros((8, LANES), jnp.float32)
    for level in range(3):
        if level == 0:
            for f in range(FIELDS):
                gather_source(f)
                finish_inside(0, 2 * f, 2 * f + 2)
                for side in range(2):
                    edge_copy(side, f, 0).wait_recv()
            gather_rest()
        else:
            finish_inside(level)
            if level == 1:
                for copy in halo_copies(2):
                    copy.start()
            packed = pack_moments(packed, (2 * level - 2, 2 * level - 1))
            if level == 1:
                wait_sent()
        for copy in halo_copies(level):
            copy.wait_recv()
        finish_faces(level)
        if level == 0:
            for copy in halo_copies(1):
                copy.start()
    packed = pack_moments(packed, (4, 5))

    def sum_over(value, slots_ref, mine, count, copies):
        slots_ref[mine] = value
        for copy in copies:
            copy.start()
        for copy in copies:
            copy.wait_recv()
        total = slots_ref[0]
        for k in range(1, count):
            total = total + slots_ref[k]
        return total

    x_copies = [
        remote(
            red_x.at[at_x],
            red_x.at[at_x],
            redx_send_sem.at[step - 1],
            redx_recv_sem.at[step - 1],
            {"mesh": x_peer(step)},
        )
        for step in range(1, mesh_x)
    ]
    z_copies = [
        remote(
            red_z.at[at_z],
            red_z.at[at_z],
            redz_send_sem.at[step - 1],
            redz_recv_sem.at[step - 1],
            {"mesh": z_peer(step)},
        )
        for step in range(1, mesh_z)
    ]
    packed = sum_over(packed, red_z, at_z, mesh_z, z_copies)
    packed = sum_over(packed, red_x, at_x, mesh_x, x_copies)

    m0, m1, m2, m3, m4, m5 = [
        packed if m == 0 else pltpu.roll(packed, LANES - m, 1) for m in range(MOMENTS)
    ]
    s0, s1, s2 = lax.rsqrt(m1), lax.rsqrt(m3), lax.rsqrt(m5)
    l10 = m2 * s0 * s1
    l20 = m3 * s0 * s2
    h21 = m4 * s1 * s2
    d1 = 1.0 - l10 * l10
    l21 = (h21 - l20 * l10) / d1
    d2 = 1.0 - l20 * l20 - l21 * l21 * d1
    y0 = m0 * s0
    y1 = m1 * s1 - l10 * y0
    y2 = m2 * s2 - l20 * y0 - l21 * y1
    c2 = y2 / d2
    c1 = y1 / d1 - l21 * c2
    c0 = y0 - l10 * c1 - l20 * c2
    c0, c1, c2 = c0 * s0, c1 * s1, c2 * s2

    for block in range(2 * FIELDS):
        f, half = block // 2, block % 2
        for k, c in enumerate((c0, c1, c2)):
            factor[k, f, 8 * half : 8 * half + 8, :] = jnp.broadcast_to(
                c[:, 8 * block : 8 * block + 1], (8, LANES)
            )

    for level in range(3):
        for copy in halo_copies(level):
            copy.wait_send()
    for copy in x_copies + z_copies:
        copy.wait_send()


def shards(mesh_x, mesh_z, velocity, element_slot):
    count = FIELDS * PLANES_PER_FIELD
    field = jnp.transpose(velocity, (0, 2, 3, 1, 4)).reshape(count, LOCAL, LANES)
    vmem = pl.BlockSpec(memory_space=pltpu.VMEM)
    f32 = jnp.float32
    dma = pltpu.SemaphoreType.DMA
    *basis, factor0, factor1, factor2 = pl.pallas_call(
        functools.partial(kernel, mesh_x, mesh_z),
        out_shape=[
            jax.ShapeDtypeStruct((count, LOCAL, LANES), f32),
        ]
        * 3
        + [
            jax.ShapeDtypeStruct((FIELDS, LOCAL, LANES), f32),
        ]
        * 3,
        in_specs=[pl.BlockSpec(memory_space=pltpu.HBM)] * 3,
        out_specs=[vmem] * 6,
        scratch_shapes=[
            pltpu.VMEM((count, LOCAL, LANES), f32),
            pltpu.VMEM((1, LANES), jnp.int32),
            pltpu.VMEM((TABLE_ROWS, 256), jnp.bfloat16),
            pltpu.VMEM((HALVES, GROUPS, TILES, LOCAL, LANES), f32),
            pltpu.VMEM((HALVES, TILES, NCOEF, LANES), f32),
            pltpu.VMEM((4 * FIELDS, NCOEF, LANES), f32),
            pltpu.VMEM((4 * FIELDS, NCOEF, LANES), f32),
            pltpu.VMEM((4 * FIELDS, NCOEF, LANES), f32),
            pltpu.VMEM((HALVES, TILES, NCOEF, LANES), f32),
            pltpu.VMEM((HALVES, GROUPS, TILES, LOCAL, LANES), f32),
            pltpu.VMEM((2, FIELDS, NODES, LOCAL, LANES), f32),
            pltpu.VMEM((2, FIELDS, NODES, LOCAL, LANES), f32),
            pltpu.VMEM((2, FIELDS, NCOEF, LANES), f32),
            pltpu.VMEM((2, FIELDS, LOCAL, LANES), f32),
            pltpu.VMEM((MOMENTS, FIELDS, LOCAL, LANES), f32),
            pltpu.VMEM((3, 2, FIELDS, LOCAL, LANES), f32),
            pltpu.VMEM((3, 2, FIELDS, LOCAL, LANES), f32),
            pltpu.VMEM((mesh_x, 8, LANES), f32),
            pltpu.VMEM((mesh_z, 8, LANES), f32),
            dma((HALVES, FIELDS, GROUPS - 1)),
            dma((HALVES, FIELDS, GROUPS - 1)),
            dma((HALVES, FIELDS)),
            dma((HALVES, FIELDS, GROUPS - 1)),
            dma((HALVES, FIELDS, GROUPS - 1)),
            dma((HALVES, FIELDS)),
            dma((3, 2)),
            dma((3, 2)),
            dma((mesh_x - 1,)),
            dma((mesh_x - 1,)),
            dma((mesh_z - 1,)),
            dma((mesh_z - 1,)),
            dma((FIELDS + 2,)),
            dma((2, FIELDS, GROUPS)),
            dma((2, FIELDS)),
        ],
        compiler_params=pltpu.CompilerParams(
            collective_id=0, has_side_effects=True, vmem_limit_bytes=50688 * 1024
        ),
    )(field, element_slot.reshape(1, LANES), jnp.asarray(transform_tables()))
    terms = [
        factor[:, None, None] * level.reshape(FIELDS, NODES, NODES, LOCAL, LANES)
        for level, factor in zip(basis, (factor0, factor1, factor2))
    ]
    result = terms[0] + terms[1] + terms[2]
    return jnp.transpose(result, (0, 3, 1, 2, 4))


def solution(mesh):
    strips = mesh.shape["mesh"]
    mesh_x = 4 if strips % 4 == 0 else 1
    placed = (P(None, "modes", None, None, "mesh"), P("mesh"))
    return jax.shard_map(
        functools.partial(shards, mesh_x, strips // mesh_x),
        mesh=mesh,
        in_specs=placed,
        out_specs=P(None, "modes", None, None, "mesh"),
        check_vma=False,
    )
```
